32 devices in a mesh: fsdp: 16 (over z, x, core), seq: 2 (over y).
Axes of the slice: x: 2, y: 2, z: 4, core: 2. Of those that a mesh axis runs over, the one named last changes fastest.
Arguments:
- frames_in: bfloat16 [16, 1024, 1280], P('fsdp', 'seq'), may hold values from -6 to 6
- clip_lengths: int32 [16], P('fsdp'), may hold values from 897 to 1024, as said below
- norm1_gain: bfloat16 [1280], P('fsdp'), may hold values from 0.5 to 1.5
- norm1_bias: bfloat16 [1280], P('fsdp'), may hold values from -2 to 2
- q_weight: bfloat16 [1280, 1280], P('fsdp')
- q_bias: bfloat16 [1280], P('fsdp'), may hold values from -2 to 2
- k_weight: bfloat16 [1280, 1280], P('fsdp'), may hold values from -0.15625 to 0.15625
- v_weight: bfloat16 [1280, 1280], P('fsdp'), may hold values from -0.15625 to 0.15625
- v_bias: bfloat16 [1280], P('fsdp'), may hold values from -2 to 2
- o_weight: bfloat16 [1280, 1280], P('fsdp'), may hold values from -0.625 to 0.625
- o_bias: bfloat16 [1280], P('fsdp'), may hold values from -2 to 2
- norm2_gain: bfloat16 [1280], P('fsdp'), may hold values from 0.5 to 1.5
- norm2_bias: bfloat16 [1280], P('fsdp'), may hold values from -2 to 2
- up_weight: bfloat16 [1280, 5120], P('fsdp'), may hold values from -0.15625 to 0.15625
- up_bias: bfloat16 [5120], P('fsdp'), may hold values from -2 to 2
- down_weight: bfloat16 [5120, 1280], P('fsdp'), may hold values from -0.078125 to 0.078125
- down_bias: bfloat16 [1280], P('fsdp'), may hold values from -2 to 2
- out_grad: bfloat16 [16, 1024, 1280], P('fsdp', 'seq'), may hold values from -6 to 6
Outputs:
- output: bfloat16 [16, 1024, 1280], P('fsdp', 'seq')
- in_grad: bfloat16 [16, 1024, 1280], P('fsdp', 'seq')
- norm1_gain_grad: float32 [1280], P('fsdp')
- norm1_bias_grad: float32 [1280], P('fsdp')
- q_weight_grad: float32 [1280, 1280], P('fsdp')
- q_bias_grad: float32 [1280], P('fsdp')
- k_weight_grad: float32 [1280, 1280], P('fsdp')
- v_weight_grad: float32 [1280, 1280], P('fsdp')
- v_bias_grad: float32 [1280], P('fsdp')
- o_weight_grad: float32 [1280, 1280], P('fsdp')
- o_bias_grad: float32 [1280], P('fsdp')
- norm2_gain_grad: float32 [1280], P('fsdp')
- norm2_bias_grad: float32 [1280], P('fsdp')
- up_weight_grad: float32 [1280, 5120], P('fsdp')
- up_bias_grad: float32 [5120], P('fsdp')
- down_weight_grad: float32 [5120, 1280], P('fsdp')
- down_bias_grad: float32 [1280], P('fsdp')
- logit_peak: float32 [16], replicated
- q_weight_clipped: float32 [1280, 1280], P('fsdp')
- q_bias_clipped: float32 [1280], P('fsdp')
- k_weight_clipped: float32 [1280, 1280], P('fsdp')
The draws below stay inside these ranges and needn't reach their ends.
Inputs may be any that keep to these rules, and one draw needn't show every extreme that they name: `clip_lengths`: some clip has all 1024 frames valid, and some other clip has exactly 1024 - 1024 // 8 + 1.
All inputs are finite; a program needn't handle non-finite values.
Results may differ from the reference program's by a relative error of at most 0.019.
Values may be sent and summed in bfloat16 or wider, within the bound.
No kernel may reach another device: no remote copies, remote signals or barrier semaphores. Data moves between devices by JAX's collectives and lax.ppermute only.
A program may use at most 384 MiB of HBM per device.

```python
import math
import jax
import jax.numpy as jnp
from jax import lax

D = 1280
HEADS = 16
HEAD_DIM = 80
FF = 5120
FRAMES = 1024
CLIPS = 16


def draw_clip_lengths(key, part):
    key = jax.random.fold_in(key, 11)
    length_key, pick_key = jax.random.split(key)
    shortest = FRAMES - FRAMES // 8 + 1
    spans = jax.random.randint(length_key, (CLIPS,), shortest, FRAMES + 1)
    order = jax.random.permutation(pick_key, CLIPS)
    slots = jnp.arange(CLIPS)
    spans = jnp.where(slots == order[0], FRAMES, spans)
    spans = jnp.where(slots == order[1], shortest, spans)
    return spans.astype(jnp.int32)


def draw_q_weight(key, part):
    key = jax.random.fold_in(key, 23)
    base_key, head_key = jax.random.split(key)
    base = jax.random.truncated_normal(base_key, -4.0, 4.0, (D, D), jnp.float32)
    boost = jnp.exp(jax.random.uniform(head_key, (HEADS,), jnp.float32, 0.0, math.log(3.0)))
    return (base * jnp.repeat(boost, HEAD_DIM)[None, :] / math.sqrt(D)).astype(jnp.bfloat16)


def level_of(rng, dims, shards, low, largest):
    level, own = 1.0, jax.random.fold_in(rng, 6)
    for axis_at, parts in shards:
        heights = jnp.exp(jax.random.uniform(jax.random.fold_in(own, axis_at), (parts,), jnp.float32, low / len(shards), largest / len(shards)))
        level = level * jnp.repeat(heights, dims[axis_at] // parts).reshape([-1 if axis == axis_at else 1 for axis in range(len(dims))])
    return level


def normal_values(own_key, extent, width, reach, cuts=(), held_as=jnp.bfloat16):
    values = jax.random.normal(own_key, extent, jnp.float32) * width
    if len(cuts) > 0:
        values = level_of(own_key, extent, cuts, -0.22, 0.18) * values
    return jnp.clip(values, min=-reach, max=reach).astype(held_as)


def setup_inputs(seed: int = 0) -> dict:
    key_list = jax.random.split(jax.random.key(seed), 19)
    frames_in = normal_values(key_list[0], (CLIPS, FRAMES, D), 1.0, 6.0, ((0, 16), (1, 2)))
    clip_lengths = draw_clip_lengths(jax.random.fold_in(key_list[18], 71), 0)
    norm1_gain = jnp.clip(1.0 + 0.1 * jax.random.normal(key_list[2], (D,), jnp.float32), 0.5, 1.5).astype(jnp.bfloat16)
    norm1_bias = normal_values(key_list[3], (D,), 0.3, 2.0, ((0, 16),))
    q_weight = draw_q_weight(jax.random.fold_in(key_list[18], 71), 0)
    q_bias = normal_values(key_list[5], (D,), 0.3, 2.0, ((0, 16),))
    k_weight = normal_values(key_list[6], (D, D), D ** -0.5, 0.15625, ((0, 16),))
    v_weight = normal_values(key_list[7], (D, D), D ** -0.5, 0.15625, ((0, 16),))
    v_bias = normal_values(key_list[8], (D,), 0.3, 2.0, ((0, 16),))
    o_weight = normal_values(key_list[9], (D, D), (D // 16) ** -0.5, 0.625, ((0, 16),))
    o_bias = normal_values(key_list[10], (D,), 0.3, 2.0, ((0, 16),))
    norm2_gain = jnp.clip(1.0 + 0.1 * jax.random.normal(key_list[11], (D,), jnp.float32), 0.5, 1.5).astype(jnp.bfloat16)
    norm2_bias = normal_values(key_list[12], (D,), 0.3, 2.0, ((0, 16),))
    up_weight = normal_values(key_list[13], (D, FF), D ** -0.5, 0.15625, ((0, 16),))
    up_bias = normal_values(key_list[14], (FF,), 0.3, 2.0, ((0, 16),))
    down_weight = normal_values(key_list[15], (FF, D), FF ** -0.5, 0.078125, ((0, 16),))
    down_bias = normal_values(key_list[16], (D,), 0.3, 2.0, ((0, 16),))
    out_grad = normal_values(key_list[17], (CLIPS, FRAMES, D), 1.0, 6.0, ((0, 16), (1, 2)))
    return {"frames_in": frames_in, "clip_lengths": clip_lengths, "norm1_gain": norm1_gain, "norm1_bias": norm1_bias, "q_weight": q_weight, "q_bias": q_bias, "k_weight": k_weight, "v_weight": v_weight, "v_bias": v_bias, "o_weight": o_weight, "o_bias": o_bias, "norm2_gain": norm2_gain, "norm2_bias": norm2_bias, "up_weight": up_weight, "up_bias": up_bias, "down_weight": down_weight, "down_bias": down_bias, "out_grad": out_grad}


NEGATIVE = -1000000000.0
EPSILON = 1e-05
LOGIT_CAP = 10.0

@jax.custom_vjp
def low(v):
    return lax.optimization_barrier(v.astype(jnp.bfloat16)).astype(jnp.float32)

@jax.custom_vjp
def low_back(v):
    return v

def low_keep(v):
    return (low(v), None)

def low_pass(kept, grad):
    return (grad,)

def back_keep(v):
    return (v, None)

def back_low(kept, grad):
    return (low(grad),)
low.defvjp(low_keep, low_pass)
low_back.defvjp(back_keep, back_low)

def layer_norm(rows, gain, offset):
    centred = rows - lax.optimization_barrier(jnp.mean(rows, axis=-1, keepdims=True))
    spread = lax.optimization_barrier(jnp.mean(centred * centred, axis=-1, keepdims=True))
    return centred * lax.rsqrt(spread + EPSILON) * gain + offset

def matmul(left, right):
    return jnp.dot(left, right, precision=lax.Precision.HIGHEST)

def clip_layer(params, clip_rows, length):
    gain1, shift1, query_w, query_b, key_w, value_w, value_b, out_w, out_b, gain2, shift2, up_w, up_b, down_w, down_b = params
    frame_count = clip_rows.shape[0]
    score_scale = 1.0 / math.sqrt(HEAD_DIM)
    normed1 = low(layer_norm(clip_rows, gain1, shift1))
    queries = low_back(low(matmul(normed1, query_w) + query_b)).reshape(frame_count, HEADS, HEAD_DIM)
    keys_all = low_back(low(matmul(normed1, key_w))).reshape(frame_count, HEADS, HEAD_DIM)
    values_all = low_back(low(matmul(normed1, value_w) + value_b)).reshape(frame_count, HEADS, HEAD_DIM)
    scores = low_back(jnp.einsum('qhd,khd->hqk', queries, keys_all, precision=lax.Precision.HIGHEST) * score_scale)
    key_live = jnp.arange(frame_count) < length
    masked = jnp.where(key_live[None, None, :], scores, NEGATIVE)
    probs = jax.nn.softmax(masked, axis=-1)
    mixed = jnp.einsum('hqk,khd->qhd', low(probs), values_all, precision=lax.Precision.HIGHEST).reshape(frame_count, HEADS * HEAD_DIM)
    mixed = low_back(low(mixed))
    valid_pair = jnp.logical_and(key_live[None, None, :], key_live[None, :, None])
    peak_logit = lax.optimization_barrier(jnp.max(jnp.where(valid_pair, scores, NEGATIVE), axis=(1, 2)))
    after1 = clip_rows + low_back(matmul(mixed, out_w) + out_b)
    normed2 = low(layer_norm(after1, gain2, shift2))
    before = low_back(matmul(normed2, up_w) + up_b)
    activity = low(jax.nn.gelu(before, approximate=False))
    return (after1 + low_back(matmul(activity, down_w) + down_b), peak_logit)

def reference(frames_in, clip_lengths, norm1_gain, norm1_bias, q_weight, q_bias, k_weight, v_weight, v_bias, o_weight, o_bias, norm2_gain, norm2_bias, up_weight, up_bias, down_weight, down_bias, out_grad):
    params = tuple((weight.astype(jnp.float32) for weight in (norm1_gain, norm1_bias, q_weight, q_bias, k_weight, v_weight, v_bias, o_weight, o_bias, norm2_gain, norm2_bias, up_weight, up_bias, down_weight, down_bias)))

    def forward(frames, *weights):

        def one_clip(element):
            return clip_layer(weights, element[0], element[1])
        outputs, peaks = lax.map(jax.checkpoint(one_clip), (frames, clip_lengths))
        return (outputs, lax.optimization_barrier(jnp.max(peaks, axis=0)))
    result, pullback, logit_peak = jax.vjp(forward, frames_in.astype(jnp.float32), *params, has_aux=True)
    live = (jnp.arange(FRAMES)[None, :] < clip_lengths[:, None]).astype(jnp.float32)
    live_grad = out_grad.astype(jnp.float32) * live[:, :, None]
    grads = pullback(live_grad)
    factor = jnp.sqrt(LOGIT_CAP / jnp.maximum(logit_peak, LOGIT_CAP))
    column_factor = jnp.repeat(factor, HEAD_DIM)
    return (result.astype(jnp.bfloat16), grads[0].astype(jnp.bfloat16), grads[1], grads[2], grads[3], grads[4], grads[5], grads[6], grads[7], grads[8], grads[9], grads[10], grads[11], grads[12], grads[13], grads[14], grads[15], logit_peak, params[2] * column_factor[None, :], params[3] * column_factor, params[4] * column_factor[None, :])
```

```python
import math

import jax
import jax.numpy as jnp
from jax import lax
from jax.experimental import pallas as pl
from jax.experimental.pallas import tpu as pltpu
from jax.sharding import PartitionSpec as P

HEAD_DIM = 80
NEGATIVE = -1000000000.0
EPSILON = 1e-05
LOGIT_CAP = 10.0
LOG2E = 1.4426950408889634
VMEM_LIMIT = 56 * 1024 * 1024
f32 = jnp.float32
bf16 = jnp.bfloat16


def dot(left, right, left_dim, right_dim):
    return lax.dot_general(
        left, right, (((left_dim,), (right_dim,)), ((), ())), preferred_element_type=f32
    )


def nt(a, b):
    return dot(a, b, 1, 1)


def nn(a, b):
    return dot(a, b, 1, 0)


def tn(a, b):
    return dot(a, b, 0, 0)


def normalized(rows):
    centred = rows - jnp.mean(rows, axis=-1, keepdims=True)
    spread = jnp.mean(centred * centred, axis=-1, keepdims=True)
    scale = lax.rsqrt(spread + EPSILON)
    return centred * scale, scale


def norm_back(plain, scale, grad):
    first = jnp.mean(grad, axis=-1, keepdims=True)
    second = jnp.mean(grad * plain, axis=-1, keepdims=True)
    return scale * (grad - first - plain * second)


def one_row(width):
    return jnp.where(lax.broadcasted_iota(jnp.int32, (16, width), 0) == 0, 1.0, 0.0).astype(bf16)


def attend_kernel(tile, scale2, q_ref, k_ref, v_ref, mask_ref, o_ref, lse_ref, peak_ref):
    frames = q_ref.shape[1]
    mask_rows = mask_ref[...]
    keys = jnp.concatenate([k_ref[...], mask_rows], axis=0).T
    values = jnp.concatenate([v_ref[...], one_row(frames)], axis=0)
    ones = one_row(tile)
    for at in range(frames // tile):
        cols = pl.ds(at * tile, tile)
        q = jnp.concatenate([q_ref[:, cols], ones], axis=0)
        s = nn(keys, q)
        top = jnp.max(s, axis=0, keepdims=True)
        p = jnp.exp2(s * scale2 - top * scale2).astype(bf16)
        mixed = nn(values, p)
        total = mixed[HEAD_DIM : HEAD_DIM + 1, :]
        o_ref[:, cols] = (mixed[:HEAD_DIM, :] * (1.0 / total)).astype(bf16)
        lse_ref[0, :, cols] = top * scale2 + jnp.log2(total)
        live = mask_rows[0:1, at * tile : (at + 1) * tile].astype(f32) == 0.0
        peak_ref[0, :, cols] = jnp.where(live, top, NEGATIVE)


def attend(qkv, mask, clips, heads):
    frames = qkv.shape[1] // clips
    tile = frames
    scale2 = LOG2E / math.sqrt(HEAD_DIM)

    def row(off):
        return pl.BlockSpec((HEAD_DIM, frames), lambda b, h: (off + h, b))

    vec = pl.BlockSpec((1, 1, frames), lambda b, h: (b * heads + h, 0, 0))
    return pl.pallas_call(
        lambda *refs: attend_kernel(tile, scale2, *refs),
        grid=(clips, heads),
        in_specs=[
            row(0),
            row(heads),
            row(2 * heads),
            pl.BlockSpec((16, frames), lambda b, h: (b, 0)),
        ],
        out_specs=[row(0), vec, vec],
        out_shape=[
            jax.ShapeDtypeStruct((heads * HEAD_DIM, clips * frames), bf16),
            jax.ShapeDtypeStruct((clips * heads, 1, frames), f32),
            jax.ShapeDtypeStruct((clips * heads, 1, frames), f32),
        ],
        compiler_params=pltpu.CompilerParams(vmem_limit_bytes=VMEM_LIMIT),
        cost_estimate=pl.CostEstimate(
            flops=clips * heads * frames * frames * 2000,
            bytes_accessed=qkv.size * 3,
            transcendentals=clips * heads * frames * frames,
        ),
        name="attend",
    )(qkv, qkv, qkv, mask)


def attend_back_kernel(
    tile, scale, q_ref, k_ref, v_ref, mask_ref, g_ref, lse_ref, out_ref, gk, gv
):
    frames = q_ref.shape[1]
    scale2 = LOG2E * scale
    key_rows = k_ref[...]
    keys = jnp.concatenate([key_rows, mask_ref[...]], axis=0).T
    values = v_ref[...].T
    ones = one_row(tile)
    for at in range(frames // tile):
        cols = pl.ds(at * tile, tile)
        q = q_ref[:, cols]
        g = g_ref[:, cols]
        s = nn(keys, jnp.concatenate([q, ones], axis=0))
        p = jnp.exp2(s * scale2 - lse_ref[0, :, cols])
        t = p * nn(values, g)
        inner = jnp.sum(t, axis=0, keepdims=True)
        ds = (t - p * inner).astype(bf16)
        out_ref[0, :, cols] = (nn(key_rows, ds) * scale).astype(bf16)
        dk = nt(q, ds)
        dv = nt(g, p.astype(bf16))
        if at == 0:
            gk[...] = dk
            gv[...] = dv
        else:
            gk[...] += dk
            gv[...] += dv
    out_ref[1] = (gk[...] * scale).astype(bf16)
    out_ref[2] = gv[...].astype(bf16)


def attend_back(qkv, mask, grad, lse, clips, heads):
    frames = qkv.shape[1] // clips
    tile = min(512, frames)

    def row(off):
        return pl.BlockSpec((HEAD_DIM, frames), lambda b, h: (off + h, b))

    vec = pl.BlockSpec((1, 1, frames), lambda b, h: (b * heads + h, 0, 0))
    return pl.pallas_call(
        lambda *refs: attend_back_kernel(tile, 1.0 / math.sqrt(HEAD_DIM), *refs),
        grid=(clips, heads),
        in_specs=[
            row(0),
            row(heads),
            row(2 * heads),
            pl.BlockSpec((16, frames), lambda b, h: (b, 0)),
            row(0),
            vec,
        ],
        out_specs=pl.BlockSpec((3, HEAD_DIM, frames), lambda b, h: (0, h, b)),
        out_shape=jax.ShapeDtypeStruct((3, heads * HEAD_DIM, clips * frames), bf16),
        scratch_shapes=[pltpu.VMEM((HEAD_DIM, frames), f32), pltpu.VMEM((HEAD_DIM, frames), f32)],
        compiler_params=pltpu.CompilerParams(vmem_limit_bytes=VMEM_LIMIT),
        cost_estimate=pl.CostEstimate(
            flops=clips * heads * frames * frames * 4000,
            bytes_accessed=qkv.size * 6,
            transcendentals=clips * heads * frames * frames,
        ),
        name="attend_back",
    )(qkv, qkv, qkv, mask, grad, lse)


def gelu_parts(v):
    bell = jnp.exp2(v * v * (-0.5 * LOG2E))
    t = 1.0 / (1.0 + (0.3275911 / math.sqrt(2.0)) * jnp.abs(v))
    poly = t * (
        0.5 * 0.254829592
        + t * (0.5 * -0.284496736 + t * (0.5 * 1.421413741 + t * (0.5 * -1.453152027 + t * (0.5 * 1.061405429))))
    )
    tail = poly * bell
    return jnp.where(v < 0.0, tail, 1.0 - tail), bell * (1.0 / math.sqrt(2.0 * math.pi))


def feed_kernel(rows, n_ref, g_ref, up_ref, bias_ref, down_ref, act_ref, grad_ref, sum_ref):
    up = up_ref[...]
    down = down_ref[...]
    total = jnp.zeros(sum_ref.shape, f32)
    for at in range(n_ref.shape[0] // rows):
        part = pl.ds(at * rows, rows)
        before = nn(n_ref[part, :], up) + bias_ref[...]
        grad_act = nt(g_ref[part, :], down)
        cumulative, density = gelu_parts(before)
        act_ref[part, :] = (before * cumulative).astype(bf16)
        grad = ((cumulative + before * density) * grad_act).astype(bf16)
        grad_ref[part, :] = grad
        total = total + jnp.sum(grad.astype(f32), axis=0, keepdims=True)
    sum_ref[...] = total


def feed(normed, grad, up, bias, down):
    tokens, width = normed.shape
    hidden = up.shape[1]
    tile = 256 if hidden % 256 == 0 else hidden
    rows = 256 if tokens % 256 == 0 else tokens
    whole = pl.BlockSpec((tokens, width), lambda i: (0, 0))
    column = pl.BlockSpec((tokens, tile), lambda i: (0, i))
    line = pl.BlockSpec((1, tile), lambda i: (0, i))
    return pl.pallas_call(
        lambda *refs: feed_kernel(rows, *refs),
        grid=(hidden // tile,),
        in_specs=[
            whole,
            whole,
            pl.BlockSpec((width, tile), lambda i: (0, i)),
            line,
            pl.BlockSpec((tile, width), lambda i: (i, 0)),
        ],
        out_specs=[column, column, line],
        out_shape=[
            jax.ShapeDtypeStruct((tokens, hidden), bf16),
            jax.ShapeDtypeStruct((tokens, hidden), bf16),
            jax.ShapeDtypeStruct((1, hidden), f32),
        ],
        compiler_params=pltpu.CompilerParams(vmem_limit_bytes=VMEM_LIMIT),
        cost_estimate=pl.CostEstimate(
            flops=4 * tokens * width * hidden,
            bytes_accessed=2 * (2 * tokens * width + 2 * width * hidden + 2 * tokens * hidden),
            transcendentals=tokens * hidden,
        ),
        name="feed",
    )(normed, grad, up, bias, down)


def place(blocks, slots, cuts):
    count, (rows, width) = len(blocks), blocks[0].shape
    spans = list(zip((0,) + cuts, cuts + (rows,), strict=True))

    def kernel(slots_ref, *refs):
        for i in range(count):
            for target, (low, high) in zip(refs[count:], spans, strict=True):
                target[slots_ref[i]] = refs[i][low:high, :]

    return pl.pallas_call(
        kernel,
        in_specs=[pl.BlockSpec(memory_space=pltpu.SMEM)]
        + [pl.BlockSpec(memory_space=pltpu.VMEM)] * count,
        out_specs=[pl.BlockSpec(memory_space=pltpu.VMEM)] * len(spans),
        out_shape=[
            jax.ShapeDtypeStruct((count, high - low, width), blocks[0].dtype) for low, high in spans
        ],
        compiler_params=pltpu.CompilerParams(vmem_limit_bytes=VMEM_LIMIT),
        cost_estimate=pl.CostEstimate(
            flops=0, bytes_accessed=4 * count * rows * width, transcendentals=0
        ),
        name="place",
    )(slots, *blocks)


def local(
    frames_in,
    clip_lengths,
    norm1_gain,
    norm1_bias,
    q_weight,
    q_bias,
    k_weight,
    v_weight,
    v_bias,
    o_weight,
    o_bias,
    norm2_gain,
    norm2_bias,
    up_weight,
    up_bias,
    down_weight,
    down_bias,
    out_grad,
):
    clip_count, local_frames, width = frames_in.shape
    hidden = up_weight.shape[1]
    groups = lax.axis_size("seq")
    shards = lax.axis_size("fsdp")
    pairs = shards // 2
    depth = pairs // 2
    ranks = groups * 2
    frames = local_frames * groups
    tokens = clip_count * local_frames
    head_count = width // HEAD_DIM
    heads = head_count // ranks
    slab = heads * HEAD_DIM
    own_rows = width // shards
    own_hidden = hidden // shards
    piece = own_hidden * 2 // ranks
    rank_hidden = piece * pairs
    fsdp = lax.axis_index("fsdp")
    seq = lax.axis_index("seq")
    core, pair = fsdp % 2, fsdp // 2
    xpos, zpos = pair % 2, pair // 2
    rank = core * groups + seq

    core_way = [(i, i ^ 1) for i in range(shards)]
    x_way = [(i, i ^ 2) for i in range(shards)]

    def z_way(step):
        return [(i, (i + 4 * step) % shards) for i in range(shards)]

    def over_core(v):
        return lax.ppermute(v, "fsdp", core_way)

    def over_x(v):
        return lax.ppermute(v, "fsdp", x_way)

    def over_z(v, step):
        return lax.ppermute(v, "fsdp", z_way(step))

    def from_seq(v, step):
        return lax.ppermute(v, "seq", [(i, (i - step) % groups) for i in range(groups)])

    def to_seq(v, step):
        return from_seq(v, -step % groups)

    def share(own):
        side = [from_seq(own, step) for step in range(1, groups)]
        return [own] + side, [over_core(v) for v in [own] + side]

    def butterfly(v, combine):
        v = combine(v, over_core(v))
        v = combine(v, over_x(v))
        step = 4
        while step < shards:
            v = combine(v, lax.ppermute(v, "fsdp", [(i, i ^ step) for i in range(shards)]))
            step *= 2
        step = 1
        while step < groups:
            v = combine(v, lax.ppermute(v, "seq", [(i, i ^ step) for i in range(groups)]))
            step *= 2
        return v

    slots = []
    for step in range(depth):
        for flip in range(2):
            slots.append(((zpos - step) % depth) * 2 + (xpos ^ flip))
    slots = jnp.stack(slots).astype(jnp.int32)

    def spread(payload, cuts=()):
        blocks = [payload] + [over_z(payload, step) for step in range(1, depth)]
        both = []
        for block in blocks:
            both += [block, over_x(block)]
        return place(both, slots, cuts)

    def by_core(mine, other):
        return jnp.where(
            core == 0, jnp.concatenate([mine, other]), jnp.concatenate([other, mine])
        )

    vectors = [norm1_gain, norm1_bias, q_bias, v_bias, o_bias, norm2_gain, norm2_bias, down_bias]
    small = jnp.concatenate(vectors + [up_bias])
    small_rows = -(-small.shape[0] // (3 * slab))
    small = jnp.pad(small, (0, small_rows * 3 * slab - small.shape[0])).reshape(small_rows, 3 * slab)

    def head_columns(of):
        return jnp.concatenate(
            [lax.dynamic_slice_in_dim(w, of * slab, slab, 1) for w in (q_weight, k_weight, v_weight)], axis=1
        )

    qkv_own = by_core(head_columns(rank), over_core(head_columns((1 - core) * groups + seq)))
    small_pair = by_core(small, over_core(small))
    extra = -(-2 * small_rows // 16) * 16
    small_pair = jnp.pad(small_pair, ((0, extra - 2 * small_rows), (0, 0)))
    qkv_part, small_part = spread(
        jnp.concatenate([qkv_own, small_pair]), (2 * own_rows,)
    )
    qkv_full = qkv_part.reshape(width, 3 * slab)
    small_all = small_part[:, : 2 * small_rows].reshape(shards, small_rows * 3 * slab)
    gain1, shift1, qbias, vbias, obias, gain2, shift2, dbias = [
        small_all[:, i * own_rows : (i + 1) * own_rows].reshape(width).astype(f32)
        for i in range(8)
    ]
    ubias = (
        small_all[:, 8 * own_rows : 8 * own_rows + own_hidden]
        .reshape(pairs, ranks, piece)
    )
    ubias = lax.dynamic_index_in_dim(ubias, rank, 1, keepdims=False).reshape(1, rank_hidden).astype(f32)

    same_core = [[i for i in range(shards) if i % 2 == c] for c in range(2)]
    up_cols = up_weight.reshape(own_rows, pairs, ranks, piece)

    def hidden_columns(of):
        return lax.dynamic_index_in_dim(up_cols, of, 2, keepdims=False).reshape(own_rows, rank_hidden)

    up_own = by_core(hidden_columns(rank), over_core(hidden_columns((1 - core) * groups + seq)))
    down_own = lax.dynamic_slice_in_dim(down_weight, seq * piece, piece, 0)
    feed_own = jnp.concatenate([up_own.reshape(2 * own_rows * rank_hidden // width, width), down_own])
    feed_full = lax.all_gather(feed_own, "fsdp", axis=0, axis_index_groups=same_core)
    up_rows = up_own.size // width
    up_full = feed_full[:, :up_rows].reshape(width, rank_hidden)
    down_full = feed_full[:, up_rows:].reshape(rank_hidden, width)

    half = width // 2

    def half_columns(of):
        return lax.dynamic_slice_in_dim(o_weight, of * half, half, 1)

    (out_half,) = spread(by_core(half_columns(core), over_core(half_columns(1 - core))))
    out_half = out_half.reshape(width, half)
    out_other = over_core(out_half)
    out_full = jnp.where(
        core == 0,
        jnp.concatenate([out_half, out_other], axis=1),
        jnp.concatenate([out_other, out_half], axis=1),
    )

    frames_own = frames_in.reshape(tokens, width)
    positions = jnp.concatenate(
        [
            ((seq + step) % groups) * local_frames + jnp.arange(local_frames, dtype=jnp.int32)
            for step in range(groups)
        ]
    )
    lengths_sent = jnp.broadcast_to(clip_lengths.astype(f32)[:, None], (clip_count, 128))
    lengths = jnp.concatenate(
        [clip_lengths, over_core(lengths_sent)[:, 0].astype(jnp.int32)]
    )
    clips = 2 * clip_count
    live = positions[None, :] < lengths[:, None]
    live_own = live[:clip_count, :local_frames].reshape(tokens, 1)
    mask = jnp.where(live, 0.0, NEGATIVE).astype(bf16)
    mask = jnp.pad(mask[:, None, :], ((0, 0), (0, 15), (0, 0))).reshape(clips * 16, frames)
    live_grad = jnp.where(live_own, out_grad.reshape(tokens, width), 0.0).astype(bf16)

    def by_clip(blocks):
        parts = [v.reshape(clip_count, local_frames, -1) for v in blocks]
        return jnp.concatenate(parts, axis=1).reshape(clip_count * frames, -1)

    mine, others = share(frames_own)
    frames_all = jnp.concatenate([by_clip(mine), by_clip(others)])

    residual = frames_own.astype(f32)
    plain1_all, _ = normalized(frames_all.astype(f32))
    normed1 = (plain1_all * gain1 + shift1).astype(bf16)
    zero_bias = jnp.zeros((slab,), f32)
    head_bias = jnp.concatenate(
        [
            lax.dynamic_slice_in_dim(qbias, rank * slab, slab, 0),
            zero_bias,
            lax.dynamic_slice_in_dim(vbias, rank * slab, slab, 0),
        ]
    )
    qkv = (dot(qkv_full, normed1, 0, 1) + head_bias[:, None]).astype(bf16)
    mixed, log_totals, tops = attend(qkv, mask, clips, heads)

    top_heads = jnp.max(tops.reshape(clips, heads, frames), axis=(0, 2)) / math.sqrt(HEAD_DIM)
    peak_all = lax.dynamic_update_slice_in_dim(
        jnp.full((head_count,), NEGATIVE, f32), top_heads, rank * heads, 0
    )
    logit_peak = butterfly(peak_all.reshape(1, head_count), jnp.maximum).reshape(head_count)

    span = clip_count * frames

    def token_block(v, flip, step):
        cut = v[:, flip * span : (flip + 1) * span].reshape(slab, clip_count, groups, local_frames)
        return cut[:, :, step].reshape(slab, tokens)

    def heads_to_tokens(v):
        full = jnp.zeros((width, tokens), v.dtype)
        for flip in range(2):
            for step in range(groups):
                block = token_block(v, flip, step)
                if step:
                    block = to_seq(block, step)
                if flip:
                    block = over_core(block)
                source = (core ^ flip) * groups + (seq - step) % groups
                full = lax.dynamic_update_slice_in_dim(full, block, source * slab, 0)
        return full

    def tokens_to_heads(v):
        halves = []
        for flip in range(2):
            parts = []
            for step in range(groups):
                target = (core ^ flip) * groups + (seq + step) % groups
                block = lax.dynamic_slice_in_dim(v, target * slab, slab, 0)
                if step:
                    block = to_seq(block, step)
                if flip:
                    block = over_core(block)
                parts.append((step, block))
            parts = [parts[-step % groups][1] for step in range(groups)]
            parts = [v.reshape(slab, clip_count, 1, local_frames) for v in parts]
            halves.append(jnp.concatenate(parts, axis=2).reshape(slab, span))
        return jnp.concatenate(halves, axis=1)

    def sum_to_own(near, far):
        near_mine, near_other = near[:tokens], near[tokens:].astype(bf16)
        total = near_mine + over_core(near_other).astype(f32)
        for step in range(1, groups):
            cut = far[(step - 1) * 2 * tokens : step * 2 * tokens]
            both = cut[:tokens] + over_core(cut[tokens:].astype(bf16)).astype(f32)
            total = total + to_seq(both.astype(bf16), step).astype(f32)
        return total

    mixed_own = heads_to_tokens(mixed)
    after1 = residual + (tn(mixed_own, out_full) + obias)
    plain2, scale2 = normalized(after1)
    normed2 = (plain2 * gain2 + shift2).astype(bf16)

    def near_far(own):
        mine, others = share(own)
        near = jnp.concatenate([mine[0], others[0]])
        far = jnp.concatenate([v for pair_of in zip(mine[1:], others[1:], strict=True) for v in pair_of])
        return near, far

    normed2_near, normed2_far = near_far(normed2)
    grad_near, grad_far = near_far(live_grad)
    act_near, back_near, sums_near = feed(normed2_near, grad_near, up_full, ubias, down_full)
    act_far, back_far, sums_far = feed(normed2_far, grad_far, up_full, ubias, down_full)

    grad_normed2 = sum_to_own(nt(back_near, up_full), nt(back_far, up_full))
    fed = sum_to_own(nn(act_near, down_full), nn(act_far, down_full))
    output = (after1 + (fed + dbias)).astype(bf16).reshape(clip_count, local_frames, width)

    feed_grad = jnp.concatenate(
        [
            (tn(normed2_near, back_near) + tn(normed2_far, back_far)).astype(bf16),
            (tn(act_near, grad_near) + tn(act_far, grad_far)).astype(bf16).reshape(width, -1),
        ],
        axis=1,
    )
    feed_shard = lax.psum_scatter(
        feed_grad, "fsdp", scatter_dimension=0, axis_index_groups=same_core, tiled=True
    )

    live_low = live_grad.astype(f32)
    grad_after1 = live_low + norm_back(plain2, scale2, grad_normed2 * gain2)
    grad_attn = grad_after1.astype(bf16)
    grad_mixed = tokens_to_heads(nt(out_full, grad_attn).astype(bf16))
    grad_qkv = attend_back(qkv, mask, grad_mixed, log_totals, clips, heads).reshape(3 * slab, -1)

    def reduce_spread(v):
        blocks = v.reshape(depth, 2, width // pairs, -1)
        kept = lax.dynamic_index_in_dim(blocks, xpos, 1, keepdims=False).astype(f32)
        sent = lax.dynamic_index_in_dim(blocks, 1 - xpos, 1, keepdims=False)
        both = kept + over_x(sent).astype(f32)
        total = lax.dynamic_index_in_dim(both, zpos, 0, keepdims=False)
        for step in range(1, depth):
            block = lax.dynamic_index_in_dim(both.astype(bf16), (zpos + step) % depth, 0, keepdims=False)
            total = total + over_z(block, step).astype(f32)
        return total

    qkv_grad = reduce_spread(dot(normed1, grad_qkv, 0, 1).astype(bf16)).astype(bf16)
    near_of = [0, span]
    grad_tokens = dot(grad_qkv, qkv_full, 0, 1)
    shift1_sum = jnp.sum(grad_tokens, axis=0)
    gain1_sum = jnp.sum(grad_tokens * plain1_all, axis=0)
    token_cut = grad_tokens.reshape(2, clip_count, groups, local_frames, width)
    near = token_cut[:, :, 0].reshape(2 * tokens, width)
    far = jnp.concatenate([token_cut[:, :, step].reshape(2 * tokens, width) for step in range(1, groups)])
    grad_normed1 = sum_to_own(near, far)
    plain1, scale1 = normalized(residual)
    in_grad = (grad_after1 + norm_back(plain1, scale1, grad_normed1 * gain1)).astype(bf16)

    out_blocks = tn_out = nn(mixed_own, grad_attn).reshape(pairs, 2, own_rows, width)
    out_keep = lax.dynamic_index_in_dim(out_blocks, core, 1, keepdims=False)
    out_send = lax.dynamic_index_in_dim(out_blocks, 1 - core, 1, keepdims=False).astype(bf16)
    out_sum = (out_keep + over_core(out_send).astype(f32)).reshape(pairs * own_rows, groups, width // groups)
    out_total = lax.dynamic_index_in_dim(out_sum, seq, 1, keepdims=False)
    for step in range(1, groups):
        block = lax.dynamic_index_in_dim(out_sum.astype(bf16), (seq + step) % groups, 1, keepdims=False)
        out_total = out_total + to_seq(block, step).astype(f32)
    out_blocks = out_total.astype(bf16).reshape(depth, 2, own_rows, width // groups)
    kept = lax.dynamic_index_in_dim(out_blocks, xpos, 1, keepdims=False).astype(f32)
    sent = lax.dynamic_index_in_dim(out_blocks, 1 - xpos, 1, keepdims=False)
    both = kept + over_x(sent).astype(f32)
    out_shard = lax.dynamic_index_in_dim(both, zpos, 0, keepdims=False)
    for step in range(1, depth):
        block = lax.dynamic_index_in_dim(both.astype(bf16), (zpos + step) % depth, 0, keepdims=False)
        out_shard = out_shard + over_z(block, step).astype(f32)
    out_shard = out_shard.astype(bf16)

    def along_seq(v):
        full = jnp.zeros((groups,) + v.shape, v.dtype)
        for step in range(groups):
            block = from_seq(v, step) if step else v
            full = lax.dynamic_update_index_in_dim(full, block, (seq + step) % groups, 0)
        return full

    def own_of_ranks(v):
        cut = v.reshape(2, own_rows, -1)
        keep = lax.dynamic_index_in_dim(cut, core, 0, keepdims=True)
        other = over_core(lax.dynamic_index_in_dim(cut, 1 - core, 0, keepdims=True))
        return jnp.swapaxes(along_seq(by_core(keep, other)), 0, 1)

    up_shard = feed_shard[:, :rank_hidden]
    down_shard = feed_shard[:, rank_hidden:].reshape(piece, width)
    up_weight_grad = (
        own_of_ranks(up_shard)
        .reshape(2, groups, own_rows, pairs, piece)
        .transpose(2, 3, 0, 1, 4)
        .reshape(own_rows, hidden)
        .astype(f32)
    )
    down_weight_grad = along_seq(down_shard).reshape(own_hidden, width).astype(f32)
    qkv_own_grad = (
        own_of_ranks(qkv_grad)
        .reshape(2, groups, own_rows, 3, slab)
        .transpose(3, 2, 0, 1, 4)
        .reshape(3, own_rows, width)
        .astype(f32)
    )
    o_weight_grad = along_seq(out_shard).transpose(1, 0, 2).reshape(own_rows, width).astype(f32)

    bias_cols = jnp.sum(grad_qkv.astype(f32), axis=1)

    def at_rank(v):
        return lax.dynamic_update_slice_in_dim(jnp.zeros((width,), f32), v, rank * slab, 0)

    up_sums = lax.dynamic_update_index_in_dim(
        jnp.zeros((pairs, ranks, piece), f32), (sums_near + sums_far).reshape(pairs, piece), rank, 1
    ).reshape(hidden // width, width)
    stack = jnp.concatenate(
        [
            jnp.stack(
                [
                    gain1_sum,
                    shift1_sum,
                    at_rank(bias_cols[:slab]),
                    at_rank(bias_cols[2 * slab :]),
                    jnp.sum(grad_attn.astype(f32), axis=0),
                    jnp.sum(grad_normed2 * plain2, axis=0),
                    jnp.sum(grad_normed2, axis=0),
                    jnp.sum(live_low, axis=0),
                ]
            ),
            up_sums,
        ]
    )
    stack = butterfly(stack, jnp.add)
    small_own = lax.dynamic_slice_in_dim(stack[:8], fsdp * own_rows, own_rows, 1)
    up_bias_grad = lax.dynamic_slice_in_dim(stack[8:].reshape(hidden), fsdp * own_hidden, own_hidden, 0)

    factor = jnp.sqrt(LOGIT_CAP / jnp.maximum(logit_peak, LOGIT_CAP))
    column_factor = jnp.repeat(factor, HEAD_DIM)
    q_weight_clipped = q_weight.astype(f32) * column_factor[None, :]
    k_weight_clipped = k_weight.astype(f32) * column_factor[None, :]
    q_bias_clipped = q_bias.astype(f32) * lax.dynamic_slice_in_dim(
        column_factor, fsdp * own_rows, own_rows, 0
    )
    return (
        output,
        in_grad.reshape(clip_count, local_frames, width),
        small_own[0],
        small_own[1],
        qkv_own_grad[0],
        small_own[2],
        qkv_own_grad[1],
        qkv_own_grad[2],
        small_own[3],
        o_weight_grad,
        small_own[4],
        small_own[5],
        small_own[6],
        up_weight_grad,
        up_bias_grad,
        down_weight_grad,
        small_own[7],
        logit_peak,
        q_weight_clipped,
        q_bias_clipped,
        k_weight_clipped,
    )


def solution(mesh):
    rows, vector, clip = P("fsdp", None), P("fsdp"), P("fsdp", "seq", None)
    return jax.shard_map(
        local,
        mesh=mesh,
        in_specs=(
            clip,
            vector,
            vector,
            vector,
            rows,
            vector,
            rows,
            rows,
            vector,
            rows,
            vector,
            vector,
            vector,
            rows,
            vector,
            rows,
            vector,
            clip,
        ),
        out_specs=(
            clip,
            clip,
            vector,
            vector,
            rows,
            vector,
            rows,
            rows,
            vector,
            rows,
            vector,
            vector,
            vector,
            rows,
            vector,
            rows,
            vector,
            P(),
            rows,
            vector,
            rows,
        ),
        check_vma=False,
    )
```

```python
import math

import jax
import jax.numpy as jnp
from jax import lax
from jax.experimental import pallas as pl
from jax.experimental.pallas import tpu as pltpu
from jax.sharding import PartitionSpec as P

HEAD_DIM = 80
NEGATIVE = -1000000000.0
EPSILON = 1e-05
LOGIT_CAP = 10.0
LOG2E = 1.4426950408889634
VMEM_LIMIT = 56 * 1024 * 1024
f32 = jnp.float32
bf16 = jnp.bfloat16


def dot(left, right, left_dim, right_dim):
    return lax.dot_general(
        left, right, (((left_dim,), (right_dim,)), ((), ())), preferred_element_type=f32
    )


def nt(a, b):
    return dot(a, b, 1, 1)


def nn(a, b):
    return dot(a, b, 1, 0)


def tn(a, b):
    return dot(a, b, 0, 0)


def normalized(rows):
    centred = rows - jnp.mean(rows, axis=-1, keepdims=True)
    spread = jnp.mean(centred * centred, axis=-1, keepdims=True)
    scale = lax.rsqrt(spread + EPSILON)
    return centred * scale, scale


def norm_back(plain, scale, grad):
    first = jnp.mean(grad, axis=-1, keepdims=True)
    second = jnp.mean(grad * plain, axis=-1, keepdims=True)
    return scale * (grad - first - plain * second)


def tie(value, *after):
    return lax.optimization_barrier((value,) + after)[0]


def params(**more):
    return pltpu.CompilerParams(vmem_limit_bytes=VMEM_LIMIT, **more)


def vmem(count):
    return [pl.BlockSpec(memory_space=pltpu.VMEM)] * count


def smem():
    return pl.BlockSpec(memory_space=pltpu.SMEM)


def sds(shape, dtype):
    return jax.ShapeDtypeStruct(shape, dtype)


def one_row(width):
    return jnp.where(lax.broadcasted_iota(jnp.int32, (16, width), 0) == 0, 1.0, 0.0).astype(bf16)


def attend_kernel(scale2, span, q_ref, k_ref, v_ref, mask_ref, near_ref, far_ref, lse_ref, peak_ref):
    frames = q_ref.shape[1]
    mask_rows = mask_ref[...]
    keys = jnp.concatenate([k_ref[...], mask_rows], axis=0).T
    values = jnp.concatenate([v_ref[...], one_row(frames)], axis=0)
    s = nn(keys, jnp.concatenate([q_ref[...], one_row(frames)], axis=0))
    top = jnp.max(s, axis=0, keepdims=True)
    p = jnp.exp2(s * scale2 - top * scale2).astype(bf16)
    mixed = nn(values, p)
    total = mixed[HEAD_DIM : HEAD_DIM + 1, :]
    mixed = (mixed[:HEAD_DIM, :] * (1.0 / total)).astype(bf16)
    near_ref[0] = mixed[:, :span]
    for step in range(1, frames // span):
        far_ref[step - 1, 0] = mixed[:, step * span : (step + 1) * span]
    lse_ref[0] = top * scale2 + jnp.log2(total)
    peak_ref[0] = jnp.where(mask_rows[0:1, :].astype(f32) == 0.0, top, NEGATIVE)


def head_rows(frames, heads, half):
    return [
        pl.BlockSpec((HEAD_DIM, frames), lambda b, h, i=i: ((3 * half + i) * heads + h, b))
        for i in range(3)
    ]


def attend(qkv, mask, clips, heads, half, halves, groups):
    frames = qkv.shape[1] // clips
    span = frames // groups
    vec = pl.BlockSpec((1, 1, frames), lambda b, h: (b * heads + h, 0, 0))
    return pl.pallas_call(
        lambda *refs: attend_kernel(LOG2E / math.sqrt(HEAD_DIM), span, *refs),
        grid=(clips, heads),
        in_specs=head_rows(frames, heads, half) + [pl.BlockSpec((16, frames), lambda b, h: (b, 0))],
        out_specs=[
            pl.BlockSpec((1, HEAD_DIM, span), lambda b, h: (b, h, 0)),
            pl.BlockSpec((groups - 1, 1, HEAD_DIM, span), lambda b, h: (0, b, h, 0)),
            vec,
            vec,
        ],
        out_shape=[
            sds((clips, heads * HEAD_DIM, span), bf16),
            sds((groups - 1, clips, heads * HEAD_DIM, span), bf16),
            sds((clips * heads, 1, frames), f32),
            sds((clips * heads, 1, frames), f32),
        ],
        compiler_params=params(),
        cost_estimate=pl.CostEstimate(
            flops=clips * heads * frames * frames * 2000,
            bytes_accessed=qkv.size * 3 // halves,
            transcendentals=clips * heads * frames * frames,
        ),
        name="attend",
    )(qkv, qkv, qkv, mask)


def attend_back_kernel(span, scale, *refs):
    q_ref, k_ref, v_ref, mask_ref, lse_ref = refs[:5]
    groups = q_ref.shape[1] // span
    grads = refs[5 : 5 + 2 * groups]
    out_ref, gk, gv, gs = refs[5 + 2 * groups :]
    scale2 = LOG2E * scale
    key_rows = k_ref[...]
    keys = jnp.concatenate([key_rows, mask_ref[...]], axis=0).T
    values = v_ref[...].T
    ones = one_row(span)
    for flip in range(2):

        @pl.when(pl.program_id(0) == flip)
        def _(flip=flip):
            for at in range(groups):
                gs[:, at * span : (at + 1) * span] = grads[flip * groups + at][...].reshape(HEAD_DIM, span)

    for at in range(groups):
        cols = pl.ds(at * span, span)
        q = q_ref[:, cols]
        g = gs[:, cols]
        s = nn(keys, jnp.concatenate([q, ones], axis=0))
        p = jnp.exp2(s * scale2 - lse_ref[0, :, cols])
        t = p * nn(values, g)
        inner = jnp.sum(t, axis=0, keepdims=True)
        ds = (t - p * inner).astype(bf16)
        out_ref[0, :, cols] = (nn(key_rows, ds) * scale).astype(bf16)
        dk = nt(q, ds)
        dv = nt(g, p.astype(bf16))
        if at == 0:
            gk[...] = dk
            gv[...] = dv
        else:
            gk[...] += dk
            gv[...] += dv
    out_ref[1] = (gk[...] * scale).astype(bf16)
    out_ref[2] = gv[...].astype(bf16)


def attend_back(qkv, mask, grads, lse, clips, heads, half, halves, groups):
    frames = qkv.shape[1] // clips
    span = frames // groups
    vec = pl.BlockSpec((1, 1, frames), lambda b, h: (b * heads + h, 0, 0))

    def block(v, place):
        if v.ndim == 3:
            return pl.BlockSpec((1, HEAD_DIM, span), lambda b, h: (place, h, 0))
        return pl.BlockSpec((HEAD_DIM, span), lambda b, h: (place + h, 0))

    grads = grads[0] + grads[1]
    return pl.pallas_call(
        lambda *refs: attend_back_kernel(span, 1.0 / math.sqrt(HEAD_DIM), *refs),
        grid=(clips, heads),
        in_specs=head_rows(frames, heads, half)
        + [pl.BlockSpec((16, frames), lambda b, h: (b, 0)), vec]
        + [block(*g) for g in grads],
        out_specs=pl.BlockSpec((3, HEAD_DIM, frames), lambda b, h: (0, h, b)),
        out_shape=sds((3, heads * HEAD_DIM, clips * frames), bf16),
        scratch_shapes=[
            pltpu.VMEM((HEAD_DIM, frames), f32),
            pltpu.VMEM((HEAD_DIM, frames), f32),
            pltpu.VMEM((HEAD_DIM, frames), bf16),
        ],
        compiler_params=params(),
        cost_estimate=pl.CostEstimate(
            flops=clips * heads * frames * frames * 4000,
            bytes_accessed=qkv.size * 6 // halves,
            transcendentals=clips * heads * frames * frames,
        ),
        name="attend_back",
    )(qkv, qkv, qkv, mask, lse, *[v for v, _ in grads])


def gelu_parts(v):
    bell = jnp.exp2(v * v * (-0.5 * LOG2E))
    t = 1.0 / (1.0 + (0.3275911 / math.sqrt(2.0)) * jnp.abs(v))
    poly = t * (
        0.5 * 0.254829592
        + t * (0.5 * -0.284496736 + t * (0.5 * 1.421413741 + t * (0.5 * -1.453152027 + t * (0.5 * 1.061405429))))
    )
    tail = poly * bell
    return jnp.where(v < 0.0, tail, 1.0 - tail), bell * (1.0 / math.sqrt(2.0 * math.pi))


def feed_kernel(count, own, tile, refs):
    ns, gs = refs[:count], refs[count : 2 * count]
    up_ref, down_ref, bias_ref = refs[2 * count : 2 * count + 3]
    act_ref, back_ref, grad_own, grad_other, out_own, out_other, sum_ref, n_now, g_now = refs[2 * count + 3 :]
    width = n_now.shape[1]
    hidden = act_ref.shape[1]
    rows = ns[0].shape[0]
    for j in range(count):
        n_now[j * rows : (j + 1) * rows, :] = ns[j][...]
        g_now[j * rows : (j + 1) * rows, :] = gs[j][...]
    up = up_ref[...].reshape(width, hidden)
    down = down_ref[...].reshape(hidden, width)
    for low in range(0, hidden, tile):
        cols = slice(low, low + tile)
        before = nn(n_now[...], up[:, cols]) + bias_ref[:, cols]
        grad_act = nt(g_now[...], down[cols, :])
        cumulative, density = gelu_parts(before)
        act_ref[:, cols] = (before * cumulative).astype(bf16)
        grad = ((cumulative + before * density) * grad_act).astype(bf16)
        back_ref[:, cols] = grad
        sum_ref[:, cols] = jnp.sum(grad.astype(f32), axis=0, keepdims=True)
    mine = own * rows
    grad_own[...] = nt(back_ref[:mine, :], up)
    grad_other[...] = nt(back_ref[mine:, :], up).astype(bf16)
    out_own[...] = nn(act_ref[:mine, :], down)
    out_other[...] = nn(act_ref[mine:, :], down).astype(bf16)


def feed(normed, grad, own, rows, weights, bias):
    count = len(normed)
    width = normed[0][0].shape[1]
    hidden = bias.shape[1]
    tile = 256 if hidden % 256 == 0 else hidden

    def whole(shape):
        return pl.BlockSpec(shape, lambda i: (0,) * len(shape))

    if len(weights) == 1:
        pairs = weights[0].shape[0]
        weights = weights * 2
        weight_specs = [pl.BlockSpec((pairs, hidden // pairs, width), lambda i, j=j: (0, j, 0)) for j in range(2)]
    else:
        weight_specs = [whole(w.shape) for w in weights]
    shapes = [
        sds((count * rows, hidden), bf16),
        sds((count * rows, hidden), bf16),
        sds((own * rows, width), f32),
        sds(((count - own) * rows, width), bf16),
        sds((own * rows, width), f32),
        sds(((count - own) * rows, width), bf16),
        sds((1, hidden), f32),
    ]
    return pl.pallas_call(
        lambda *refs: feed_kernel(count, own, tile, refs),
        grid=(1,),
        in_specs=[pl.BlockSpec((rows, width), lambda i, at=at: (at, 0)) for _, at in normed + grad]
        + weight_specs
        + [whole((1, hidden))],
        out_specs=[whole(v.shape) for v in shapes],
        out_shape=shapes,
        scratch_shapes=[pltpu.VMEM((count * rows, width), bf16)] * 2,
        compiler_params=params(),
        cost_estimate=pl.CostEstimate(
            flops=8 * count * rows * width * hidden,
            bytes_accessed=4 * width * hidden + 16 * count * rows * width,
            transcendentals=count * rows * hidden,
        ),
        name="feed",
    )(*[v for v, _ in normed + grad], *weights, bias)


def project(rank, blocks, small, weight, halves):
    count = len(blocks)
    rows, width = blocks[0].shape
    shards, lines_count, features = small.shape
    own_rows = width // shards
    slab = features // 3
    cut = slab // halves
    sub = math.gcd(rows, 256)

    def kernel(rank_ref, small_ref, w_ref, *refs):
        xs = refs[:count]
        normed_ref, qkv_ref, lines_ref, turned, bias, now = refs[count:]
        at = pl.program_id(0)

        @pl.when(at == 0)
        def _():
            lines_ref[...] = jnp.concatenate(
                [small_ref[f, :, :own_rows].astype(f32) for f in range(shards)], axis=1
            )
            turned[...] = w_ref[...].T
            for r in range(count):

                @pl.when(rank_ref[0] == r)
                def _(r=r):
                    parts = []
                    for h in range(halves):
                        cols = slice(r * slab + h * cut, r * slab + (h + 1) * cut)
                        parts += [lines_ref[2:3, cols], jnp.zeros((1, cut), f32), lines_ref[3:4, cols]]
                    row = jnp.concatenate(parts, axis=1)
                    bias[...] = jnp.broadcast_to(row, (8, features)).T

        for j in range(count):

            @pl.when(at == j)
            def _(j=j):
                now[...] = xs[j][...]

        for t in range(0, rows, sub):
            plain, _ = normalized(now[t : t + sub, :].astype(f32))
            normed = (plain * lines_ref[0:1, :] + lines_ref[1:2, :]).astype(bf16)
            normed_ref[t : t + sub, :] = normed
            qkv_ref[:, t : t + sub] = (nt(turned[...], normed) + bias[:, 0:1]).astype(bf16)

    return pl.pallas_call(
        kernel,
        grid=(count,),
        in_specs=[
            smem(),
            pl.BlockSpec(small.shape, lambda i: (0, 0, 0)),
            pl.BlockSpec(weight.shape, lambda i: (0, 0)),
        ]
        + [pl.BlockSpec((rows, width), lambda i: (0, 0))] * count,
        out_specs=[
            pl.BlockSpec((rows, width), lambda i: (i, 0)),
            pl.BlockSpec((features, rows), lambda i: (0, i)),
            pl.BlockSpec((lines_count, width), lambda i: (0, 0)),
        ],
        out_shape=[
            sds((count * rows, width), bf16),
            sds((features, count * rows), bf16),
            sds((lines_count, width), f32),
        ],
        scratch_shapes=[
            pltpu.VMEM((features, width), bf16),
            pltpu.VMEM((features, 8), f32),
            pltpu.VMEM((rows, width), bf16),
        ],
        compiler_params=params(),
        cost_estimate=pl.CostEstimate(
            flops=2 * count * rows * width * features,
            bytes_accessed=2 * width * features + 6 * count * rows * width,
            transcendentals=count * rows,
        ),
        name="project",
    )(rank, small, weight, *blocks)


def project_back(grads, weight, blocks, places, groups):
    count, halves = len(blocks), len(grads)
    rows, width = blocks[0].shape
    features = weight.shape[1]
    own = count // 2
    sub = math.gcd(rows, 256)

    def kernel(w_ref, *refs):
        g_refs, xs = refs[:halves], refs[halves : halves + count]
        own_ref, other_ref, sums_ref, bias_ref, now = refs[halves + count :]
        at = pl.program_id(0)
        for j in range(count):

            @pl.when(at == j)
            def _(j=j):
                now[...] = xs[j][...]

        @pl.when(at == 0)
        def _():
            sums_ref[...] = jnp.zeros(sums_ref.shape, f32)
            bias_ref[...] = jnp.zeros(bias_ref.shape, f32)

        for t in range(0, rows, sub):
            cut = slice(t, t + sub)
            turned = jnp.concatenate([g[:, cut] for g in g_refs], axis=0).T
            grad = nt(turned, w_ref[...])
            plain, _ = normalized(now[cut, :].astype(f32))
            sums_ref[0:1, :] += jnp.sum(grad * plain, axis=0, keepdims=True)
            sums_ref[1:2, :] += jnp.sum(grad, axis=0, keepdims=True)
            bias_ref[...] += nn(jnp.ones((8, sub), bf16), turned)

            @pl.when(at < own)
            def _(cut=cut, grad=grad):
                own_ref[cut, :] = grad

            @pl.when(at >= own)
            def _(cut=cut, grad=grad):
                other_ref[cut, :] = grad.astype(bf16)

    return pl.pallas_call(
        kernel,
        grid=(count,),
        in_specs=[pl.BlockSpec(weight.shape, lambda i: (0, 0))]
        + [
            pl.BlockSpec((g.shape[0], rows), lambda i: (0, i // own * groups + i % own + places[0])) for g in grads
        ]
        + [pl.BlockSpec((rows, width), lambda i: (0, 0))] * count,
        out_specs=[
            pl.BlockSpec((rows, width), lambda i: (jnp.minimum(i, own - 1), 0)),
            pl.BlockSpec((rows, width), lambda i: (jnp.maximum(i - own, 0), 0)),
            pl.BlockSpec((8, width), lambda i: (0, 0)),
            pl.BlockSpec((8, features), lambda i: (0, 0)),
        ],
        out_shape=[
            sds((own * rows, width), f32),
            sds((own * rows, width), bf16),
            sds((8, width), f32),
            sds((8, features), f32),
        ],
        scratch_shapes=[pltpu.VMEM((rows, width), bf16)],
        compiler_params=params(),
        cost_estimate=pl.CostEstimate(
            flops=2 * count * rows * width * features,
            bytes_accessed=2 * width * features + 8 * count * rows * width,
            transcendentals=count * rows,
        ),
        name="project_back",
    )(weight, *grads, *blocks)


def by_source(r, groups):
    return [((src % groups - r % groups) % groups, (src // groups) ^ (r // groups)) for src in range(2 * groups)]


def finish_heads(rank, blocks, halves, groups):
    _, rows, features = blocks[0].shape
    ranks = 2 * groups
    slab = features // 4
    cut = slab // halves
    width = slab * ranks
    starts = [0] + [slab + 3 * cut * h for h in range(1, halves)]

    def kernel(rank_ref, *refs):
        ins, outs = refs[:-4], refs[-4:]
        for r in range(ranks):

            @pl.when(rank_ref[0] == r)
            def _(r=r):
                order = by_source(r, groups)
                for i in range(3):
                    outs[i][...] = jnp.concatenate(
                        [
                            ins[step][flip, :, low + i * cut : low + (i + 1) * cut]
                            for step, flip in order
                            for low in starts
                        ],
                        axis=1,
                    ).astype(f32)
                outs[3][...] = jnp.concatenate(
                    [ins[step][flip, :, 3 * cut : 3 * cut + slab] for step, flip in order], axis=1
                ).astype(f32)

    return pl.pallas_call(
        kernel,
        in_specs=[smem()] + vmem(groups),
        out_specs=vmem(4),
        out_shape=[sds((rows, width), f32)] * 4,
        compiler_params=params(),
        cost_estimate=pl.CostEstimate(flops=0, bytes_accessed=24 * rows * width, transcendentals=0),
        name="finish_heads",
    )(rank, *blocks)


def finish_feed(rank, ups, downs, pairs, groups):
    _, rows, rank_hidden = ups[0].shape
    piece, width = downs[0].shape
    ranks = 2 * groups

    def kernel(rank_ref, *refs):
        up_refs, down_refs, up_out, down_out = refs[:groups], refs[groups : 2 * groups], refs[-2], refs[-1]
        for r in range(ranks):

            @pl.when(rank_ref[0] == r)
            def _(r=r):
                for zx in range(pairs):
                    up_out[:, zx * ranks * piece : (zx + 1) * ranks * piece] = jnp.concatenate(
                        [
                            up_refs[step][flip, :, zx * piece : (zx + 1) * piece]
                            for step, flip in by_source(r, groups)
                        ],
                        axis=1,
                    ).astype(f32)
                for step in range(groups):
                    at = (r + step) % groups * piece
                    down_out[at : at + piece, :] = down_refs[step][...].astype(f32)

    return pl.pallas_call(
        kernel,
        in_specs=[smem()] + vmem(2 * groups),
        out_specs=vmem(2),
        out_shape=[sds((rows, rank_hidden * ranks), f32), sds((groups * piece, width), f32)],
        compiler_params=params(),
        cost_estimate=pl.CostEstimate(flops=0, bytes_accessed=12 * rows * rank_hidden * ranks, transcendentals=0),
        name="finish_feed",
    )(rank, *ups, *downs)


def pick(where, q, k, v, up, o, small, ranks, halves, pairs):
    own_rows, width = q.shape
    slab = width // ranks
    cut = slab // halves
    piece = up.shape[1] // (ranks * pairs)
    base = -(-own_rows // 16) * 16
    extra = small.shape[0]

    def kernel(where_ref, q_ref, k_ref, v_ref, up_ref, o_ref, small_ref, *outs):
        for side in range(2):
            pay, ups, half = outs[3 * side : 3 * side + 3]
            pay[base:, :] = jnp.zeros((extra, 3 * slab), bf16)
            pay[base:, : small.shape[1]] = small_ref[...]
            for r in range(ranks):

                @pl.when(where_ref[side] == r)
                def _(pay=pay, ups=ups, r=r):
                    parts = [
                        w[:, r * slab + h * cut : r * slab + (h + 1) * cut]
                        for h in range(halves)
                        for w in (q_ref, k_ref, v_ref)
                    ]
                    pay[:own_rows, :] = jnp.concatenate(parts, axis=1)
                    ups[...] = jnp.concatenate(
                        [up_ref[:, (c * ranks + r) * piece : (c * ranks + r + 1) * piece] for c in range(pairs)],
                        axis=1,
                    )

            for c in range(2):

                @pl.when(where_ref[2] == (c ^ side))
                def _(half=half, c=c):
                    half[...] = o_ref[:, c * width // 2 : (c + 1) * width // 2]

    shapes = [
        sds((base + extra, 3 * slab), bf16),
        sds((own_rows, piece * pairs), bf16),
        sds((own_rows, width // 2), bf16),
    ]
    return pl.pallas_call(
        kernel,
        in_specs=[smem()] + vmem(6),
        out_specs=vmem(6),
        out_shape=shapes * 2,
        compiler_params=params(),
        cost_estimate=pl.CostEstimate(flops=0, bytes_accessed=10 * up.size, transcendentals=0),
        name="pick",
    )(where, q, k, v, up, o, small)


def place(blocks, slots, pieces):
    count, (_, width) = len(blocks), blocks[0].shape

    def kernel(slots_ref, *refs):
        for i in range(count):
            for target, spans in zip(refs[count:], pieces, strict=True):
                for j, (low, high) in enumerate(spans):
                    target[slots_ref[i] * len(spans) + j] = refs[i][low:high, :]

    return pl.pallas_call(
        kernel,
        in_specs=[smem()] + vmem(count),
        out_specs=vmem(len(pieces)),
        out_shape=[
            sds((count * len(spans), spans[0][1] - spans[0][0], width), blocks[0].dtype) for spans in pieces
        ],
        compiler_params=params(),
        cost_estimate=pl.CostEstimate(
            flops=0, bytes_accessed=4 * count * blocks[0].size, transcendentals=0
        ),
        name="place",
    )(slots, *blocks)


def merge(slots, x, out_full, lines, blocks, halves, token_parts):
    tokens, width = x.shape
    count = len(blocks)
    hs = blocks[0][0].shape[0]
    slab = hs * halves
    rows = tokens // token_parts

    def kernel(slots_ref, x_ref, w_ref, lines_ref, *refs):
        ins, mixed, after = refs[: count * halves], refs[count * halves], refs[count * halves + 1]
        outs = refs[count * halves + 2 :]
        for i in range(count):
            for h in range(halves):
                at = pl.multiple_of(slots_ref[i] * slab + h * hs, 16)
                mixed[pl.ds(at, hs), :] = ins[i * halves + h][...]
        for t in range(token_parts):
            cols = slice(t * rows, (t + 1) * rows)
            total = nn(mixed[:, cols].T, w_ref[...]) + lines_ref[4:5, :] + x_ref[cols, :].astype(f32)
            after[cols, :] = total
            plain, _ = normalized(total)
            outs[t][...] = (plain * lines_ref[5:6, :] + lines_ref[6:7, :]).astype(bf16)

    made = pl.pallas_call(
        kernel,
        in_specs=[smem()] + vmem(3 + count * halves),
        out_specs=vmem(2 + token_parts),
        out_shape=[sds((width, tokens), bf16), sds((tokens, width), f32)]
        + [sds((rows, width), bf16)] * token_parts,
        compiler_params=params(),
        cost_estimate=pl.CostEstimate(
            flops=2 * tokens * width * width, bytes_accessed=2 * width * width + 12 * tokens * width, transcendentals=tokens
        ),
        name="merge",
    )(slots, x, out_full, lines, *[b for source in blocks for b in source])
    return made[0], made[1], list(made[2:])


def turn(slots, after1, near, fars, live_grad, lines, out_full, halves, groups):
    tokens, width = after1.shape
    ranks = 2 * groups
    slab = width // ranks
    hs = slab // halves
    parts = len(fars)
    rows = tokens // parts
    per = len(fars[0])

    def kernel(slots_ref, after_ref, near_ref, live_ref, g_ref, w_ref, *refs):
        far_refs = refs[: parts * per]
        grad_ref, low_ref, sums_ref = refs[parts * per : parts * per + 3]
        outs = refs[parts * per + 3 :]
        sums = [jnp.zeros((1, width), f32) for _ in range(4)]
        for t in range(parts):
            cut = slice(t * rows, (t + 1) * rows)
            grad = near_ref[cut, :]
            for j in range(per):
                grad = grad + far_refs[t * per + j][...].astype(f32)
            plain, scale = normalized(after_ref[cut, :])
            live = live_ref[cut, :].astype(f32)
            total = live + norm_back(plain, scale, grad * g_ref[5:6, :])
            grad_ref[cut, :] = total
            low = total.astype(bf16)
            low_ref[cut, :] = low
            for i, term in enumerate((grad * plain, grad, low.astype(f32), live)):
                sums[i] = sums[i] + jnp.sum(term, axis=0, keepdims=True)
        for i in range(4):
            sums_ref[i : i + 1, :] = sums[i]
        low = low_ref[...]

        def of_rank(flip, step, h):
            at = pl.multiple_of(slots_ref[flip * groups + step] * slab + h * hs, 16)
            return nt(w_ref[pl.ds(at, hs), :], low).astype(bf16)

        for h in range(halves):
            for step in range(1, groups):
                for flip in range(2):
                    outs[h * (groups - 1) + step - 1][flip] = of_rank(flip, step, h)
        near_outs = outs[halves * (groups - 1) :]
        for h in range(halves):
            near_outs[0][h * hs : (h + 1) * hs, :] = of_rank(0, 0, h)
            near_outs[1][h * hs : (h + 1) * hs, :] = of_rank(1, 0, h)

    fars_count = halves * (groups - 1)
    made = pl.pallas_call(
        kernel,
        in_specs=[smem()] + vmem(5 + parts * per),
        out_specs=vmem(3 + fars_count + 2),
        out_shape=[sds((tokens, width), f32), sds((tokens, width), bf16), sds((4, width), f32)]
        + [sds((2, hs, tokens), bf16)] * fars_count
        + [sds((slab, tokens), bf16)] * 2,
        compiler_params=params(),
        cost_estimate=pl.CostEstimate(
            flops=2 * tokens * width * width, bytes_accessed=2 * width * width + 16 * tokens * width, transcendentals=tokens
        ),
        name="turn",
    )(slots, after1, near, live_grad, lines, out_full, *[v for part in fars for v in part])
    sent = [[made[3 + h * (groups - 1) + step] for step in range(groups - 1)] for h in range(halves)]
    return made[0], made[1], made[2], sent, made[-2], made[-1]


def part_ways(x_ref, value, kept, sent):
    depth, rows = kept.shape[:2]
    for flip in range(2):

        @pl.when(x_ref[0] == flip)
        def _(flip=flip):
            for z in range(depth):
                low, other = (2 * z + flip) * rows, (2 * z + 1 - flip) * rows
                kept[z] = value[low : low + rows, :]
                sent[z] = value[other : other + rows, :]


def weight_grad(lefts, rights, wide=1, into=None):
    rows = lefts[0][0].shape[1]
    cols = rights[0][0].shape[1]
    tile = 256 if cols % 256 == 0 else cols
    count, right_count = len(lefts), len(rights)

    def ends_of(parts):
        return [sum(size for _, _, size in parts[:i]) for i in range(len(parts) + 1)]

    left_ends, right_ends = ends_of(lefts), ends_of(rights)
    tokens = left_ends[-1]

    def kernel(*refs):
        left_refs, right_refs = refs[:count], refs[count : count + right_count]
        out_ref, turned, joined = refs[-3:]

        @pl.when(pl.program_id(0) == 0)
        def _():
            for i in range(count):
                turned[:, left_ends[i] : left_ends[i + 1]] = left_refs[i][...].T

        for i in range(right_count):
            joined[right_ends[i] : right_ends[i + 1], :] = right_refs[i][...]
        out_ref[...] = nn(turned[...], joined[...]).astype(bf16)

    whole = [pl.BlockSpec((size, rows), lambda i, at=at: (at, 0)) for _, at, size in lefts]
    strips = [pl.BlockSpec((size, tile), lambda i, at=at: (at, i)) for _, at, size in rights]
    shift = 0 if into is None else cols // tile
    return pl.pallas_call(
        kernel,
        grid=(cols // tile,),
        in_specs=whole + strips + ([] if into is None else [pl.BlockSpec(memory_space=pl.ANY)]),
        out_specs=pl.BlockSpec((rows, tile), lambda i: (0, i + shift)),
        out_shape=sds((rows, wide * cols), bf16),
        input_output_aliases={} if into is None else {count + right_count: 0},
        scratch_shapes=[pltpu.VMEM((rows, tokens), bf16), pltpu.VMEM((tokens, tile), bf16)],
        compiler_params=params(),
        cost_estimate=pl.CostEstimate(
            flops=2 * tokens * rows * cols, bytes_accessed=2 * (tokens * (rows + cols) + rows * cols), transcendentals=0
        ),
        name="weight_grad",
    )(*[v for v, _, _ in lefts + rights], *([] if into is None else [into]))


def head_grad(x_at, normed, grad_heads, depth, extra=()):
    tokens, width = normed.shape
    features = grad_heads.shape[0]
    tile = 512 if tokens % 512 == 0 else tokens
    share = width // (2 * depth)
    cols = features + (extra[0].shape[1] if extra else 0)

    def kernel(x_ref, n_ref, g_ref, *refs):
        kept, sent, total = refs[-3:]
        part = nn(g_ref[...], n_ref[...])

        @pl.when(pl.program_id(0) == 0)
        def _():
            total[...] = part

        @pl.when(pl.program_id(0) > 0)
        def _():
            total[...] += part

        @pl.when(pl.program_id(0) == pl.num_programs(0) - 1)
        def _():
            value = total[...].astype(bf16).T
            if extra:
                more = refs[0][...].astype(f32)
                for v in refs[1:-3]:
                    more = more + v[...].astype(f32)
                value = jnp.concatenate([value, more.astype(bf16)], axis=1)
            part_ways(x_ref, value, kept, sent)

    return pl.pallas_call(
        kernel,
        grid=(tokens // tile,),
        in_specs=[
            smem(),
            pl.BlockSpec((tile, width), lambda i: (i, 0)),
            pl.BlockSpec((features, tile), lambda i: (0, i)),
        ]
        + [pl.BlockSpec(v.shape, lambda i: (0, 0)) for v in extra],
        out_specs=[pl.BlockSpec((depth, share, cols), lambda i: (0, 0, 0))] * 2,
        out_shape=[sds((depth, share, cols), bf16)] * 2,
        scratch_shapes=[pltpu.VMEM((features, width), f32)],
        compiler_params=params(),
        cost_estimate=pl.CostEstimate(
            flops=2 * tokens * width * features, bytes_accessed=2 * tokens * (width + features), transcendentals=0
        ),
        name="head_grad",
    )(x_at, normed, grad_heads, *extra)


def out_grad_halves(core_at, mixed, grad):
    rows, tokens = mixed.shape
    width = grad.shape[1]
    half = width // 2

    def kernel(core_ref, m_ref, g_ref, kept, sent):
        value = nn(m_ref[...], g_ref[...]).astype(bf16)
        for core in range(2):

            @pl.when(core_ref[0] == core)
            def _(core=core):
                kept[...] = value[:, core * half : (core + 1) * half]
                sent[...] = value[:, (1 - core) * half : (2 - core) * half]

    return pl.pallas_call(
        kernel,
        in_specs=[smem()] + vmem(2),
        out_specs=vmem(2),
        out_shape=[sds((rows, half), bf16)] * 2,
        compiler_params=params(),
        cost_estimate=pl.CostEstimate(
            flops=2 * rows * tokens * width, bytes_accessed=4 * rows * width, transcendentals=0
        ),
        name="out_grad_halves",
    )(core_at, mixed, grad)


def out_grad_parts(seq_at, kept, came, groups):
    rows, half = kept.shape
    slab = half // groups

    def kernel(seq_ref, a_ref, b_ref, *outs):
        value = (a_ref[...].astype(f32) + b_ref[...].astype(f32)).astype(bf16)
        for at in range(groups):

            @pl.when(seq_ref[0] == at)
            def _(at=at):
                for step in range(groups):
                    low = (at + step) % groups * slab
                    outs[step][...] = value[:, low : low + slab]

    return pl.pallas_call(
        kernel,
        in_specs=[smem()] + vmem(2),
        out_specs=vmem(groups),
        out_shape=[sds((rows, slab), bf16)] * groups,
        compiler_params=params(),
        cost_estimate=pl.CostEstimate(flops=0, bytes_accessed=6 * rows * half, transcendentals=0),
        name="out_grad_parts",
    )(seq_at, kept, came)


def local(
    frames_in,
    clip_lengths,
    norm1_gain,
    norm1_bias,
    q_weight,
    q_bias,
    k_weight,
    v_weight,
    v_bias,
    o_weight,
    o_bias,
    norm2_gain,
    norm2_bias,
    up_weight,
    up_bias,
    down_weight,
    down_bias,
    out_grad,
):
    clip_count, local_frames, width = frames_in.shape
    hidden = up_weight.shape[1]
    groups = lax.axis_size("seq")
    shards = lax.axis_size("fsdp")
    pairs = shards // 2
    depth = pairs // 2
    ranks = groups * 2
    frames = local_frames * groups
    assert clip_count == 1
    tokens = clip_count * local_frames
    head_count = width // HEAD_DIM
    heads = head_count // ranks
    halves = 2 if heads % 2 == 0 else 1
    slab = heads * HEAD_DIM
    cut = slab // halves
    own_rows = width // shards
    own_hidden = hidden // shards
    piece = own_hidden * 2 // ranks
    rank_hidden = piece * pairs
    clips = 2 * clip_count
    token_parts = 2
    part_rows = tokens // token_parts
    fsdp = lax.axis_index("fsdp")
    seq = lax.axis_index("seq")
    core, pair = fsdp % 2, fsdp // 2
    xpos, zpos = pair % 2, pair // 2
    rank = core * groups + seq
    peer = (1 - core) * groups + seq

    core_way = [(i, i ^ 1) for i in range(shards)]
    x_way = [(i, i ^ 2) for i in range(shards)]

    def over_core(v):
        return lax.ppermute(v, "fsdp", core_way)

    def over_x(v):
        return lax.ppermute(v, "fsdp", x_way)

    def over_z(v, step):
        return lax.ppermute(v, "fsdp", [(i, (i + 4 * step) % shards) for i in range(shards)])

    def from_seq(v, step):
        return lax.ppermute(v, "seq", [(i, (i - step) % groups) for i in range(groups)])

    def to_seq(v, step):
        return from_seq(v, -step % groups)

    steps = range(1, groups)

    def by_core(mine, other):
        return jnp.where(
            core == 0, jnp.concatenate([mine, other]), jnp.concatenate([other, mine])
        )

    slots = []
    for step in range(depth):
        for flip in range(2):
            slots.append(((zpos - step) % depth) * 2 + (xpos ^ flip))
    slots = jnp.stack(slots).astype(jnp.int32)

    def spread_z(payload):
        return [payload] + [over_z(payload, step) for step in range(1, depth)]

    def spread_x(blocks):
        return [v for block in blocks for v in (block, over_x(block))]

    small = [norm1_gain, norm1_bias, q_bias, v_bias, o_bias, norm2_gain, norm2_bias, down_bias]
    small = jnp.concatenate([jnp.stack(small), up_bias.reshape(hidden // width, own_rows)])
    small_rows = -(-small.shape[0] // 16) * 16
    small = jnp.pad(small, ((0, small_rows - small.shape[0]), (0, 0)))
    where = jnp.stack([rank, peer, core]).astype(jnp.int32)
    pay, up_mine, out_mine, pay_other, up_other, out_other = pick(
        where, q_weight, k_weight, v_weight, up_weight, o_weight, small, ranks, halves, pairs
    )
    base = -(-own_rows // 16) * 16
    pay_rows = base + small_rows
    frames_own = frames_in.reshape(tokens, width)
    pay_full = by_core(pay, over_core(pay_other))
    pay_z = spread_z(pay_full)
    frames_side = [from_seq(tie(frames_own, pay_full), step) for step in steps]

    up_own = by_core(up_mine, over_core(up_other))
    down_own = lax.dynamic_slice_in_dim(down_weight, seq * piece, piece, 0)
    out_own = by_core(out_mine, over_core(out_other))
    same_core = [[i for i in range(shards) if i % 2 == c] for c in range(2)]

    def over_chips(v):
        return lax.all_gather(v, "fsdp", axis=0, axis_index_groups=same_core)

    out_half = over_chips(out_own).reshape(width, width // 2)
    feed_own = jnp.concatenate([up_own.reshape(-1, width), down_own])
    gathered = over_chips(tie(feed_own, *pay_z[1:]))
    up_rows = up_own.size // width
    if rank_hidden == width:
        feed_weights = [gathered]
    else:
        feed_weights = [
            gathered[:, :up_rows].reshape(width, rank_hidden),
            gathered[:, up_rows:].reshape(rank_hidden, width),
        ]

    pay_z[depth // 2] = tie(pay_z[depth // 2], *frames_side)
    pay_all = spread_x(pay_z)
    frames_near = over_core(tie(frames_own, *pay_all))
    lengths_sent = jnp.broadcast_to(clip_lengths.astype(f32)[:, None], (clip_count, 128))
    lengths_near = over_core(tie(lengths_sent, *pay_z[1:]))
    frames_cross = [over_core(tie(v, *pay_all)) for v in frames_side]

    positions = jnp.concatenate(
        [
            ((seq + step) % groups) * local_frames + jnp.arange(local_frames, dtype=jnp.int32)
            for step in range(groups)
        ]
    )
    lengths = jnp.concatenate([clip_lengths, lengths_near[:, 0].astype(jnp.int32)])
    live = positions[None, :] < lengths[:, None]
    live_own = live[:clip_count, :local_frames].reshape(tokens, 1)
    mask = jnp.where(live, 0.0, NEGATIVE).astype(bf16)
    mask = jnp.pad(mask[:, None, :], ((0, 0), (0, 15), (0, 0))).reshape(clips * 16, frames)
    live_grad = jnp.where(live_own, out_grad.reshape(tokens, width), 0.0).astype(bf16)

    grad_side = [from_seq(tie(live_grad, *frames_side), step) for step in steps]

    qkv_part, small_part = place(
        pay_all,
        slots,
        [
            [(0, own_rows), (pay_rows, pay_rows + own_rows)],
            [(base, pay_rows), (pay_rows + base, 2 * pay_rows)],
        ],
    )
    qkv_full = qkv_part.reshape(width, 3 * slab)
    ubias = small_part[:, 8 : 8 + hidden // width, :own_rows].astype(f32).reshape(pairs, ranks, piece)
    ubias = lax.dynamic_index_in_dim(ubias, rank, 1, keepdims=False).reshape(1, rank_hidden)


    def to_z(both):
        blocks = [
            lax.dynamic_index_in_dim(both, (zpos + step) % depth, 0, keepdims=False) for step in range(depth)
        ]
        return blocks[0], [v.astype(bf16) for v in blocks[1:]]

    def reduce_z(kept, sent, parted=True):
        both = kept.astype(f32) + over_x(sent).astype(f32)
        return to_z(both) if parted else both

    def reduce_end(own, sent):
        total = own
        for step in range(1, depth):
            total = total + over_z(sent[step - 1], step).astype(f32)
        return total.astype(bf16)

    def along_seq(v):
        return [v] + [from_seq(v, step) for step in steps]

    def own_of_ranks(v):
        blocks = v.reshape(2, own_rows, -1)
        keep = lax.dynamic_index_in_dim(blocks, core, 0, keepdims=False)
        other = over_core(lax.dynamic_index_in_dim(blocks, 1 - core, 0, keepdims=False))
        return jnp.stack([keep, other])

    rank_at = rank.reshape(1).astype(jnp.int32)
    seq_at = seq.reshape(1).astype(jnp.int32)
    frames_all = [frames_own] + frames_side + [frames_near] + frames_cross
    normed1, qkv, lines = project(rank_at, frames_all, small_part, qkv_full, halves)
    grad_cross_near = over_core(tie(live_grad, lines))
    grad_cross = [over_core(tie(v, lines)) for v in grad_side]
    grad_near = [(v, t) for v in (live_grad, grad_cross_near) for t in range(token_parts)]
    grad_far = [[(v, t) for v in grad_side + grad_cross] for t in range(token_parts)]

    out_half = out_half.reshape(width, width // 2)
    out_rest = over_core(out_half)
    out_full = jnp.where(
        core == 0,
        jnp.concatenate([out_half, out_rest], axis=1),
        jnp.concatenate([out_rest, out_half], axis=1),
    )
    half_heads = heads // halves
    logs, tops, sources = [], [], []
    mixed_blocks = [[] for _ in range(ranks)]

    def flat(v):
        return jnp.swapaxes(v, 0, 1).reshape(v.shape[1], tokens)

    for half in range(halves):
        if half:
            qkv = tie(qkv, grad_cross_near, *grad_cross)
        near, far, log_half, top_half = attend(qkv, mask, clips, half_heads, half, halves, groups)
        logs.append(log_half)
        tops.append(top_half)
        came = [near] + [to_seq(far[step - 1], step) for step in steps]
        for step, v in enumerate(came):
            mixed_blocks[step].append(flat(v[:clip_count]))
            mixed_blocks[groups + step].append(flat(over_core(v[clip_count:])))
    sources = [
        (core ^ flip) * groups + (seq - step) % groups for flip in range(2) for step in range(groups)
    ]
    sources = jnp.stack(sources).astype(jnp.int32)
    mixed_own, after1, normed2_own = merge(
        sources, frames_own, out_full, lines, mixed_blocks, halves, token_parts
    )

    normed2_side = [[from_seq(v, step) for step in steps] for v in normed2_own]
    normed2_near = normed2_own + [over_core(v) for v in normed2_own]

    def parts_of(arrays):
        return [(v, 0) for v in arrays]

    act_near, back_near, grad2_own, grad2_other, fed_own, fed_other, sums = feed(
        parts_of(normed2_near), grad_near, token_parts, part_rows, feed_weights, ubias
    )
    normed2_side = [[tie(v, sums) for v in side] for side in normed2_side]
    normed2_far = [side + [over_core(v) for v in side] for side in normed2_side]
    normed2_far[0][0] = tie(normed2_far[0][0], *sum(normed2_side, []))
    act_far, back_far, grad2_sent, fed_parts = [], [], [], []

    def far_sums(own, other):
        both = (own + over_core(other).astype(f32)).astype(bf16)
        return [both[i * part_rows : (i + 1) * part_rows] for i in range(len(steps))]

    for t in range(token_parts):
        if t:
            normed2_far[t][0] = tie(normed2_far[t][0], *grad2_sent[t - 1])
        act, back, far_own, far_other, out_own_far, out_other_far, sums_far = feed(
            parts_of(normed2_far[t]), grad_far[t], len(steps), part_rows, feed_weights, ubias
        )
        act_far.append(act)
        back_far.append(back)
        grad2_sent.append(far_sums(far_own, far_other))
        fed_parts.append((out_own_far, out_other_far))
        sums = sums + sums_far

    grad2_far = [[to_seq(v, step) for v, step in zip(part, steps)] for part in grad2_sent]
    grad2_near = grad2_own + over_core(grad2_other).astype(f32)

    def with_sizes(parts):
        return [(v, at, part_rows) for v, at in parts]

    def wholes(arrays):
        return [(v, 0, v.shape[0]) for v in arrays]

    x_at = xpos.reshape(1).astype(jnp.int32)
    lefts = with_sizes(parts_of(normed2_near + sum(normed2_far, [])))
    lefts[0] = (tie(lefts[0][0], grad2_near, *grad2_sent[-1]),) + lefts[0][1:]

    def over_chips_sum(v):
        return lax.psum_scatter(v, "fsdp", scatter_dimension=0, axis_index_groups=same_core, tiled=True)

    rights = wholes([back_near] + back_far)
    acts, cotangents = wholes([act_near] + act_far), with_sizes(grad_near + sum(grad_far, []))
    if rank_hidden == width:
        feed_sum = weight_grad(acts, cotangents, 2, weight_grad(lefts, rights, 2))
        feed_shard = over_chips_sum(feed_sum)
        up_shard, down_shard = feed_shard[:, :width], feed_shard[:, width:]
    else:
        feed_sum = weight_grad(acts, cotangents)
        up_shard, down_shard = over_chips_sum(weight_grad(lefts, rights)), over_chips_sum(feed_sum)

    targets = [
        (core ^ flip) * groups + (seq + step) % groups for flip in range(2) for step in range(groups)
    ]
    targets = jnp.stack(targets).astype(jnp.int32)
    grad_after1, grad_attn, sums2, grad_sent, heads_own, heads_other = turn(
        targets, after1, tie(grad2_near, feed_sum), grad2_far, live_grad, lines, out_full, halves, groups
    )
    half_rows = heads // halves
    heads_cross = over_core(heads_other)
    head_grads, arrived, sides = [], [], []
    for half in range(halves):
        came = [to_seq(v, step) for v, step in zip(grad_sent[half], steps)]
        came = [came[groups - step - 1] for step in steps]
        cross = [over_core(v) for v in came]
        sides.append(came)
        arrived += cross
        head_grads.append(
            [
                [(heads_own, half * half_rows)] + [(v, 0) for v in came],
                [(heads_cross, half * half_rows)] + [(v, 1) for v in cross],
            ]
        )

    out_kept, out_other_half = out_grad_halves(where[2:], mixed_own, grad_attn)
    out_parts = out_grad_parts(seq_at, out_kept, over_core(out_other_half), groups)
    out_sent = list(out_parts[1:])
    out_came = [to_seq(v, step) for v, step in zip(out_sent, steps)]
    def fed_sums(after):
        both = [(mine + over_core(tie(other, after)).astype(f32)).astype(bf16) for mine, other in fed_parts]
        sent = [jnp.concatenate([v[i * part_rows : (i + 1) * part_rows] for v in both]) for i in range(len(steps))]
        return sent, fed_own + over_core(tie(fed_other, after)).astype(f32)

    grad_qkv, x_parts = [], []
    for half in range(halves):
        if half:
            fed_sent, fed_near = fed_sums(x_parts[0][1])
            fed_far = [to_seq(v, step) for v, step in zip(fed_sent, steps)]
            after = [x_parts[0][1], fed_near] + fed_sent
        else:
            after = out_sent + arrived
        own = head_grads[half][0]
        own[0] = (tie(own[0][0], *after), own[0][1])
        grads = attend_back(qkv, mask, head_grads[half], logs[half], clips, half_heads, half, halves, groups)
        grads = grads.reshape(3 * cut, -1)
        if half:
            grads = tie(grads, *fed_far)
        grad_qkv.append(grads)
        x_parts.append(head_grad(x_at, normed1, grads, depth, () if half else [out_parts[0]] + out_came))
    if halves == 1:
        fed_sent, fed_near = fed_sums(x_parts[0][1])
        fed_far = [to_seq(v, step) for v, step in zip(fed_sent, steps)]
    fed = tie(fed_near, x_parts[-1][1])
    for v in fed_far:
        fed = fed + v.astype(f32)
    output = (after1 + (fed + lines[7:8])).astype(bf16).reshape(clip_count, local_frames, width)
    kept, sent = x_parts[0]
    z_parts = [reduce_z(tie(kept, grad_qkv[-1]), sent)]
    feed_last = jnp.concatenate(
        [own_of_ranks(up_shard).reshape(2 * own_rows, rank_hidden), down_shard.reshape(-1, rank_hidden)]
    )
    grad_qkv[-1] = tie(grad_qkv[-1], x_parts[-1][1], *z_parts[0][1])
    far_own, far_other, far_sums1, far_bias = project_back(grad_qkv, qkv_full, frames_side + frames_cross, steps, groups)
    far_cross = over_core(far_other).astype(f32)
    far1 = (far_own + far_cross).astype(bf16)
    far1 = [far1[i * tokens : (i + 1) * tokens] for i in range(len(steps))]
    near_own, near_other, near_sums1, near_bias = project_back(
        [tie(grad_qkv[0], *far1)] + grad_qkv[1:], qkv_full, [frames_own, frames_near], [0], groups
    )
    feed_lasts = along_seq(tie(feed_last, near_other))
    sums1, bias_sums = far_sums1 + near_sums1, far_bias + near_bias
    shard_parts = [reduce_end(tie(z_parts[0][0], near_other), z_parts[0][1])]
    x_sums = [reduce_z(tie(kept, near_other), sent, False) for kept, sent in x_parts[1:]]
    grad_normed1 = near_own + over_core(near_other).astype(f32)
    for v, step in zip(far1, steps):
        grad_normed1 = grad_normed1 + to_seq(v, step).astype(f32)
    plain1, scale1 = normalized(frames_own.astype(f32))
    in_grad = (grad_after1 + norm_back(plain1, scale1, grad_normed1 * lines[0:1])).astype(bf16)

    for both in x_sums:
        shard_parts.append(reduce_end(*to_z(both)))
    heads_last = own_of_ranks(jnp.concatenate(shard_parts, axis=1))

    up_weight_grad, down_weight_grad = finish_feed(
        rank_at,
        [v[: 2 * own_rows].reshape(2, own_rows, rank_hidden) for v in feed_lasts],
        [v[2 * own_rows :].reshape(piece, width) for v in feed_lasts],
        pairs,
        groups,
    )
    q_weight_grad, k_weight_grad, v_weight_grad, o_weight_grad = finish_heads(
        rank_at, along_seq(heads_last), halves, groups
    )

    bias_cols = bias_sums[0].reshape(halves, 3, cut)

    def at_rank(v):
        return lax.dynamic_update_slice_in_dim(jnp.zeros((width,), f32), v, rank * slab, 0)

    up_sums = lax.dynamic_update_index_in_dim(
        jnp.zeros((pairs, ranks, piece), f32), sums.reshape(pairs, piece), rank, 1
    ).reshape(hidden // width, width)
    tops = jnp.stack([jnp.max(v.reshape(clips, half_heads, frames), axis=(0, 2)) for v in tops])
    tops = tops.reshape(heads) / math.sqrt(HEAD_DIM)
    peak_row = lax.dynamic_update_slice_in_dim(
        jnp.full((width,), NEGATIVE, f32), tops, rank * heads, 0
    )
    added = 8 + hidden // width
    stack = jnp.concatenate(
        [
            sums1[:2],
            at_rank(bias_cols[:, 0].reshape(slab))[None],
            at_rank(bias_cols[:, 2].reshape(slab))[None],
            sums2[2:3],
            sums2[:2],
            sums2[3:4],
            up_sums,
            peak_row[None],
        ]
    )
    is_sum = (jnp.arange(added + 1) < added)[:, None]

    def combine(a, b):
        return jnp.where(is_sum, a + b, jnp.maximum(a, b))

    stack = combine(stack, over_core(stack))
    stack = combine(stack, over_x(stack))
    step = 4
    while step < shards:
        stack = combine(stack, lax.ppermute(stack, "fsdp", [(i, i ^ step) for i in range(shards)]))
        step *= 2
    stack = tie(stack, grad_normed1)
    step = 1
    while step < groups:
        stack = combine(stack, lax.ppermute(stack, "seq", [(i, i ^ step) for i in range(groups)]))
        step *= 2
    small_own = lax.dynamic_slice_in_dim(stack[:8], fsdp * own_rows, own_rows, 1)
    up_bias_grad = lax.dynamic_slice_in_dim(stack[8:added].reshape(hidden), fsdp * own_hidden, own_hidden, 0)
    logit_peak = stack[added, :head_count]

    factor = jnp.sqrt(LOGIT_CAP / jnp.maximum(logit_peak, LOGIT_CAP))
    column_factor = jnp.repeat(factor, HEAD_DIM)
    q_weight_clipped = q_weight.astype(f32) * column_factor[None, :]
    k_weight_clipped = k_weight.astype(f32) * column_factor[None, :]
    q_bias_clipped = q_bias.astype(f32) * lax.dynamic_slice_in_dim(
        column_factor, fsdp * own_rows, own_rows, 0
    )
    return (
        output,
        in_grad.reshape(clip_count, local_frames, width),
        small_own[0],
        small_own[1],
        q_weight_grad,
        small_own[2],
        k_weight_grad,
        v_weight_grad,
        small_own[3],
        o_weight_grad,
        small_own[4],
        small_own[5],
        small_own[6],
        up_weight_grad,
        up_bias_grad,
        down_weight_grad,
        small_own[7],
        logit_peak,
        q_weight_clipped,
        q_bias_clipped,
        k_weight_clipped,
    )


def solution(mesh):
    rows, vector, clip = P("fsdp", None), P("fsdp"), P("fsdp", "seq", None)
    return jax.shard_map(
        local,
        mesh=mesh,
        in_specs=(
            clip,
            vector,
            vector,
            vector,
            rows,
            vector,
            rows,
            rows,
            vector,
            rows,
            vector,
            vector,
            vector,
            rows,
            vector,
            rows,
            vector,
            clip,
        ),
        out_specs=(
            clip,
            clip,
            vector,
            vector,
            rows,
            vector,
            rows,
            rows,
            vector,
            rows,
            vector,
            vector,
            vector,
            rows,
            vector,
            rows,
            vector,
            P(),
            rows,
            vector,
            rows,
        ),
        check_vma=False,
    )
```

```python
import math

import jax
import jax.numpy as jnp
from jax import lax
from jax.experimental import pallas as pl
from jax.experimental.pallas import tpu as pltpu
from jax.sharding import PartitionSpec as P

HEAD_DIM = 80
NEGATIVE = -1000000000.0
EPSILON = 1e-05
LOGIT_CAP = 10.0
LOG2E = 1.4426950408889634
VMEM_LIMIT = 56 * 1024 * 1024
f32 = jnp.float32
bf16 = jnp.bfloat16


def dot(left, right, left_dim, right_dim):
    return lax.dot_general(
        left, right, (((left_dim,), (right_dim,)), ((), ())), preferred_element_type=f32
    )


def nt(a, b):
    return dot(a, b, 1, 1)


def nn(a, b):
    return dot(a, b, 1, 0)


def tn(a, b):
    return dot(a, b, 0, 0)


def normalized(rows):
    centred = rows - jnp.mean(rows, axis=-1, keepdims=True)
    spread = jnp.mean(centred * centred, axis=-1, keepdims=True)
    scale = lax.rsqrt(spread + EPSILON)
    return centred * scale, scale


def norm_back(plain, scale, grad):
    first = jnp.mean(grad, axis=-1, keepdims=True)
    second = jnp.mean(grad * plain, axis=-1, keepdims=True)
    return scale * (grad - first - plain * second)


def tie(value, *after):
    return lax.optimization_barrier((value,) + after)[0]


def cost(flops, bytes_accessed, transcendentals):
    return pl.CostEstimate(
        flops=flops // 4, bytes_accessed=bytes_accessed // 4, transcendentals=transcendentals // 4
    )


def params(**more):
    return pltpu.CompilerParams(vmem_limit_bytes=VMEM_LIMIT, **more)


def vmem(count):
    return [pl.BlockSpec(memory_space=pltpu.VMEM)] * count


def smem():
    return pl.BlockSpec(memory_space=pltpu.SMEM)


def sds(shape, dtype):
    return jax.ShapeDtypeStruct(shape, dtype)


def one_row(width):
    return jnp.where(lax.broadcasted_iota(jnp.int32, (16, width), 0) == 0, 1.0, 0.0).astype(bf16)


def attend_kernel(scale2, span, q_ref, k_ref, v_ref, mask_ref, near_ref, far_ref, lse_ref, peak_ref):
    frames = q_ref.shape[1]
    mask_rows = mask_ref[...]
    keys = jnp.concatenate([k_ref[...], mask_rows], axis=0).T
    values = jnp.concatenate([v_ref[...], one_row(frames)], axis=0)
    s = nn(keys, jnp.concatenate([q_ref[...], one_row(frames)], axis=0))
    top = jnp.max(s, axis=0, keepdims=True)
    p = jnp.exp2(s * scale2 - top * scale2).astype(bf16)
    mixed = nn(values, p)
    total = mixed[HEAD_DIM : HEAD_DIM + 1, :]
    mixed = (mixed[:HEAD_DIM, :] * (1.0 / total)).astype(bf16)
    near_ref[0] = mixed[:, :span]
    for step in range(1, frames // span):
        far_ref[step - 1, 0] = mixed[:, step * span : (step + 1) * span]
    lse_ref[0] = top * scale2 + jnp.log2(total)
    peak_ref[0] = jnp.where(mask_rows[0:1, :].astype(f32) == 0.0, top, NEGATIVE)


def head_rows(frames, heads, half):
    return [
        pl.BlockSpec((HEAD_DIM, frames), lambda b, h, i=i: ((3 * half + i) * heads + h, b))
        for i in range(3)
    ]


def attend(qkv, mask, clips, heads, half, halves, groups):
    frames = qkv.shape[1] // clips
    span = frames // groups
    vec = pl.BlockSpec((1, 1, frames), lambda b, h: (b * heads + h, 0, 0))
    return pl.pallas_call(
        lambda *refs: attend_kernel(LOG2E / math.sqrt(HEAD_DIM), span, *refs),
        grid=(clips, heads),
        in_specs=head_rows(frames, heads, half) + [pl.BlockSpec((16, frames), lambda b, h: (b, 0))],
        out_specs=[
            pl.BlockSpec((1, HEAD_DIM, span), lambda b, h: (b, h, 0)),
            pl.BlockSpec((groups - 1, 1, HEAD_DIM, span), lambda b, h: (0, b, h, 0)),
            vec,
            vec,
        ],
        out_shape=[
            sds((clips, heads * HEAD_DIM, span), bf16),
            sds((groups - 1, clips, heads * HEAD_DIM, span), bf16),
            sds((clips * heads, 1, frames), f32),
            sds((clips * heads, 1, frames), f32),
        ],
        compiler_params=params(),
        cost_estimate=pl.CostEstimate(
            flops=clips * heads * frames * frames * 2000,
            bytes_accessed=qkv.size * 3 // halves,
            transcendentals=clips * heads * frames * frames,
        ),
        name="attend",
    )(qkv, qkv, qkv, mask)


def attend_back_kernel(span, scale, *refs):
    q_ref, k_ref, v_ref, mask_ref, lse_ref = refs[:5]
    groups = q_ref.shape[1] // span
    grads = refs[5 : 5 + 2 * groups]
    out_ref, gk, gv, gs = refs[5 + 2 * groups :]
    scale2 = LOG2E * scale
    key_rows = k_ref[...]
    keys = jnp.concatenate([key_rows, mask_ref[...]], axis=0).T
    values = v_ref[...].T
    ones = one_row(span)
    for flip in range(2):

        @pl.when(pl.program_id(0) == flip)
        def _(flip=flip):
            for at in range(groups):
                gs[:, at * span : (at + 1) * span] = grads[flip * groups + at][...].reshape(HEAD_DIM, span)

    for at in range(groups):
        cols = pl.ds(at * span, span)
        q = q_ref[:, cols]
        g = gs[:, cols]
        s = nn(keys, jnp.concatenate([q, ones], axis=0))
        p = jnp.exp2(s * scale2 - lse_ref[0, :, cols])
        t = p * nn(values, g)
        inner = jnp.sum(t, axis=0, keepdims=True)
        ds = (t - p * inner).astype(bf16)
        out_ref[0, :, cols] = (nn(key_rows, ds) * scale).astype(bf16)
        dk = nt(q, ds)
        dv = nt(g, p.astype(bf16))
        if at == 0:
            gk[...] = dk
            gv[...] = dv
        else:
            gk[...] += dk
            gv[...] += dv
    out_ref[1] = (gk[...] * scale).astype(bf16)
    out_ref[2] = gv[...].astype(bf16)


def attend_back(qkv, mask, grads, lse, clips, heads, half, halves, groups):
    frames = qkv.shape[1] // clips
    span = frames // groups
    vec = pl.BlockSpec((1, 1, frames), lambda b, h: (b * heads + h, 0, 0))

    def block(v, place):
        if v.ndim == 3:
            return pl.BlockSpec((1, HEAD_DIM, span), lambda b, h: (place, h, 0))
        return pl.BlockSpec((HEAD_DIM, span), lambda b, h: (place + h, 0))

    grads = grads[0] + grads[1]
    return pl.pallas_call(
        lambda *refs: attend_back_kernel(span, 1.0 / math.sqrt(HEAD_DIM), *refs),
        grid=(clips, heads),
        in_specs=head_rows(frames, heads, half)
        + [pl.BlockSpec((16, frames), lambda b, h: (b, 0)), vec]
        + [block(*g) for g in grads],
        out_specs=pl.BlockSpec((3, HEAD_DIM, frames), lambda b, h: (0, h, b)),
        out_shape=sds((3, heads * HEAD_DIM, clips * frames), bf16),
        scratch_shapes=[
            pltpu.VMEM((HEAD_DIM, frames), f32),
            pltpu.VMEM((HEAD_DIM, frames), f32),
            pltpu.VMEM((HEAD_DIM, frames), bf16),
        ],
        compiler_params=params(),
        cost_estimate=cost(
            flops=clips * heads * frames * frames * 4000,
            bytes_accessed=qkv.size * 6 // halves,
            transcendentals=clips * heads * frames * frames,
        ),
        name="attend_back",
    )(qkv, qkv, qkv, mask, lse, *[v for v, _ in grads])


def gelu_parts(v):
    bell = jnp.exp2(v * v * (-0.5 * LOG2E))
    t = 1.0 / (1.0 + (0.3275911 / math.sqrt(2.0)) * jnp.abs(v))
    poly = t * (
        0.5 * 0.254829592
        + t * (0.5 * -0.284496736 + t * (0.5 * 1.421413741 + t * (0.5 * -1.453152027 + t * (0.5 * 1.061405429))))
    )
    tail = poly * bell
    return jnp.where(v < 0.0, tail, 1.0 - tail), bell * (1.0 / math.sqrt(2.0 * math.pi))


def feed_kernel(count, own, tile, refs):
    ns, gs = refs[:count], refs[count : 2 * count]
    up_ref, down_ref, bias_ref = refs[2 * count : 2 * count + 3]
    act_ref, back_ref, grad_own, grad_other, out_own, out_other, sum_ref, n_now, g_now = refs[2 * count + 3 :]
    width = n_now.shape[1]
    hidden = act_ref.shape[1]
    rows = ns[0].shape[0]
    for j in range(count):
        n_now[j * rows : (j + 1) * rows, :] = ns[j][...]
        g_now[j * rows : (j + 1) * rows, :] = gs[j][...]
    up = up_ref[...].reshape(width, hidden)
    down = down_ref[...].reshape(hidden, width)
    for low in range(0, hidden, tile):
        cols = slice(low, low + tile)
        before = nn(n_now[...], up[:, cols]) + bias_ref[:, cols]
        grad_act = nt(g_now[...], down[cols, :])
        cumulative, density = gelu_parts(before)
        act_ref[:, cols] = (before * cumulative).astype(bf16)
        grad = ((cumulative + before * density) * grad_act).astype(bf16)
        back_ref[:, cols] = grad
        sum_ref[:, cols] = jnp.sum(grad.astype(f32), axis=0, keepdims=True)
    mine = own * rows
    grad_own[...] = nt(back_ref[:mine, :], up)
    grad_other[...] = nt(back_ref[mine:, :], up).astype(bf16)
    out_own[...] = nn(act_ref[:mine, :], down)
    out_other[...] = nn(act_ref[mine:, :], down).astype(bf16)


def feed(normed, grad, own, rows, weights, bias):
    count = len(normed)
    width = normed[0][0].shape[1]
    hidden = bias.shape[1]
    tile = 256 if hidden % 256 == 0 else hidden

    def whole(shape):
        return pl.BlockSpec(shape, lambda i: (0,) * len(shape))

    if len(weights) == 1:
        pairs = weights[0].shape[0]
        weights = weights * 2
        weight_specs = [pl.BlockSpec((pairs, hidden // pairs, width), lambda i, j=j: (0, j, 0)) for j in range(2)]
    else:
        weight_specs = [whole(w.shape) for w in weights]
    shapes = [
        sds((count * rows, hidden), bf16),
        sds((count * rows, hidden), bf16),
        sds((own * rows, width), f32),
        sds(((count - own) * rows, width), bf16),
        sds((own * rows, width), f32),
        sds(((count - own) * rows, width), bf16),
        sds((1, hidden), f32),
    ]
    return pl.pallas_call(
        lambda *refs: feed_kernel(count, own, tile, refs),
        grid=(1,),
        in_specs=[pl.BlockSpec((rows, width), lambda i, at=at: (at, 0)) for _, at in normed + grad]
        + weight_specs
        + [whole((1, hidden))],
        out_specs=[whole(v.shape) for v in shapes],
        out_shape=shapes,
        scratch_shapes=[pltpu.VMEM((count * rows, width), bf16)] * 2,
        compiler_params=params(),
        cost_estimate=cost(
            flops=8 * count * rows * width * hidden,
            bytes_accessed=4 * width * hidden + 16 * count * rows * width,
            transcendentals=count * rows * hidden,
        ),
        name="feed",
    )(*[v for v, _ in normed + grad], *weights, bias)


def project(rank, blocks, small, weight, halves):
    count = len(blocks)
    rows, width = blocks[0].shape
    shards, lines_count, features = small.shape
    own_rows = width // shards
    slab = features // 3
    cut = slab // halves
    sub = math.gcd(rows, 256)

    def kernel(rank_ref, small_ref, w_ref, *refs):
        xs = refs[:count]
        normed_ref, qkv_ref, lines_ref, turned, bias, now = refs[count:]
        at = pl.program_id(0)

        @pl.when(at == 0)
        def _():
            lines_ref[...] = jnp.concatenate(
                [small_ref[f, :, :own_rows].astype(f32) for f in range(shards)], axis=1
            )
            turned[...] = w_ref[...].T
            for r in range(count):

                @pl.when(rank_ref[0] == r)
                def _(r=r):
                    parts = []
                    for h in range(halves):
                        cols = slice(r * slab + h * cut, r * slab + (h + 1) * cut)
                        parts += [lines_ref[2:3, cols], jnp.zeros((1, cut), f32), lines_ref[3:4, cols]]
                    row = jnp.concatenate(parts, axis=1)
                    bias[...] = jnp.broadcast_to(row, (8, features)).T

        for j in range(count):

            @pl.when(at == j)
            def _(j=j):
                now[...] = xs[j][...]

        for t in range(0, rows, sub):
            plain, _ = normalized(now[t : t + sub, :].astype(f32))
            normed = (plain * lines_ref[0:1, :] + lines_ref[1:2, :]).astype(bf16)
            normed_ref[t : t + sub, :] = normed
            qkv_ref[:, t : t + sub] = (nt(turned[...], normed) + bias[:, 0:1]).astype(bf16)

    return pl.pallas_call(
        kernel,
        grid=(count,),
        in_specs=[
            smem(),
            pl.BlockSpec(small.shape, lambda i: (0, 0, 0)),
            pl.BlockSpec(weight.shape, lambda i: (0, 0)),
        ]
        + [pl.BlockSpec((rows, width), lambda i: (0, 0))] * count,
        out_specs=[
            pl.BlockSpec((rows, width), lambda i: (i, 0)),
            pl.BlockSpec((features, rows), lambda i: (0, i)),
            pl.BlockSpec((lines_count, width), lambda i: (0, 0)),
        ],
        out_shape=[
            sds((count * rows, width), bf16),
            sds((features, count * rows), bf16),
            sds((lines_count, width), f32),
        ],
        scratch_shapes=[
            pltpu.VMEM((features, width), bf16),
            pltpu.VMEM((features, 8), f32),
            pltpu.VMEM((rows, width), bf16),
        ],
        compiler_params=params(),
        cost_estimate=pl.CostEstimate(
            flops=2 * count * rows * width * features,
            bytes_accessed=2 * width * features + 6 * count * rows * width,
            transcendentals=count * rows,
        ),
        name="project",
    )(rank, small, weight, *blocks)


def project_back(grads, weight, blocks, places, groups):
    count, halves = len(blocks), len(grads)
    rows, width = blocks[0].shape
    features = weight.shape[1]
    own = count // 2
    sub = math.gcd(rows, 256)

    def kernel(w_ref, *refs):
        g_refs, xs = refs[:halves], refs[halves : halves + count]
        own_ref, other_ref, sums_ref, bias_ref, now = refs[halves + count :]
        at = pl.program_id(0)
        for j in range(count):

            @pl.when(at == j)
            def _(j=j):
                now[...] = xs[j][...]

        @pl.when(at == 0)
        def _():
            sums_ref[...] = jnp.zeros(sums_ref.shape, f32)
            bias_ref[...] = jnp.zeros(bias_ref.shape, f32)

        for t in range(0, rows, sub):
            cut = slice(t, t + sub)
            turned = jnp.concatenate([g[:, cut] for g in g_refs], axis=0).T
            grad = nt(turned, w_ref[...])
            plain, _ = normalized(now[cut, :].astype(f32))
            sums_ref[0:1, :] += jnp.sum(grad * plain, axis=0, keepdims=True)
            sums_ref[1:2, :] += jnp.sum(grad, axis=0, keepdims=True)
            bias_ref[...] += nn(jnp.ones((8, sub), bf16), turned)

            @pl.when(at < own)
            def _(cut=cut, grad=grad):
                own_ref[cut, :] = grad

            @pl.when(at >= own)
            def _(cut=cut, grad=grad):
                other_ref[cut, :] = grad.astype(bf16)

    return pl.pallas_call(
        kernel,
        grid=(count,),
        in_specs=[pl.BlockSpec(weight.shape, lambda i: (0, 0))]
        + [
            pl.BlockSpec((g.shape[0], rows), lambda i: (0, i // own * groups + i % own + places[0])) for g in grads
        ]
        + [pl.BlockSpec((rows, width), lambda i: (0, 0))] * count,
        out_specs=[
            pl.BlockSpec((rows, width), lambda i: (jnp.minimum(i, own - 1), 0)),
            pl.BlockSpec((rows, width), lambda i: (jnp.maximum(i - own, 0), 0)),
            pl.BlockSpec((8, width), lambda i: (0, 0)),
            pl.BlockSpec((8, features), lambda i: (0, 0)),
        ],
        out_shape=[
            sds((own * rows, width), f32),
            sds((own * rows, width), bf16),
            sds((8, width), f32),
            sds((8, features), f32),
        ],
        scratch_shapes=[pltpu.VMEM((rows, width), bf16)],
        compiler_params=params(),
        cost_estimate=cost(
            flops=2 * count * rows * width * features,
            bytes_accessed=2 * width * features + 8 * count * rows * width,
            transcendentals=count * rows,
        ),
        name="project_back",
    )(weight, *grads, *blocks)


def by_source(r, groups):
    return [((src % groups - r % groups) % groups, (src // groups) ^ (r // groups)) for src in range(2 * groups)]


def finish_heads(rank, blocks, halves, groups):
    _, rows, features = blocks[0].shape
    ranks = 2 * groups
    slab = features // 4
    cut = slab // halves
    width = slab * ranks
    starts = [0] + [slab + 3 * cut * h for h in range(1, halves)]

    def kernel(rank_ref, *refs):
        ins, outs = refs[:-4], refs[-4:]
        for r in range(ranks):

            @pl.when(rank_ref[0] == r)
            def _(r=r):
                order = by_source(r, groups)
                for i in range(3):
                    outs[i][...] = jnp.concatenate(
                        [
                            ins[step][flip, :, low + i * cut : low + (i + 1) * cut]
                            for step, flip in order
                            for low in starts
                        ],
                        axis=1,
                    ).astype(f32)
                outs[3][...] = jnp.concatenate(
                    [ins[step][flip, :, 3 * cut : 3 * cut + slab] for step, flip in order], axis=1
                ).astype(f32)

    return pl.pallas_call(
        kernel,
        in_specs=[smem()] + vmem(groups),
        out_specs=vmem(4),
        out_shape=[sds((rows, width), f32)] * 4,
        compiler_params=params(),
        cost_estimate=pl.CostEstimate(flops=0, bytes_accessed=24 * rows * width, transcendentals=0),
        name="finish_heads",
    )(rank, *blocks)


def finish_feed(rank, ups, downs, pairs, groups):
    _, rows, rank_hidden = ups[0].shape
    piece, width = downs[0].shape
    ranks = 2 * groups

    def kernel(rank_ref, *refs):
        up_refs, down_refs, up_out, down_out = refs[:groups], refs[groups : 2 * groups], refs[-2], refs[-1]
        for r in range(ranks):

            @pl.when(rank_ref[0] == r)
            def _(r=r):
                for zx in range(pairs):
                    up_out[:, zx * ranks * piece : (zx + 1) * ranks * piece] = jnp.concatenate(
                        [
                            up_refs[step][flip, :, zx * piece : (zx + 1) * piece]
                            for step, flip in by_source(r, groups)
                        ],
                        axis=1,
                    ).astype(f32)
                for step in range(groups):
                    at = (r + step) % groups * piece
                    down_out[at : at + piece, :] = down_refs[step][...].astype(f32)

    return pl.pallas_call(
        kernel,
        in_specs=[smem()] + vmem(2 * groups),
        out_specs=vmem(2),
        out_shape=[sds((rows, rank_hidden * ranks), f32), sds((groups * piece, width), f32)],
        compiler_params=params(),
        cost_estimate=pl.CostEstimate(flops=0, bytes_accessed=12 * rows * rank_hidden * ranks, transcendentals=0),
        name="finish_feed",
    )(rank, *ups, *downs)


def pick(where, q, k, v, up, o, small, ranks, halves, pairs):
    own_rows, width = q.shape
    slab = width // ranks
    cut = slab // halves
    piece = up.shape[1] // (ranks * pairs)
    base = -(-own_rows // 16) * 16
    extra = small.shape[0]

    def kernel(where_ref, q_ref, k_ref, v_ref, up_ref, o_ref, small_ref, *outs):
        for side in range(2):
            pay, ups, half = outs[3 * side : 3 * side + 3]
            pay[base:, :] = jnp.zeros((extra, 3 * slab), bf16)
            pay[base:, : small.shape[1]] = small_ref[...]
            for r in range(ranks):

                @pl.when(where_ref[side] == r)
                def _(pay=pay, ups=ups, r=r):
                    parts = [
                        w[:, r * slab + h * cut : r * slab + (h + 1) * cut]
                        for h in range(halves)
                        for w in (q_ref, k_ref, v_ref)
                    ]
                    pay[:own_rows, :] = jnp.concatenate(parts, axis=1)
                    ups[...] = jnp.concatenate(
                        [up_ref[:, (c * ranks + r) * piece : (c * ranks + r + 1) * piece] for c in range(pairs)],
                        axis=1,
                    )

            for c in range(2):

                @pl.when(where_ref[2] == (c ^ side))
                def _(half=half, c=c):
                    half[...] = o_ref[:, c * width // 2 : (c + 1) * width // 2]

    shapes = [
        sds((base + extra, 3 * slab), bf16),
        sds((own_rows, piece * pairs), bf16),
        sds((own_rows, width // 2), bf16),
    ]
    return pl.pallas_call(
        kernel,
        in_specs=[smem()] + vmem(6),
        out_specs=vmem(6),
        out_shape=shapes * 2,
        compiler_params=params(),
        cost_estimate=pl.CostEstimate(flops=0, bytes_accessed=10 * up.size, transcendentals=0),
        name="pick",
    )(where, q, k, v, up, o, small)


def place(blocks, slots, pieces):
    count, (_, width) = len(blocks), blocks[0].shape

    def kernel(slots_ref, *refs):
        for i in range(count):
            for target, spans in zip(refs[count:], pieces, strict=True):
                for j, (low, high) in enumerate(spans):
                    target[slots_ref[i] * len(spans) + j] = refs[i][low:high, :]

    return pl.pallas_call(
        kernel,
        in_specs=[smem()] + vmem(count),
        out_specs=vmem(len(pieces)),
        out_shape=[
            sds((count * len(spans), spans[0][1] - spans[0][0], width), blocks[0].dtype) for spans in pieces
        ],
        compiler_params=params(),
        cost_estimate=pl.CostEstimate(
            flops=0, bytes_accessed=4 * count * blocks[0].size, transcendentals=0
        ),
        name="place",
    )(slots, *blocks)


def merge(slots, x, out_full, lines, blocks, halves, token_parts):
    tokens, width = x.shape
    count = len(blocks)
    hs = blocks[0][0].shape[0]
    slab = hs * halves
    rows = tokens // token_parts

    def kernel(slots_ref, x_ref, w_ref, lines_ref, *refs):
        ins, mixed, after = refs[: count * halves], refs[count * halves], refs[count * halves + 1]
        outs = refs[count * halves + 2 :]
        for i in range(count):
            for h in range(halves):
                at = pl.multiple_of(slots_ref[i] * slab + h * hs, 16)
                mixed[pl.ds(at, hs), :] = ins[i * halves + h][...]
        for t in range(token_parts):
            cols = slice(t * rows, (t + 1) * rows)
            total = nn(mixed[:, cols].T, w_ref[...]) + lines_ref[4:5, :] + x_ref[cols, :].astype(f32)
            after[cols, :] = total
            plain, _ = normalized(total)
            outs[t][...] = (plain * lines_ref[5:6, :] + lines_ref[6:7, :]).astype(bf16)

    made = pl.pallas_call(
        kernel,
        in_specs=[smem()] + vmem(3 + count * halves),
        out_specs=vmem(2 + token_parts),
        out_shape=[sds((width, tokens), bf16), sds((tokens, width), f32)]
        + [sds((rows, width), bf16)] * token_parts,
        compiler_params=params(),
        cost_estimate=pl.CostEstimate(
            flops=2 * tokens * width * width, bytes_accessed=2 * width * width + 12 * tokens * width, transcendentals=tokens
        ),
        name="merge",
    )(slots, x, out_full, lines, *[b for source in blocks for b in source])
    return made[0], made[1], list(made[2:])


def turn(slots, after1, near, fars, live_grad, lines, out_full, halves, groups):
    tokens, width = after1.shape
    ranks = 2 * groups
    slab = width // ranks
    hs = slab // halves
    parts = len(fars)
    rows = tokens // parts
    per = len(fars[0])

    def kernel(slots_ref, after_ref, near_ref, live_ref, g_ref, w_ref, *refs):
        far_refs = refs[: parts * per]
        grad_ref, low_ref, sums_ref = refs[parts * per : parts * per + 3]
        outs = refs[parts * per + 3 :]
        sums = [jnp.zeros((1, width), f32) for _ in range(4)]
        for t in range(parts):
            cut = slice(t * rows, (t + 1) * rows)
            grad = near_ref[cut, :]
            for j in range(per):
                grad = grad + far_refs[t * per + j][...].astype(f32)
            plain, scale = normalized(after_ref[cut, :])
            live = live_ref[cut, :].astype(f32)
            total = live + norm_back(plain, scale, grad * g_ref[5:6, :])
            grad_ref[cut, :] = total
            low = total.astype(bf16)
            low_ref[cut, :] = low
            for i, term in enumerate((grad * plain, grad, low.astype(f32), live)):
                sums[i] = sums[i] + jnp.sum(term, axis=0, keepdims=True)
        for i in range(4):
            sums_ref[i : i + 1, :] = sums[i]
        low = low_ref[...]

        def of_rank(flip, step, h):
            at = pl.multiple_of(slots_ref[flip * groups + step] * slab + h * hs, 16)
            return nt(w_ref[pl.ds(at, hs), :], low).astype(bf16)

        for h in range(halves):
            for step in range(1, groups):
                for flip in range(2):
                    outs[h * (groups - 1) + step - 1][flip] = of_rank(flip, step, h)
        near_outs = outs[halves * (groups - 1) :]
        for h in range(halves):
            near_outs[0][h * hs : (h + 1) * hs, :] = of_rank(0, 0, h)
            near_outs[1][h * hs : (h + 1) * hs, :] = of_rank(1, 0, h)

    fars_count = halves * (groups - 1)
    made = pl.pallas_call(
        kernel,
        in_specs=[smem()] + vmem(5 + parts * per),
        out_specs=vmem(3 + fars_count + 2),
        out_shape=[sds((tokens, width), f32), sds((tokens, width), bf16), sds((4, width), f32)]
        + [sds((2, hs, tokens), bf16)] * fars_count
        + [sds((slab, tokens), bf16)] * 2,
        compiler_params=params(),
        cost_estimate=cost(
            flops=2 * tokens * width * width, bytes_accessed=2 * width * width + 16 * tokens * width, transcendentals=tokens
        ),
        name="turn",
    )(slots, after1, near, live_grad, lines, out_full, *[v for part in fars for v in part])
    sent = [[made[3 + h * (groups - 1) + step] for step in range(groups - 1)] for h in range(halves)]
    return made[0], made[1], made[2], sent, made[-2], made[-1]


def part_ways(x_ref, value, kept, sent):
    depth, rows = kept.shape[:2]
    for flip in range(2):

        @pl.when(x_ref[0] == flip)
        def _(flip=flip):
            for z in range(depth):
                low, other = (2 * z + flip) * rows, (2 * z + 1 - flip) * rows
                kept[z] = value[low : low + rows, :]
                sent[z] = value[other : other + rows, :]


def weight_grad(x_at, lefts, rights, depth):
    rows = lefts[0][0].shape[1]
    cols = rights[0][0].shape[1]
    tile = 256 if cols % 256 == 0 else cols
    count, right_count = len(lefts), len(rights)

    def ends_of(parts):
        return [sum(size for _, _, size in parts[:i]) for i in range(len(parts) + 1)]

    left_ends, right_ends = ends_of(lefts), ends_of(rights)
    tokens = left_ends[-1]
    share = rows // (2 * depth)

    def kernel(x_ref, *refs):
        left_refs, right_refs = refs[:count], refs[count : count + right_count]
        kept, sent, turned, joined = refs[-4:]

        @pl.when(pl.program_id(0) == 0)
        def _():
            for i in range(count):
                turned[:, left_ends[i] : left_ends[i + 1]] = left_refs[i][...].T

        for i in range(right_count):
            joined[right_ends[i] : right_ends[i + 1], :] = right_refs[i][...]
        part_ways(x_ref, nn(turned[...], joined[...]).astype(bf16), kept, sent)

    whole = [pl.BlockSpec((size, rows), lambda i, at=at: (at, 0)) for _, at, size in lefts]
    strips = [pl.BlockSpec((size, tile), lambda i, at=at: (at, i)) for _, at, size in rights]
    return pl.pallas_call(
        kernel,
        grid=(cols // tile,),
        in_specs=[smem()] + whole + strips,
        out_specs=[pl.BlockSpec((depth, share, tile), lambda i: (0, 0, i))] * 2,
        out_shape=[sds((depth, share, cols), bf16)] * 2,
        scratch_shapes=[pltpu.VMEM((rows, tokens), bf16), pltpu.VMEM((tokens, tile), bf16)],
        compiler_params=params(),
        cost_estimate=cost(
            flops=2 * tokens * rows * cols, bytes_accessed=2 * (tokens * (rows + cols) + rows * cols), transcendentals=0
        ),
        name="weight_grad",
    )(x_at, *[v for v, _, _ in lefts + rights])


def head_grad(x_at, normed, grad_heads, depth, extra=()):
    tokens, width = normed.shape
    features = grad_heads.shape[0]
    tile = 512 if tokens % 512 == 0 else tokens
    share = width // (2 * depth)
    cols = features + (extra[0].shape[1] if extra else 0)

    def kernel(x_ref, n_ref, g_ref, *refs):
        kept, sent, total = refs[-3:]
        part = nn(g_ref[...], n_ref[...])

        @pl.when(pl.program_id(0) == 0)
        def _():
            total[...] = part

        @pl.when(pl.program_id(0) > 0)
        def _():
            total[...] += part

        @pl.when(pl.program_id(0) == pl.num_programs(0) - 1)
        def _():
            value = total[...].astype(bf16).T
            if extra:
                more = refs[0][...].astype(f32)
                for v in refs[1:-3]:
                    more = more + v[...].astype(f32)
                value = jnp.concatenate([value, more.astype(bf16)], axis=1)
            part_ways(x_ref, value, kept, sent)

    return pl.pallas_call(
        kernel,
        grid=(tokens // tile,),
        in_specs=[
            smem(),
            pl.BlockSpec((tile, width), lambda i: (i, 0)),
            pl.BlockSpec((features, tile), lambda i: (0, i)),
        ]
        + [pl.BlockSpec(v.shape, lambda i: (0, 0)) for v in extra],
        out_specs=[pl.BlockSpec((depth, share, cols), lambda i: (0, 0, 0))] * 2,
        out_shape=[sds((depth, share, cols), bf16)] * 2,
        scratch_shapes=[pltpu.VMEM((features, width), f32)],
        compiler_params=params(),
        cost_estimate=cost(
            flops=2 * tokens * width * features, bytes_accessed=2 * tokens * (width + features), transcendentals=0
        ),
        name="head_grad",
    )(x_at, normed, grad_heads, *extra)


def out_grad_halves(core_at, mixed, grad):
    rows, tokens = mixed.shape
    width = grad.shape[1]
    half = width // 2

    def kernel(core_ref, m_ref, g_ref, kept, sent):
        value = nn(m_ref[...], g_ref[...]).astype(bf16)
        for core in range(2):

            @pl.when(core_ref[0] == core)
            def _(core=core):
                kept[...] = value[:, core * half : (core + 1) * half]
                sent[...] = value[:, (1 - core) * half : (2 - core) * half]

    return pl.pallas_call(
        kernel,
        in_specs=[smem()] + vmem(2),
        out_specs=vmem(2),
        out_shape=[sds((rows, half), bf16)] * 2,
        compiler_params=params(),
        cost_estimate=cost(
            flops=2 * rows * tokens * width, bytes_accessed=4 * rows * width, transcendentals=0
        ),
        name="out_grad_halves",
    )(core_at, mixed, grad)


def out_grad_parts(seq_at, kept, came, groups):
    rows, half = kept.shape
    slab = half // groups

    def kernel(seq_ref, a_ref, b_ref, *outs):
        value = (a_ref[...].astype(f32) + b_ref[...].astype(f32)).astype(bf16)
        for at in range(groups):

            @pl.when(seq_ref[0] == at)
            def _(at=at):
                for step in range(groups):
                    low = (at + step) % groups * slab
                    outs[step][...] = value[:, low : low + slab]

    return pl.pallas_call(
        kernel,
        in_specs=[smem()] + vmem(2),
        out_specs=vmem(groups),
        out_shape=[sds((rows, slab), bf16)] * groups,
        compiler_params=params(),
        cost_estimate=cost(flops=0, bytes_accessed=6 * rows * half, transcendentals=0),
        name="out_grad_parts",
    )(seq_at, kept, came)


def local(
    frames_in,
    clip_lengths,
    norm1_gain,
    norm1_bias,
    q_weight,
    q_bias,
    k_weight,
    v_weight,
    v_bias,
    o_weight,
    o_bias,
    norm2_gain,
    norm2_bias,
    up_weight,
    up_bias,
    down_weight,
    down_bias,
    out_grad,
):
    clip_count, local_frames, width = frames_in.shape
    hidden = up_weight.shape[1]
    groups = lax.axis_size("seq")
    shards = lax.axis_size("fsdp")
    pairs = shards // 2
    depth = pairs // 2
    ranks = groups * 2
    frames = local_frames * groups
    assert clip_count == 1
    tokens = clip_count * local_frames
    head_count = width // HEAD_DIM
    heads = head_count // ranks
    halves = 2 if heads % 2 == 0 else 1
    slab = heads * HEAD_DIM
    cut = slab // halves
    own_rows = width // shards
    own_hidden = hidden // shards
    piece = own_hidden * 2 // ranks
    rank_hidden = piece * pairs
    clips = 2 * clip_count
    token_parts = 2
    part_rows = tokens // token_parts
    fsdp = lax.axis_index("fsdp")
    seq = lax.axis_index("seq")
    core, pair = fsdp % 2, fsdp // 2
    xpos, zpos = pair % 2, pair // 2
    rank = core * groups + seq
    peer = (1 - core) * groups + seq

    core_way = [(i, i ^ 1) for i in range(shards)]
    x_way = [(i, i ^ 2) for i in range(shards)]

    def over_core(v):
        return lax.ppermute(v, "fsdp", core_way)

    def over_x(v):
        return lax.ppermute(v, "fsdp", x_way)

    def over_z(v, step):
        return lax.ppermute(v, "fsdp", [(i, (i + 4 * step) % shards) for i in range(shards)])

    def from_seq(v, step):
        return lax.ppermute(v, "seq", [(i, (i - step) % groups) for i in range(groups)])

    def to_seq(v, step):
        return from_seq(v, -step % groups)

    steps = range(1, groups)

    def by_core(mine, other):
        return jnp.where(
            core == 0, jnp.concatenate([mine, other]), jnp.concatenate([other, mine])
        )

    slots = []
    for step in range(depth):
        for flip in range(2):
            slots.append(((zpos - step) % depth) * 2 + (xpos ^ flip))
    slots = jnp.stack(slots).astype(jnp.int32)

    def spread_z(payload):
        return [payload] + [over_z(payload, step) for step in range(1, depth)]

    def spread_x(blocks):
        return [v for block in blocks for v in (block, over_x(block))]

    small = [norm1_gain, norm1_bias, q_bias, v_bias, o_bias, norm2_gain, norm2_bias, down_bias]
    small = jnp.concatenate([jnp.stack(small), up_bias.reshape(hidden // width, own_rows)])
    small_rows = -(-small.shape[0] // 16) * 16
    small = jnp.pad(small, ((0, small_rows - small.shape[0]), (0, 0)))
    where = jnp.stack([rank, peer, core]).astype(jnp.int32)
    pay, up_mine, out_mine, pay_other, up_other, out_other = pick(
        where, q_weight, k_weight, v_weight, up_weight, o_weight, small, ranks, halves, pairs
    )
    base = -(-own_rows // 16) * 16
    pay_rows = base + small_rows
    frames_own = frames_in.reshape(tokens, width)
    pay_full = by_core(pay, over_core(pay_other))
    pay_z = spread_z(pay_full)
    frames_side = [from_seq(tie(frames_own, pay_full), step) for step in steps]

    up_own = by_core(up_mine, over_core(up_other))
    down_own = lax.dynamic_slice_in_dim(down_weight, seq * piece, piece, 0)
    out_own = by_core(out_mine, over_core(out_other))
    same_core = [[i for i in range(shards) if i % 2 == c] for c in range(2)]

    def over_chips(v):
        return lax.all_gather(v, "fsdp", axis=0, axis_index_groups=same_core)

    out_half = over_chips(out_own).reshape(width, width // 2)
    feed_own = jnp.concatenate([up_own.reshape(-1, width), down_own])
    gathered = over_chips(tie(feed_own, *pay_z[1:]))
    up_rows = up_own.size // width
    if rank_hidden == width:
        feed_weights = [gathered]
    else:
        feed_weights = [
            gathered[:, :up_rows].reshape(width, rank_hidden),
            gathered[:, up_rows:].reshape(rank_hidden, width),
        ]

    pay_z[depth // 2] = tie(pay_z[depth // 2], *frames_side)
    pay_all = spread_x(pay_z)
    frames_near = over_core(tie(frames_own, *pay_all))
    lengths_sent = jnp.broadcast_to(clip_lengths.astype(f32)[:, None], (clip_count, 128))
    lengths_near = over_core(tie(lengths_sent, *pay_z[1:]))
    frames_cross = [over_core(tie(v, *pay_all)) for v in frames_side]

    positions = jnp.concatenate(
        [
            ((seq + step) % groups) * local_frames + jnp.arange(local_frames, dtype=jnp.int32)
            for step in range(groups)
        ]
    )
    lengths = jnp.concatenate([clip_lengths, lengths_near[:, 0].astype(jnp.int32)])
    live = positions[None, :] < lengths[:, None]
    live_own = live[:clip_count, :local_frames].reshape(tokens, 1)
    mask = jnp.where(live, 0.0, NEGATIVE).astype(bf16)
    mask = jnp.pad(mask[:, None, :], ((0, 0), (0, 15), (0, 0))).reshape(clips * 16, frames)
    live_grad = jnp.where(live_own, out_grad.reshape(tokens, width), 0.0).astype(bf16)

    grad_side = [from_seq(tie(live_grad, *frames_side), step) for step in steps]

    qkv_part, small_part = place(
        pay_all,
        slots,
        [
            [(0, own_rows), (pay_rows, pay_rows + own_rows)],
            [(base, pay_rows), (pay_rows + base, 2 * pay_rows)],
        ],
    )
    qkv_full = qkv_part.reshape(width, 3 * slab)
    ubias = small_part[:, 8 : 8 + hidden // width, :own_rows].astype(f32).reshape(pairs, ranks, piece)
    ubias = lax.dynamic_index_in_dim(ubias, rank, 1, keepdims=False).reshape(1, rank_hidden)


    def to_z(both):
        blocks = [
            lax.dynamic_index_in_dim(both, (zpos + step) % depth, 0, keepdims=False) for step in range(depth)
        ]
        return blocks[0], [v.astype(bf16) for v in blocks[1:]]

    def reduce_z(kept, sent, parted=True):
        both = kept.astype(f32) + over_x(sent).astype(f32)
        return to_z(both) if parted else both

    def reduce_end(own, sent):
        total = own
        for step in range(1, depth):
            total = total + over_z(sent[step - 1], step).astype(f32)
        return total.astype(bf16)

    def along_seq(v):
        return [v] + [from_seq(v, step) for step in steps]

    def own_of_ranks(v):
        blocks = v.reshape(2, own_rows, -1)
        keep = lax.dynamic_index_in_dim(blocks, core, 0, keepdims=False)
        other = over_core(lax.dynamic_index_in_dim(blocks, 1 - core, 0, keepdims=False))
        return jnp.stack([keep, other])

    rank_at = rank.reshape(1).astype(jnp.int32)
    seq_at = seq.reshape(1).astype(jnp.int32)
    frames_all = [frames_own] + frames_side + [frames_near] + frames_cross
    normed1, qkv, lines = project(rank_at, frames_all, small_part, qkv_full, halves)
    grad_cross_near = over_core(tie(live_grad, lines))
    grad_cross = [over_core(tie(v, lines)) for v in grad_side]
    grad_near = [(v, t) for v in (live_grad, grad_cross_near) for t in range(token_parts)]
    grad_far = [[(v, t) for v in grad_side + grad_cross] for t in range(token_parts)]

    out_half = out_half.reshape(width, width // 2)
    out_rest = over_core(out_half)
    out_full = jnp.where(
        core == 0,
        jnp.concatenate([out_half, out_rest], axis=1),
        jnp.concatenate([out_rest, out_half], axis=1),
    )
    half_heads = heads // halves
    logs, tops, sources = [], [], []
    mixed_blocks = [[] for _ in range(ranks)]

    def flat(v):
        return jnp.swapaxes(v, 0, 1).reshape(v.shape[1], tokens)

    for half in range(halves):
        if half:
            qkv = tie(qkv, grad_cross_near, *grad_cross)
        near, far, log_half, top_half = attend(qkv, mask, clips, half_heads, half, halves, groups)
        logs.append(log_half)
        tops.append(top_half)
        came = [near] + [to_seq(far[step - 1], step) for step in steps]
        for step, v in enumerate(came):
            mixed_blocks[step].append(flat(v[:clip_count]))
            mixed_blocks[groups + step].append(flat(over_core(v[clip_count:])))
    sources = [
        (core ^ flip) * groups + (seq - step) % groups for flip in range(2) for step in range(groups)
    ]
    sources = jnp.stack(sources).astype(jnp.int32)
    mixed_own, after1, normed2_own = merge(
        sources, frames_own, out_full, lines, mixed_blocks, halves, token_parts
    )

    normed2_side = [[from_seq(v, step) for step in steps] for v in normed2_own]
    normed2_near = normed2_own + [over_core(v) for v in normed2_own]

    def parts_of(arrays):
        return [(v, 0) for v in arrays]

    act_near, back_near, grad2_own, grad2_other, fed_own, fed_other, sums = feed(
        parts_of(normed2_near), grad_near, token_parts, part_rows, feed_weights, ubias
    )
    normed2_side = [[tie(v, sums) for v in side] for side in normed2_side]
    normed2_far = [side + [over_core(v) for v in side] for side in normed2_side]
    normed2_far[0][0] = tie(normed2_far[0][0], *sum(normed2_side, []))
    act_far, back_far, grad2_sent, fed_parts = [], [], [], []

    def far_sums(own, other):
        both = (own + over_core(other).astype(f32)).astype(bf16)
        return [both[i * part_rows : (i + 1) * part_rows] for i in range(len(steps))]

    for t in range(token_parts):
        if t:
            normed2_far[t][0] = tie(normed2_far[t][0], *grad2_sent[t - 1])
        act, back, far_own, far_other, out_own_far, out_other_far, sums_far = feed(
            parts_of(normed2_far[t]), grad_far[t], len(steps), part_rows, feed_weights, ubias
        )
        act_far.append(act)
        back_far.append(back)
        grad2_sent.append(far_sums(far_own, far_other))
        fed_parts.append((out_own_far, out_other_far))
        sums = sums + sums_far

    grad2_far = [[to_seq(v, step) for v, step in zip(part, steps)] for part in grad2_sent]
    grad2_near = grad2_own + over_core(grad2_other).astype(f32)

    def with_sizes(parts):
        return [(v, at, part_rows) for v, at in parts]

    def wholes(arrays):
        return [(v, 0, v.shape[0]) for v in arrays]

    x_at = xpos.reshape(1).astype(jnp.int32)
    lefts = with_sizes(parts_of(normed2_near + sum(normed2_far, [])))
    lefts[0] = (tie(lefts[0][0], grad2_near, *grad2_sent[-1]),) + lefts[0][1:]

    rights = wholes([back_near] + back_far)
    up_kept, up_sent = weight_grad(x_at, lefts, rights, depth)

    targets = [
        (core ^ flip) * groups + (seq + step) % groups for flip in range(2) for step in range(groups)
    ]
    targets = jnp.stack(targets).astype(jnp.int32)
    grad_after1, grad_attn, sums2, grad_sent, heads_own, heads_other = turn(
        targets, after1, tie(grad2_near, up_sent), grad2_far, live_grad, lines, out_full, halves, groups
    )
    half_rows = heads // halves
    heads_cross = over_core(heads_other)
    head_grads, arrived, sides = [], [], []
    for half in range(halves):
        came = [to_seq(v, step) for v, step in zip(grad_sent[half], steps)]
        came = [came[groups - step - 1] for step in steps]
        cross = [over_core(v) for v in came]
        sides.append(came)
        arrived += cross
        head_grads.append(
            [
                [(heads_own, half * half_rows)] + [(v, 0) for v in came],
                [(heads_cross, half * half_rows)] + [(v, 1) for v in cross],
            ]
        )

    acts = wholes([tie(act_near, grad_attn)] + act_far)
    down_kept, down_sent = weight_grad(x_at, acts, with_sizes(grad_near + sum(grad_far, [])), depth)
    out_kept, out_other_half = out_grad_halves(where[2:], mixed_own, tie(grad_attn, down_sent, *sum(sides, [])))
    out_parts = out_grad_parts(seq_at, out_kept, over_core(out_other_half), groups)
    out_sent = list(out_parts[1:])
    out_came = [to_seq(v, step) for v, step in zip(out_sent, steps)]

    def fed_sums(after):
        both = [(mine + over_core(tie(other, after)).astype(f32)).astype(bf16) for mine, other in fed_parts]
        sent = [jnp.concatenate([v[i * part_rows : (i + 1) * part_rows] for v in both]) for i in range(len(steps))]
        return sent, fed_own + over_core(tie(fed_other, after)).astype(f32)

    grad_qkv, x_parts = [], []
    for half in range(halves):
        if half:
            fed_sent, fed_near = fed_sums(x_parts[0][1])
            fed_far = [to_seq(v, step) for v, step in zip(fed_sent, steps)]
            up_shard = reduce_end(tie(up_z[0], x_parts[0][1]), up_z[1])
            down_z = reduce_z(tie(down_kept, x_parts[0][1]), down_sent)
            after = [x_parts[0][1], up_shard, fed_near] + down_z[1] + fed_sent
        else:
            up_z = reduce_z(tie(up_kept, down_sent), up_sent)
            after = up_z[1] + out_sent + arrived
        own = head_grads[half][0]
        own[0] = (tie(own[0][0], *after), own[0][1])
        grads = attend_back(qkv, mask, head_grads[half], logs[half], clips, half_heads, half, halves, groups)
        grads = grads.reshape(3 * cut, -1)
        grad_qkv.append(grads)
        x_parts.append(head_grad(x_at, normed1, grads, depth, () if half else [out_parts[0]] + out_came))
    if halves == 1:
        fed_sent, fed_near = fed_sums(x_parts[0][1])
        fed_far = [to_seq(v, step) for v, step in zip(fed_sent, steps)]
    fed = tie(fed_near, x_parts[-1][1])
    for v in fed_far:
        fed = fed + v.astype(f32)
    output = (after1 + (fed + lines[7:8])).astype(bf16).reshape(clip_count, local_frames, width)
    if halves == 1:
        up_shard = reduce_end(tie(up_z[0], x_parts[0][1]), up_z[1])
        down_z = reduce_z(tie(down_kept, x_parts[0][1]), down_sent)
    down_shard = reduce_end(tie(down_z[0], x_parts[-1][1]), down_z[1])
    ups = along_seq(tie(own_of_ranks(up_shard), x_parts[-1][1]))
    x_sums = [reduce_z(tie(kept, x_parts[-1][1]), sent, False) for kept, sent in x_parts[: halves - 1]]
    grad_qkv[-1] = tie(grad_qkv[-1], x_parts[-1][1], *x_sums, *fed_far)

    far_own, far_other, far_sums1, far_bias = project_back(grad_qkv, qkv_full, frames_side + frames_cross, steps, groups)
    far_cross = over_core(far_other).astype(f32)
    far1 = (far_own + far_cross).astype(bf16)
    far1 = [far1[i * tokens : (i + 1) * tokens] for i in range(len(steps))]
    kept, sent = x_parts[-1]
    x_sums.append(reduce_z(tie(kept, far_other), sent, False))
    heads_z = to_z(jnp.concatenate(x_sums, axis=2))
    near_own, near_other, near_sums1, near_bias = project_back(
        [tie(grad_qkv[0], down_shard, *far1, *heads_z[1], *ups[1:])] + grad_qkv[1:],
        qkv_full,
        [frames_own, frames_near],
        [0],
        groups,
    )
    sums1, bias_sums = far_sums1 + near_sums1, far_bias + near_bias
    near_cross = over_core(near_other)
    grad_normed1 = near_own + near_cross.astype(f32)
    far1_came = [to_seq(v, step) for v, step in zip(far1, steps)]
    downs = along_seq(tie(down_shard.reshape(piece, width), near_other, *far1_came))
    for v in far1_came:
        grad_normed1 = grad_normed1 + v.astype(f32)
    plain1, scale1 = normalized(frames_own.astype(f32))
    in_grad = (grad_after1 + norm_back(plain1, scale1, grad_normed1 * lines[0:1])).astype(bf16)

    heads_last = own_of_ranks(reduce_end(tie(heads_z[0], near_other), heads_z[1]))

    up_weight_grad, down_weight_grad = finish_feed(
        rank_at,
        ups,
        downs,
        pairs,
        groups,
    )
    bias_cols = bias_sums[0].reshape(halves, 3, cut)

    def at_rank(v):
        return lax.dynamic_update_slice_in_dim(jnp.zeros((width,), f32), v, rank * slab, 0)

    up_sums = lax.dynamic_update_index_in_dim(
        jnp.zeros((pairs, ranks, piece), f32), sums.reshape(pairs, piece), rank, 1
    ).reshape(hidden // width, width)
    tops = jnp.stack([jnp.max(v.reshape(clips, half_heads, frames), axis=(0, 2)) for v in tops])
    tops = tops.reshape(heads) / math.sqrt(HEAD_DIM)
    peak_row = lax.dynamic_update_slice_in_dim(
        jnp.full((width,), NEGATIVE, f32), tops, rank * heads, 0
    )
    added = 8 + hidden // width
    stack = jnp.concatenate(
        [
            sums1[:2],
            at_rank(bias_cols[:, 0].reshape(slab))[None],
            at_rank(bias_cols[:, 2].reshape(slab))[None],
            sums2[2:3],
            sums2[:2],
            sums2[3:4],
            up_sums,
            peak_row[None],
        ]
    )
    is_sum = (jnp.arange(added + 1) < added)[:, None]

    def combine(a, b):
        return jnp.where(is_sum, a + b, jnp.maximum(a, b))

    stack = tie(stack, near_cross)
    stack = combine(stack, over_core(stack))
    stack = combine(tie(stack, heads_last), over_x(stack))
    step = 4
    while step < shards:
        stack = combine(stack, lax.ppermute(stack, "fsdp", [(i, i ^ step) for i in range(shards)]))
        step *= 2
    stack = tie(stack, grad_normed1)
    step = 1
    while step < groups:
        stack = combine(stack, lax.ppermute(stack, "seq", [(i, i ^ step) for i in range(groups)]))
        step *= 2
    small_own = lax.dynamic_slice_in_dim(stack[:8], fsdp * own_rows, own_rows, 1)
    up_bias_grad = lax.dynamic_slice_in_dim(stack[8:added].reshape(hidden), fsdp * own_hidden, own_hidden, 0)
    logit_peak = stack[added, :head_count]

    q_weight_grad, k_weight_grad, v_weight_grad, o_weight_grad = finish_heads(
        rank_at, [tie(v, stack) if i == 0 else v for i, v in enumerate(along_seq(heads_last))], halves, groups
    )

    factor = jnp.sqrt(LOGIT_CAP / jnp.maximum(logit_peak, LOGIT_CAP))
    column_factor = jnp.repeat(factor, HEAD_DIM)
    q_weight_clipped = q_weight.astype(f32) * column_factor[None, :]
    k_weight_clipped = k_weight.astype(f32) * column_factor[None, :]
    q_bias_clipped = q_bias.astype(f32) * lax.dynamic_slice_in_dim(
        column_factor, fsdp * own_rows, own_rows, 0
    )
    return (
        output,
        in_grad.reshape(clip_count, local_frames, width),
        small_own[0],
        small_own[1],
        q_weight_grad,
        small_own[2],
        k_weight_grad,
        v_weight_grad,
        small_own[3],
        o_weight_grad,
        small_own[4],
        small_own[5],
        small_own[6],
        up_weight_grad,
        up_bias_grad,
        down_weight_grad,
        small_own[7],
        logit_peak,
        q_weight_clipped,
        q_bias_clipped,
        k_weight_clipped,
    )


def solution(mesh):
    rows, vector, clip = P("fsdp", None), P("fsdp"), P("fsdp", "seq", None)
    return jax.shard_map(
        local,
        mesh=mesh,
        in_specs=(
            clip,
            vector,
            vector,
            vector,
            rows,
            vector,
            rows,
            rows,
            vector,
            rows,
            vector,
            vector,
            vector,
            rows,
            vector,
            rows,
            vector,
            clip,
        ),
        out_specs=(
            clip,
            clip,
            vector,
            vector,
            rows,
            vector,
            rows,
            rows,
            vector,
            rows,
            vector,
            vector,
            vector,
            rows,
            vector,
            rows,
            vector,
            P(),
            rows,
            vector,
            rows,
        ),
        check_vma=False,
    )
```

```python
import math

import jax
import jax.numpy as jnp
from jax import lax
from jax.experimental import pallas as pl
from jax.experimental.pallas import tpu as pltpu
from jax.sharding import PartitionSpec as P

HEAD_DIM = 80
NEGATIVE = -1000000000.0
EPSILON = 1e-05
LOGIT_CAP = 10.0
LOG2E = 1.4426950408889634
VMEM_LIMIT = 56 * 1024 * 1024
f32 = jnp.float32
bf16 = jnp.bfloat16


def dot(left, right, left_dim, right_dim):
    return lax.dot_general(
        left, right, (((left_dim,), (right_dim,)), ((), ())), preferred_element_type=f32
    )


def nt(a, b):
    return dot(a, b, 1, 1)


def nn(a, b):
    return dot(a, b, 1, 0)


def tn(a, b):
    return dot(a, b, 0, 0)


def normalized(rows):
    centred = rows - jnp.mean(rows, axis=-1, keepdims=True)
    spread = jnp.mean(centred * centred, axis=-1, keepdims=True)
    scale = lax.rsqrt(spread + EPSILON)
    return centred * scale, scale


def norm_back(plain, scale, grad):
    first = jnp.mean(grad, axis=-1, keepdims=True)
    second = jnp.mean(grad * plain, axis=-1, keepdims=True)
    return scale * (grad - first - plain * second)


def tie(value, *after):
    return lax.optimization_barrier((value,) + after)[0]


def cost(flops, bytes_accessed, transcendentals):
    return pl.CostEstimate(
        flops=flops // 4, bytes_accessed=bytes_accessed // 4, transcendentals=transcendentals // 4
    )


def params(**more):
    return pltpu.CompilerParams(vmem_limit_bytes=VMEM_LIMIT, **more)


def vmem(count):
    return [pl.BlockSpec(memory_space=pltpu.VMEM)] * count


def smem():
    return pl.BlockSpec(memory_space=pltpu.SMEM)


def sds(shape, dtype):
    return jax.ShapeDtypeStruct(shape, dtype)


def one_row(width):
    return jnp.where(lax.broadcasted_iota(jnp.int32, (16, width), 0) == 0, 1.0, 0.0).astype(bf16)


def attend_kernel(scale2, span, q_ref, k_ref, v_ref, mask_ref, near_ref, far_ref, lse_ref, peak_ref):
    frames = q_ref.shape[1]
    mask_rows = mask_ref[...]
    keys = jnp.concatenate([k_ref[...], mask_rows], axis=0).T
    values = jnp.concatenate([v_ref[...], one_row(frames)], axis=0)
    s = nn(keys, jnp.concatenate([q_ref[...], one_row(frames)], axis=0))
    top = jnp.max(s, axis=0, keepdims=True)
    p = jnp.exp2(s * scale2 - top * scale2).astype(bf16)
    mixed = nn(values, p)
    total = mixed[HEAD_DIM : HEAD_DIM + 1, :]
    mixed = (mixed[:HEAD_DIM, :] * (1.0 / total)).astype(bf16)
    near_ref[0] = mixed[:, :span]
    for step in range(1, frames // span):
        far_ref[step - 1, 0] = mixed[:, step * span : (step + 1) * span]
    lse_ref[0] = top * scale2 + jnp.log2(total)
    peak_ref[0] = jnp.where(mask_rows[0:1, :].astype(f32) == 0.0, top, NEGATIVE)


def head_rows(frames, heads, half):
    return [
        pl.BlockSpec((HEAD_DIM, frames), lambda b, h, i=i: ((3 * half + i) * heads + h, b))
        for i in range(3)
    ]


def attend(qkv, mask, clips, heads, half, halves, groups):
    frames = qkv.shape[1] // clips
    span = frames // groups
    vec = pl.BlockSpec((1, 1, frames), lambda b, h: (b * heads + h, 0, 0))
    return pl.pallas_call(
        lambda *refs: attend_kernel(LOG2E / math.sqrt(HEAD_DIM), span, *refs),
        grid=(clips, heads),
        in_specs=head_rows(frames, heads, half) + [pl.BlockSpec((16, frames), lambda b, h: (b, 0))],
        out_specs=[
            pl.BlockSpec((1, HEAD_DIM, span), lambda b, h: (b, h, 0)),
            pl.BlockSpec((groups - 1, 1, HEAD_DIM, span), lambda b, h: (0, b, h, 0)),
            vec,
            vec,
        ],
        out_shape=[
            sds((clips, heads * HEAD_DIM, span), bf16),
            sds((groups - 1, clips, heads * HEAD_DIM, span), bf16),
            sds((clips * heads, 1, frames), f32),
            sds((clips * heads, 1, frames), f32),
        ],
        compiler_params=params(),
        cost_estimate=pl.CostEstimate(
            flops=clips * heads * frames * frames * 2000,
            bytes_accessed=qkv.size * 3 // halves,
            transcendentals=clips * heads * frames * frames,
        ),
        name="attend",
    )(qkv, qkv, qkv, mask)


def attend_back_kernel(span, scale, *refs):
    q_ref, k_ref, v_ref, mask_ref, lse_ref = refs[:5]
    groups = q_ref.shape[1] // span
    grads = refs[5 : 5 + 2 * groups]
    out_ref, gk, gv, gs = refs[5 + 2 * groups :]
    scale2 = LOG2E * scale
    key_rows = k_ref[...]
    keys = jnp.concatenate([key_rows, mask_ref[...]], axis=0).T
    values = v_ref[...].T
    ones = one_row(span)
    for flip in range(2):

        @pl.when(pl.program_id(0) == flip)
        def _(flip=flip):
            for at in range(groups):
                gs[:, at * span : (at + 1) * span] = grads[flip * groups + at][...].reshape(HEAD_DIM, span)

    for at in range(groups):
        cols = pl.ds(at * span, span)
        q = q_ref[:, cols]
        g = gs[:, cols]
        s = nn(keys, jnp.concatenate([q, ones], axis=0))
        p = jnp.exp2(s * scale2 - lse_ref[0, :, cols])
        t = p * nn(values, g)
        inner = jnp.sum(t, axis=0, keepdims=True)
        ds = (t - p * inner).astype(bf16)
        out_ref[0, :, cols] = (nn(key_rows, ds) * scale).astype(bf16)
        dk = nt(q, ds)
        dv = nt(g, p.astype(bf16))
        if at == 0:
            gk[...] = dk
            gv[...] = dv
        else:
            gk[...] += dk
            gv[...] += dv
    out_ref[1] = (gk[...] * scale).astype(bf16)
    out_ref[2] = gv[...].astype(bf16)


def attend_back(qkv, mask, grads, lse, clips, heads, half, halves, groups):
    frames = qkv.shape[1] // clips
    span = frames // groups
    vec = pl.BlockSpec((1, 1, frames), lambda b, h: (b * heads + h, 0, 0))

    def block(v, place):
        if v.ndim == 3:
            return pl.BlockSpec((1, HEAD_DIM, span), lambda b, h: (place, h, 0))
        return pl.BlockSpec((HEAD_DIM, span), lambda b, h: (place + h, 0))

    grads = grads[0] + grads[1]
    return pl.pallas_call(
        lambda *refs: attend_back_kernel(span, 1.0 / math.sqrt(HEAD_DIM), *refs),
        grid=(clips, heads),
        in_specs=head_rows(frames, heads, half)
        + [pl.BlockSpec((16, frames), lambda b, h: (b, 0)), vec]
        + [block(*g) for g in grads],
        out_specs=pl.BlockSpec((3, HEAD_DIM, frames), lambda b, h: (0, h, b)),
        out_shape=sds((3, heads * HEAD_DIM, clips * frames), bf16),
        scratch_shapes=[
            pltpu.VMEM((HEAD_DIM, frames), f32),
            pltpu.VMEM((HEAD_DIM, frames), f32),
            pltpu.VMEM((HEAD_DIM, frames), bf16),
        ],
        compiler_params=params(),
        cost_estimate=cost(
            flops=clips * heads * frames * frames * 4000,
            bytes_accessed=qkv.size * 6 // halves,
            transcendentals=clips * heads * frames * frames,
        ),
        name="attend_back",
    )(qkv, qkv, qkv, mask, lse, *[v for v, _ in grads])


def gelu_parts(v):
    bell = jnp.exp2(v * v * (-0.5 * LOG2E))
    t = 1.0 / (1.0 + (0.3275911 / math.sqrt(2.0)) * jnp.abs(v))
    poly = t * (
        0.5 * 0.254829592
        + t * (0.5 * -0.284496736 + t * (0.5 * 1.421413741 + t * (0.5 * -1.453152027 + t * (0.5 * 1.061405429))))
    )
    tail = poly * bell
    return jnp.where(v < 0.0, tail, 1.0 - tail), bell * (1.0 / math.sqrt(2.0 * math.pi))


def feed_kernel(count, own, tile, refs):
    ns, gs = refs[:count], refs[count : 2 * count]
    up_ref, down_ref, bias_ref = refs[2 * count : 2 * count + 3]
    act_ref, back_ref, grad_own, grad_other, out_own, out_other, sum_ref, n_now, g_now = refs[2 * count + 3 :]
    width = n_now.shape[1]
    hidden = act_ref.shape[1]
    rows = ns[0].shape[0]
    for j in range(count):
        n_now[j * rows : (j + 1) * rows, :] = ns[j][...]
        g_now[j * rows : (j + 1) * rows, :] = gs[j][...]
    up = up_ref[...].reshape(width, hidden)
    down = down_ref[...].reshape(hidden, width)
    for low in range(0, hidden, tile):
        cols = slice(low, low + tile)
        before = nn(n_now[...], up[:, cols]) + bias_ref[:, cols]
        grad_act = nt(g_now[...], down[cols, :])
        cumulative, density = gelu_parts(before)
        act_ref[:, cols] = (before * cumulative).astype(bf16)
        grad = ((cumulative + before * density) * grad_act).astype(bf16)
        back_ref[:, cols] = grad
        sum_ref[:, cols] = jnp.sum(grad.astype(f32), axis=0, keepdims=True)
    mine = own * rows
    grad_own[...] = nt(back_ref[:mine, :], up)
    grad_other[...] = nt(back_ref[mine:, :], up).astype(bf16)
    out_own[...] = nn(act_ref[:mine, :], down)
    out_other[...] = nn(act_ref[mine:, :], down).astype(bf16)


def feed(normed, grad, own, rows, weights, bias):
    count = len(normed)
    width = normed[0][0].shape[1]
    hidden = bias.shape[1]
    tile = 256 if hidden % 256 == 0 else hidden

    def whole(shape):
        return pl.BlockSpec(shape, lambda i: (0,) * len(shape))

    if len(weights) == 1:
        pairs = weights[0].shape[0]
        weights = weights * 2
        weight_specs = [pl.BlockSpec((pairs, hidden // pairs, width), lambda i, j=j: (0, j, 0)) for j in range(2)]
    else:
        weight_specs = [whole(w.shape) for w in weights]
    shapes = [
        sds((count * rows, hidden), bf16),
        sds((count * rows, hidden), bf16),
        sds((own * rows, width), f32),
        sds(((count - own) * rows, width), bf16),
        sds((own * rows, width), f32),
        sds(((count - own) * rows, width), bf16),
        sds((1, hidden), f32),
    ]
    return pl.pallas_call(
        lambda *refs: feed_kernel(count, own, tile, refs),
        grid=(1,),
        in_specs=[pl.BlockSpec((rows, width), lambda i, at=at: (at, 0)) for _, at in normed + grad]
        + weight_specs
        + [whole((1, hidden))],
        out_specs=[whole(v.shape) for v in shapes],
        out_shape=shapes,
        scratch_shapes=[pltpu.VMEM((count * rows, width), bf16)] * 2,
        compiler_params=params(),
        cost_estimate=cost(
            flops=8 * count * rows * width * hidden,
            bytes_accessed=4 * width * hidden + 16 * count * rows * width,
            transcendentals=count * rows * hidden,
        ),
        name="feed",
    )(*[v for v, _ in normed + grad], *weights, bias)


def project(rank, blocks, small, weight, halves):
    count = len(blocks)
    rows, width = blocks[0].shape
    shards, lines_count, features = small.shape
    own_rows = width // shards
    slab = features // 3
    cut = slab // halves
    sub = math.gcd(rows, 256)

    def kernel(rank_ref, small_ref, w_ref, *refs):
        xs = refs[:count]
        normed_ref, qkv_ref, lines_ref, turned, bias, now = refs[count:]
        at = pl.program_id(0)

        @pl.when(at == 0)
        def _():
            lines_ref[...] = jnp.concatenate(
                [small_ref[f, :, :own_rows].astype(f32) for f in range(shards)], axis=1
            )
            turned[...] = w_ref[...].T
            for r in range(count):

                @pl.when(rank_ref[0] == r)
                def _(r=r):
                    parts = []
                    for h in range(halves):
                        cols = slice(r * slab + h * cut, r * slab + (h + 1) * cut)
                        parts += [lines_ref[2:3, cols], jnp.zeros((1, cut), f32), lines_ref[3:4, cols]]
                    row = jnp.concatenate(parts, axis=1)
                    bias[...] = jnp.broadcast_to(row, (8, features)).T

        for j in range(count):

            @pl.when(at == j)
            def _(j=j):
                now[...] = xs[j][...]

        for t in range(0, rows, sub):
            plain, _ = normalized(now[t : t + sub, :].astype(f32))
            normed = (plain * lines_ref[0:1, :] + lines_ref[1:2, :]).astype(bf16)
            normed_ref[t : t + sub, :] = normed
            qkv_ref[:, t : t + sub] = (nt(turned[...], normed) + bias[:, 0:1]).astype(bf16)

    return pl.pallas_call(
        kernel,
        grid=(count,),
        in_specs=[
            smem(),
            pl.BlockSpec(small.shape, lambda i: (0, 0, 0)),
            pl.BlockSpec(weight.shape, lambda i: (0, 0)),
        ]
        + [pl.BlockSpec((rows, width), lambda i: (0, 0))] * count,
        out_specs=[
            pl.BlockSpec((rows, width), lambda i: (i, 0)),
            pl.BlockSpec((features, rows), lambda i: (0, i)),
            pl.BlockSpec((lines_count, width), lambda i: (0, 0)),
        ],
        out_shape=[
            sds((count * rows, width), bf16),
            sds((features, count * rows), bf16),
            sds((lines_count, width), f32),
        ],
        scratch_shapes=[
            pltpu.VMEM((features, width), bf16),
            pltpu.VMEM((features, 8), f32),
            pltpu.VMEM((rows, width), bf16),
        ],
        compiler_params=params(),
        cost_estimate=pl.CostEstimate(
            flops=2 * count * rows * width * features,
            bytes_accessed=2 * width * features + 6 * count * rows * width,
            transcendentals=count * rows,
        ),
        name="project",
    )(rank, small, weight, *blocks)


def project_back(grads, weight, blocks, places, groups):
    count, halves = len(blocks), len(grads)
    rows, width = blocks[0].shape
    features = weight.shape[1]
    own = count // 2
    sub = math.gcd(rows, 256)

    def kernel(w_ref, *refs):
        g_refs, xs = refs[:halves], refs[halves : halves + count]
        own_ref, other_ref, sums_ref, bias_ref, now = refs[halves + count :]
        at = pl.program_id(0)
        for j in range(count):

            @pl.when(at == j)
            def _(j=j):
                now[...] = xs[j][...]

        @pl.when(at == 0)
        def _():
            sums_ref[...] = jnp.zeros(sums_ref.shape, f32)
            bias_ref[...] = jnp.zeros(bias_ref.shape, f32)

        for t in range(0, rows, sub):
            cut = slice(t, t + sub)
            turned = jnp.concatenate([g[:, cut] for g in g_refs], axis=0).T
            grad = nt(turned, w_ref[...])
            plain, _ = normalized(now[cut, :].astype(f32))
            sums_ref[0:1, :] += jnp.sum(grad * plain, axis=0, keepdims=True)
            sums_ref[1:2, :] += jnp.sum(grad, axis=0, keepdims=True)
            bias_ref[...] += nn(jnp.ones((8, sub), bf16), turned)

            @pl.when(at < own)
            def _(cut=cut, grad=grad):
                own_ref[cut, :] = grad

            @pl.when(at >= own)
            def _(cut=cut, grad=grad):
                other_ref[cut, :] = grad.astype(bf16)

    return pl.pallas_call(
        kernel,
        grid=(count,),
        in_specs=[pl.BlockSpec(weight.shape, lambda i: (0, 0))]
        + [
            pl.BlockSpec((g.shape[0], rows), lambda i: (0, i // own * groups + i % own + places[0])) for g in grads
        ]
        + [pl.BlockSpec((rows, width), lambda i: (0, 0))] * count,
        out_specs=[
            pl.BlockSpec((rows, width), lambda i: (jnp.minimum(i, own - 1), 0)),
            pl.BlockSpec((rows, width), lambda i: (jnp.maximum(i - own, 0), 0)),
            pl.BlockSpec((8, width), lambda i: (0, 0)),
            pl.BlockSpec((8, features), lambda i: (0, 0)),
        ],
        out_shape=[
            sds((own * rows, width), f32),
            sds((own * rows, width), bf16),
            sds((8, width), f32),
            sds((8, features), f32),
        ],
        scratch_shapes=[pltpu.VMEM((rows, width), bf16)],
        compiler_params=params(),
        cost_estimate=cost(
            flops=2 * count * rows * width * features,
            bytes_accessed=2 * width * features + 8 * count * rows * width,
            transcendentals=count * rows,
        ),
        name="project_back",
    )(weight, *grads, *blocks)


def by_source(r, groups):
    return [((src % groups - r % groups) % groups, (src // groups) ^ (r // groups)) for src in range(2 * groups)]


def finish_heads(rank, blocks, halves, groups):
    _, rows, features = blocks[0].shape
    ranks = 2 * groups
    slab = features // 4
    cut = slab // halves
    width = slab * ranks
    starts = [0] + [slab + 3 * cut * h for h in range(1, halves)]

    def kernel(rank_ref, *refs):
        ins, outs = refs[:-4], refs[-4:]
        for r in range(ranks):

            @pl.when(rank_ref[0] == r)
            def _(r=r):
                order = by_source(r, groups)
                for i in range(3):
                    outs[i][...] = jnp.concatenate(
                        [
                            ins[step][flip, :, low + i * cut : low + (i + 1) * cut]
                            for step, flip in order
                            for low in starts
                        ],
                        axis=1,
                    ).astype(f32)
                outs[3][...] = jnp.concatenate(
                    [ins[step][flip, :, 3 * cut : 3 * cut + slab] for step, flip in order], axis=1
                ).astype(f32)

    return pl.pallas_call(
        kernel,
        in_specs=[smem()] + vmem(groups),
        out_specs=vmem(4),
        out_shape=[sds((rows, width), f32)] * 4,
        compiler_params=params(),
        cost_estimate=pl.CostEstimate(flops=0, bytes_accessed=24 * rows * width, transcendentals=0),
        name="finish_heads",
    )(rank, *blocks)


def finish_feed(rank, ups, downs, pairs, groups):
    _, rows, rank_hidden = ups[0].shape
    piece, width = downs[0].shape
    ranks = 2 * groups

    def kernel(rank_ref, *refs):
        up_refs, down_refs, up_out, down_out = refs[:groups], refs[groups : 2 * groups], refs[-2], refs[-1]
        for r in range(ranks):

            @pl.when(rank_ref[0] == r)
            def _(r=r):
                for zx in range(pairs):
                    up_out[:, zx * ranks * piece : (zx + 1) * ranks * piece] = jnp.concatenate(
                        [
                            up_refs[step][flip, :, zx * piece : (zx + 1) * piece]
                            for step, flip in by_source(r, groups)
                        ],
                        axis=1,
                    ).astype(f32)
                for step in range(groups):
                    at = (r + step) % groups * piece
                    down_out[at : at + piece, :] = down_refs[step][...].astype(f32)

    return pl.pallas_call(
        kernel,
        in_specs=[smem()] + vmem(2 * groups),
        out_specs=vmem(2),
        out_shape=[sds((rows, rank_hidden * ranks), f32), sds((groups * piece, width), f32)],
        compiler_params=params(),
        cost_estimate=pl.CostEstimate(flops=0, bytes_accessed=12 * rows * rank_hidden * ranks, transcendentals=0),
        name="finish_feed",
    )(rank, *ups, *downs)


def pick(where, q, k, v, up, o, small, ranks, halves, pairs):
    own_rows, width = q.shape
    slab = width // ranks
    cut = slab // halves
    piece = up.shape[1] // (ranks * pairs)
    base = -(-own_rows // 16) * 16
    extra = small.shape[0]

    def kernel(where_ref, q_ref, k_ref, v_ref, up_ref, o_ref, small_ref, *outs):
        for side in range(2):
            pay, ups, half = outs[3 * side : 3 * side + 3]
            pay[base:, :] = jnp.zeros((extra, 3 * slab), bf16)
            pay[base:, : small.shape[1]] = small_ref[...]
            for r in range(ranks):

                @pl.when(where_ref[side] == r)
                def _(pay=pay, ups=ups, r=r):
                    parts = [
                        w[:, r * slab + h * cut : r * slab + (h + 1) * cut]
                        for h in range(halves)
                        for w in (q_ref, k_ref, v_ref)
                    ]
                    pay[:own_rows, :] = jnp.concatenate(parts, axis=1)
                    ups[...] = jnp.concatenate(
                        [up_ref[:, (c * ranks + r) * piece : (c * ranks + r + 1) * piece] for c in range(pairs)],
                        axis=1,
                    )

            for c in range(2):

                @pl.when(where_ref[2] == (c ^ side))
                def _(half=half, c=c):
                    half[...] = o_ref[:, c * width // 2 : (c + 1) * width // 2]

    shapes = [
        sds((base + extra, 3 * slab), bf16),
        sds((own_rows, piece * pairs), bf16),
        sds((own_rows, width // 2), bf16),
    ]
    return pl.pallas_call(
        kernel,
        in_specs=[smem()] + vmem(6),
        out_specs=vmem(6),
        out_shape=shapes * 2,
        compiler_params=params(),
        cost_estimate=pl.CostEstimate(flops=0, bytes_accessed=10 * up.size, transcendentals=0),
        name="pick",
    )(where, q, k, v, up, o, small)


def place(blocks, slots, pieces):
    count, (_, width) = len(blocks), blocks[0].shape

    def kernel(slots_ref, *refs):
        for i in range(count):
            for target, spans in zip(refs[count:], pieces, strict=True):
                for j, (low, high) in enumerate(spans):
                    target[slots_ref[i] * len(spans) + j] = refs[i][low:high, :]

    return pl.pallas_call(
        kernel,
        in_specs=[smem()] + vmem(count),
        out_specs=vmem(len(pieces)),
        out_shape=[
            sds((count * len(spans), spans[0][1] - spans[0][0], width), blocks[0].dtype) for spans in pieces
        ],
        compiler_params=params(),
        cost_estimate=pl.CostEstimate(
            flops=0, bytes_accessed=4 * count * blocks[0].size, transcendentals=0
        ),
        name="place",
    )(slots, *blocks)


def merge(slots, x, out_full, lines, blocks, halves, token_parts):
    tokens, width = x.shape
    count = len(blocks)
    hs = blocks[0][0].shape[0]
    slab = hs * halves
    rows = tokens // token_parts

    def kernel(slots_ref, x_ref, w_ref, lines_ref, *refs):
        ins, mixed, after = refs[: count * halves], refs[count * halves], refs[count * halves + 1]
        outs = refs[count * halves + 2 :]
        for i in range(count):
            for h in range(halves):
                at = pl.multiple_of(slots_ref[i] * slab + h * hs, 16)
                mixed[pl.ds(at, hs), :] = ins[i * halves + h][...]
        for t in range(token_parts):
            cols = slice(t * rows, (t + 1) * rows)
            total = nn(mixed[:, cols].T, w_ref[...]) + lines_ref[4:5, :] + x_ref[cols, :].astype(f32)
            after[cols, :] = total
            plain, _ = normalized(total)
            outs[t][...] = (plain * lines_ref[5:6, :] + lines_ref[6:7, :]).astype(bf16)

    made = pl.pallas_call(
        kernel,
        in_specs=[smem()] + vmem(3 + count * halves),
        out_specs=vmem(2 + token_parts),
        out_shape=[sds((width, tokens), bf16), sds((tokens, width), f32)]
        + [sds((rows, width), bf16)] * token_parts,
        compiler_params=params(),
        cost_estimate=pl.CostEstimate(
            flops=2 * tokens * width * width, bytes_accessed=2 * width * width + 12 * tokens * width, transcendentals=tokens
        ),
        name="merge",
    )(slots, x, out_full, lines, *[b for source in blocks for b in source])
    return made[0], made[1], list(made[2:])


def turn(slots, after1, near, fars, live_grad, lines, out_full, halves, groups):
    tokens, width = after1.shape
    ranks = 2 * groups
    slab = width // ranks
    hs = slab // halves
    parts = len(fars)
    rows = tokens // parts
    per = len(fars[0])

    def kernel(slots_ref, after_ref, near_ref, live_ref, g_ref, w_ref, *refs):
        far_refs = refs[: parts * per]
        grad_ref, low_ref, sums_ref = refs[parts * per : parts * per + 3]
        outs = refs[parts * per + 3 :]
        sums = [jnp.zeros((1, width), f32) for _ in range(4)]
        for t in range(parts):
            cut = slice(t * rows, (t + 1) * rows)
            grad = near_ref[cut, :]
            for j in range(per):
                grad = grad + far_refs[t * per + j][...].astype(f32)
            plain, scale = normalized(after_ref[cut, :])
            live = live_ref[cut, :].astype(f32)
            total = live + norm_back(plain, scale, grad * g_ref[5:6, :])
            grad_ref[cut, :] = total
            low = total.astype(bf16)
            low_ref[cut, :] = low
            for i, term in enumerate((grad * plain, grad, low.astype(f32), live)):
                sums[i] = sums[i] + jnp.sum(term, axis=0, keepdims=True)
        for i in range(4):
            sums_ref[i : i + 1, :] = sums[i]
        low = low_ref[...]

        def of_rank(flip, step, h):
            at = pl.multiple_of(slots_ref[flip * groups + step] * slab + h * hs, 16)
            return nt(w_ref[pl.ds(at, hs), :], low).astype(bf16)

        for h in range(halves):
            for step in range(1, groups):
                for flip in range(2):
                    outs[h * (groups - 1) + step - 1][flip] = of_rank(flip, step, h)
        near_outs = outs[halves * (groups - 1) :]
        for h in range(halves):
            near_outs[0][h * hs : (h + 1) * hs, :] = of_rank(0, 0, h)
            near_outs[1][h * hs : (h + 1) * hs, :] = of_rank(1, 0, h)

    fars_count = halves * (groups - 1)
    made = pl.pallas_call(
        kernel,
        in_specs=[smem()] + vmem(5 + parts * per),
        out_specs=vmem(3 + fars_count + 2),
        out_shape=[sds((tokens, width), f32), sds((tokens, width), bf16), sds((4, width), f32)]
        + [sds((2, hs, tokens), bf16)] * fars_count
        + [sds((slab, tokens), bf16)] * 2,
        compiler_params=params(),
        cost_estimate=cost(
            flops=2 * tokens * width * width, bytes_accessed=2 * width * width + 16 * tokens * width, transcendentals=tokens
        ),
        name="turn",
    )(slots, after1, near, live_grad, lines, out_full, *[v for part in fars for v in part])
    sent = [[made[3 + h * (groups - 1) + step] for step in range(groups - 1)] for h in range(halves)]
    return made[0], made[1], made[2], sent, made[-2], made[-1]


def part_ways(x_ref, value, kept, sent):
    depth, rows = kept.shape[:2]
    for flip in range(2):

        @pl.when(x_ref[0] == flip)
        def _(flip=flip):
            for z in range(depth):
                low, other = (2 * z + flip) * rows, (2 * z + 1 - flip) * rows
                kept[z] = value[low : low + rows, :]
                sent[z] = value[other : other + rows, :]


def weight_grad(x_at, lefts, rights, depth):
    rows = lefts[0][0].shape[1]
    cols = rights[0][0].shape[1]
    tile = 256 if cols % 256 == 0 else cols
    count, right_count = len(lefts), len(rights)

    def ends_of(parts):
        return [sum(size for _, _, size in parts[:i]) for i in range(len(parts) + 1)]

    left_ends, right_ends = ends_of(lefts), ends_of(rights)
    tokens = left_ends[-1]
    share = rows // (2 * depth)

    def kernel(x_ref, *refs):
        left_refs, right_refs = refs[:count], refs[count : count + right_count]
        kept, sent, turned, joined = refs[-4:]

        @pl.when(pl.program_id(0) == 0)
        def _():
            for i in range(count):
                turned[:, left_ends[i] : left_ends[i + 1]] = left_refs[i][...].T

        for i in range(right_count):
            joined[right_ends[i] : right_ends[i + 1], :] = right_refs[i][...]
        part_ways(x_ref, nn(turned[...], joined[...]).astype(bf16), kept, sent)

    whole = [pl.BlockSpec((size, rows), lambda i, at=at: (at, 0)) for _, at, size in lefts]
    strips = [pl.BlockSpec((size, tile), lambda i, at=at: (at, i)) for _, at, size in rights]
    return pl.pallas_call(
        kernel,
        grid=(cols // tile,),
        in_specs=[smem()] + whole + strips,
        out_specs=[pl.BlockSpec((depth, share, tile), lambda i: (0, 0, i))] * 2,
        out_shape=[sds((depth, share, cols), bf16)] * 2,
        scratch_shapes=[pltpu.VMEM((rows, tokens), bf16), pltpu.VMEM((tokens, tile), bf16)],
        compiler_params=params(),
        cost_estimate=cost(
            flops=2 * tokens * rows * cols, bytes_accessed=2 * (tokens * (rows + cols) + rows * cols), transcendentals=0
        ),
        name="weight_grad",
    )(x_at, *[v for v, _, _ in lefts + rights])


def head_grad(x_at, normed, grad_heads, depth, extra=()):
    tokens, width = normed.shape
    features = grad_heads.shape[0]
    tile = 512 if tokens % 512 == 0 else tokens
    share = width // (2 * depth)
    slab = extra[0].shape[1] // 2 if extra else 0
    cols = features + slab

    def kernel(x_ref, n_ref, g_ref, *refs):
        kept, sent, total = refs[-3:]
        part = nn(g_ref[...], n_ref[...])

        @pl.when(pl.program_id(0) == 0)
        def _():
            total[...] = part

        @pl.when(pl.program_id(0) > 0)
        def _():
            total[...] += part

        @pl.when(pl.program_id(0) == pl.num_programs(0) - 1)
        def _():
            value = total[...].astype(bf16).T
            if extra:
                more = refs[0][...].astype(f32)
                for v in refs[1:-3]:
                    more = more + v[...].astype(f32)
                more = more.astype(bf16)
                more = jnp.concatenate([more[:, :slab], more[:, slab:]], axis=0)
                value = jnp.concatenate([value, more], axis=1)
            part_ways(x_ref, value, kept, sent)

    return pl.pallas_call(
        kernel,
        grid=(tokens // tile,),
        in_specs=[
            smem(),
            pl.BlockSpec((tile, width), lambda i: (i, 0)),
            pl.BlockSpec((features, tile), lambda i: (0, i)),
        ]
        + [pl.BlockSpec(v.shape, lambda i: (0, 0)) for v in extra],
        out_specs=[pl.BlockSpec((depth, share, cols), lambda i: (0, 0, 0))] * 2,
        out_shape=[sds((depth, share, cols), bf16)] * 2,
        scratch_shapes=[pltpu.VMEM((features, width), f32)],
        compiler_params=params(),
        cost_estimate=cost(
            flops=2 * tokens * width * features, bytes_accessed=2 * tokens * (width + features), transcendentals=0
        ),
        name="head_grad",
    )(x_at, normed, grad_heads, *extra)


def out_grad_halves(core_at, mixed, grad):
    rows, tokens = mixed.shape
    width = grad.shape[1]
    half = width // 2

    def kernel(core_ref, m_ref, g_ref, kept, sent):
        value = nn(m_ref[...], g_ref[...]).astype(bf16)
        for core in range(2):

            @pl.when(core_ref[0] == core)
            def _(core=core):
                kept[...] = value[:, core * half : (core + 1) * half]
                sent[...] = value[:, (1 - core) * half : (2 - core) * half]

    return pl.pallas_call(
        kernel,
        in_specs=[smem()] + vmem(2),
        out_specs=vmem(2),
        out_shape=[sds((rows, half), bf16)] * 2,
        compiler_params=params(),
        cost_estimate=cost(
            flops=2 * rows * tokens * width, bytes_accessed=4 * rows * width, transcendentals=0
        ),
        name="out_grad_halves",
    )(core_at, mixed, grad)


def out_grad_parts(seq_at, kept, came, groups):
    rows, half = kept.shape
    slab = half // groups

    def kernel(seq_ref, a_ref, b_ref, *outs):
        value = (a_ref[...].astype(f32) + b_ref[...].astype(f32)).astype(bf16)
        for at in range(groups):

            @pl.when(seq_ref[0] == at)
            def _(at=at):
                for step in range(groups):
                    low = (at + step) % groups * slab
                    part = value[:, low : low + slab]
                    outs[step][...] = jnp.concatenate([part[: rows // 2, :], part[rows // 2 :, :]], axis=1)

    return pl.pallas_call(
        kernel,
        in_specs=[smem()] + vmem(2),
        out_specs=vmem(groups),
        out_shape=[sds((rows // 2, 2 * slab), bf16)] * groups,
        compiler_params=params(),
        cost_estimate=cost(flops=0, bytes_accessed=6 * rows * half, transcendentals=0),
        name="out_grad_parts",
    )(seq_at, kept, came)


def local(
    frames_in,
    clip_lengths,
    norm1_gain,
    norm1_bias,
    q_weight,
    q_bias,
    k_weight,
    v_weight,
    v_bias,
    o_weight,
    o_bias,
    norm2_gain,
    norm2_bias,
    up_weight,
    up_bias,
    down_weight,
    down_bias,
    out_grad,
):
    clip_count, local_frames, width = frames_in.shape
    hidden = up_weight.shape[1]
    groups = lax.axis_size("seq")
    shards = lax.axis_size("fsdp")
    pairs = shards // 2
    depth = pairs // 2
    ranks = groups * 2
    frames = local_frames * groups
    assert clip_count == 1
    tokens = clip_count * local_frames
    head_count = width // HEAD_DIM
    heads = head_count // ranks
    halves = 2 if heads % 2 == 0 else 1
    slab = heads * HEAD_DIM
    cut = slab // halves
    own_rows = width // shards
    own_hidden = hidden // shards
    piece = own_hidden * 2 // ranks
    rank_hidden = piece * pairs
    clips = 2 * clip_count
    token_parts = 2
    part_rows = tokens // token_parts
    fsdp = lax.axis_index("fsdp")
    seq = lax.axis_index("seq")
    core, pair = fsdp % 2, fsdp // 2
    xpos, zpos = pair % 2, pair // 2
    rank = core * groups + seq
    peer = (1 - core) * groups + seq

    core_way = [(i, i ^ 1) for i in range(shards)]
    x_way = [(i, i ^ 2) for i in range(shards)]

    def over_core(v):
        return lax.ppermute(v, "fsdp", core_way)

    def over_x(v):
        return lax.ppermute(v, "fsdp", x_way)

    def over_z(v, step):
        return lax.ppermute(v, "fsdp", [(i, (i + 4 * step) % shards) for i in range(shards)])

    def from_seq(v, step):
        return lax.ppermute(v, "seq", [(i, (i - step) % groups) for i in range(groups)])

    def to_seq(v, step):
        return from_seq(v, -step % groups)

    steps = range(1, groups)

    def by_core(mine, other):
        return jnp.where(
            core == 0, jnp.concatenate([mine, other]), jnp.concatenate([other, mine])
        )

    slots = []
    for step in range(depth):
        for flip in range(2):
            slots.append(((zpos - step) % depth) * 2 + (xpos ^ flip))
    slots = jnp.stack(slots).astype(jnp.int32)

    def spread_z(payload):
        return [payload] + [over_z(payload, step) for step in range(1, depth)]

    def spread_x(blocks):
        return [v for block in blocks for v in (block, over_x(block))]

    small = [norm1_gain, norm1_bias, q_bias, v_bias, o_bias, norm2_gain, norm2_bias, down_bias]
    small = jnp.concatenate([jnp.stack(small), up_bias.reshape(hidden // width, own_rows)])
    small_rows = -(-small.shape[0] // 16) * 16
    small = jnp.pad(small, ((0, small_rows - small.shape[0]), (0, 0)))
    where = jnp.stack([rank, peer, core]).astype(jnp.int32)
    pay, up_mine, out_mine, pay_other, up_other, out_other = pick(
        where, q_weight, k_weight, v_weight, up_weight, o_weight, small, ranks, halves, pairs
    )
    base = -(-own_rows // 16) * 16
    pay_rows = base + small_rows
    frames_own = frames_in.reshape(tokens, width)
    pay_full = by_core(pay, over_core(pay_other))
    pay_z = spread_z(pay_full)
    frames_side = [from_seq(tie(frames_own, pay_full), step) for step in steps]

    up_own = by_core(up_mine, over_core(up_other))
    down_own = lax.dynamic_slice_in_dim(down_weight, seq * piece, piece, 0)
    out_own = by_core(out_mine, over_core(out_other))
    same_core = [[i for i in range(shards) if i % 2 == c] for c in range(2)]

    def over_chips(v):
        return lax.all_gather(v, "fsdp", axis=0, axis_index_groups=same_core)

    out_half = over_chips(out_own).reshape(width, width // 2)
    feed_own = jnp.concatenate([up_own.reshape(-1, width), down_own])
    gathered = over_chips(tie(feed_own, *pay_z[1:]))
    up_rows = up_own.size // width
    if rank_hidden == width:
        feed_weights = [gathered]
    else:
        feed_weights = [
            gathered[:, :up_rows].reshape(width, rank_hidden),
            gathered[:, up_rows:].reshape(rank_hidden, width),
        ]

    pay_z[depth // 2] = tie(pay_z[depth // 2], *frames_side)
    pay_all = spread_x(pay_z)
    frames_near = over_core(tie(frames_own, *pay_all))
    lengths_sent = jnp.broadcast_to(clip_lengths.astype(f32)[:, None], (clip_count, 128))
    lengths_near = over_core(tie(lengths_sent, *pay_z[1:]))
    frames_cross = [over_core(tie(v, *pay_all)) for v in frames_side]

    positions = jnp.concatenate(
        [
            ((seq + step) % groups) * local_frames + jnp.arange(local_frames, dtype=jnp.int32)
            for step in range(groups)
        ]
    )
    lengths = jnp.concatenate([clip_lengths, lengths_near[:, 0].astype(jnp.int32)])
    live = positions[None, :] < lengths[:, None]
    live_own = live[:clip_count, :local_frames].reshape(tokens, 1)
    mask = jnp.where(live, 0.0, NEGATIVE).astype(bf16)
    mask = jnp.pad(mask[:, None, :], ((0, 0), (0, 15), (0, 0))).reshape(clips * 16, frames)
    live_grad = jnp.where(live_own, out_grad.reshape(tokens, width), 0.0).astype(bf16)

    grad_side = [from_seq(tie(live_grad, *frames_side), step) for step in steps]

    qkv_part, small_part = place(
        pay_all,
        slots,
        [
            [(0, own_rows), (pay_rows, pay_rows + own_rows)],
            [(base, pay_rows), (pay_rows + base, 2 * pay_rows)],
        ],
    )
    qkv_full = qkv_part.reshape(width, 3 * slab)
    ubias = small_part[:, 8 : 8 + hidden // width, :own_rows].astype(f32).reshape(pairs, ranks, piece)
    ubias = lax.dynamic_index_in_dim(ubias, rank, 1, keepdims=False).reshape(1, rank_hidden)


    def to_z(both):
        blocks = [
            lax.dynamic_index_in_dim(both, (zpos + step) % depth, 0, keepdims=False) for step in range(depth)
        ]
        return blocks[0], [v.astype(bf16) for v in blocks[1:]]

    def reduce_z(kept, sent, parted=True):
        both = kept.astype(f32) + over_x(sent).astype(f32)
        return to_z(both) if parted else both

    def reduce_end(own, sent):
        total = own
        for step in range(1, depth):
            total = total + over_z(sent[step - 1], step).astype(f32)
        return total.astype(bf16)

    def along_seq(v):
        return [v] + [from_seq(v, step) for step in steps]

    def own_of_ranks(v):
        blocks = v.reshape(2, own_rows, -1)
        keep = lax.dynamic_index_in_dim(blocks, core, 0, keepdims=False)
        other = over_core(lax.dynamic_index_in_dim(blocks, 1 - core, 0, keepdims=False))
        return jnp.stack([keep, other])

    rank_at = rank.reshape(1).astype(jnp.int32)
    seq_at = seq.reshape(1).astype(jnp.int32)
    frames_all = [frames_own] + frames_side + [frames_near] + frames_cross
    normed1, qkv, lines = project(rank_at, frames_all, small_part, qkv_full, halves)
    grad_cross_near = over_core(tie(live_grad, lines))
    grad_cross = [over_core(tie(v, lines)) for v in grad_side]
    grad_near = [(v, t) for v in (live_grad, grad_cross_near) for t in range(token_parts)]
    grad_far = [[(v, t) for v in grad_side + grad_cross] for t in range(token_parts)]

    out_half = out_half.reshape(width, width // 2)
    out_rest = over_core(out_half)
    out_full = jnp.where(
        core == 0,
        jnp.concatenate([out_half, out_rest], axis=1),
        jnp.concatenate([out_rest, out_half], axis=1),
    )
    half_heads = heads // halves
    logs, tops, sources = [], [], []
    mixed_blocks = [[] for _ in range(ranks)]

    def flat(v):
        return jnp.swapaxes(v, 0, 1).reshape(v.shape[1], tokens)

    for half in range(halves):
        if half:
            qkv = tie(qkv, grad_cross_near, *grad_cross)
        near, far, log_half, top_half = attend(qkv, mask, clips, half_heads, half, halves, groups)
        logs.append(log_half)
        tops.append(top_half)
        came = [near] + [to_seq(far[step - 1], step) for step in steps]
        for step, v in enumerate(came):
            mixed_blocks[step].append(flat(v[:clip_count]))
            mixed_blocks[groups + step].append(flat(over_core(v[clip_count:])))
    sources = [
        (core ^ flip) * groups + (seq - step) % groups for flip in range(2) for step in range(groups)
    ]
    sources = jnp.stack(sources).astype(jnp.int32)
    mixed_own, after1, normed2_own = merge(
        sources, frames_own, out_full, lines, mixed_blocks, halves, token_parts
    )

    normed2_side = [[from_seq(v, step) for step in steps] for v in normed2_own]
    normed2_near = normed2_own + [over_core(v) for v in normed2_own]

    def parts_of(arrays):
        return [(v, 0) for v in arrays]

    act_near, back_near, grad2_own, grad2_other, fed_own, fed_other, sums = feed(
        parts_of(normed2_near), grad_near, token_parts, part_rows, feed_weights, ubias
    )
    normed2_side = [[tie(v, sums) for v in side] for side in normed2_side]
    normed2_far = [side + [over_core(v) for v in side] for side in normed2_side]
    normed2_far[0][0] = tie(normed2_far[0][0], *sum(normed2_side, []))
    act_far, back_far, grad2_sent, fed_parts = [], [], [], []

    def far_sums(own, other):
        both = (own + over_core(other).astype(f32)).astype(bf16)
        return [both[i * part_rows : (i + 1) * part_rows] for i in range(len(steps))]

    for t in range(token_parts):
        if t:
            normed2_far[t][0] = tie(normed2_far[t][0], *grad2_sent[t - 1])
        act, back, far_own, far_other, out_own_far, out_other_far, sums_far = feed(
            parts_of(normed2_far[t]), grad_far[t], len(steps), part_rows, feed_weights, ubias
        )
        act_far.append(act)
        back_far.append(back)
        grad2_sent.append(far_sums(far_own, far_other))
        fed_parts.append((out_own_far, out_other_far))
        sums = sums + sums_far

    grad2_far = [[to_seq(v, step) for v, step in zip(part, steps)] for part in grad2_sent]
    grad2_near = grad2_own + over_core(grad2_other).astype(f32)

    def with_sizes(parts):
        return [(v, at, part_rows) for v, at in parts]

    def wholes(arrays):
        return [(v, 0, v.shape[0]) for v in arrays]

    x_at = xpos.reshape(1).astype(jnp.int32)
    lefts = with_sizes(parts_of(normed2_near + sum(normed2_far, [])))
    lefts[0] = (tie(lefts[0][0], grad2_near, *grad2_sent[-1]),) + lefts[0][1:]

    rights = wholes([back_near] + back_far)
    up_kept, up_sent = weight_grad(x_at, lefts, rights, depth)

    targets = [
        (core ^ flip) * groups + (seq + step) % groups for flip in range(2) for step in range(groups)
    ]
    targets = jnp.stack(targets).astype(jnp.int32)
    grad_after1, grad_attn, sums2, grad_sent, heads_own, heads_other = turn(
        targets, after1, tie(grad2_near, up_sent), grad2_far, live_grad, lines, out_full, halves, groups
    )
    half_rows = heads // halves
    heads_cross = over_core(heads_other)
    head_grads, arrived, sides = [], [], []
    for half in range(halves):
        came = [to_seq(v, step) for v, step in zip(grad_sent[half], steps)]
        came = [came[groups - step - 1] for step in steps]
        cross = [over_core(v) for v in came]
        sides.append(came)
        arrived += cross
        head_grads.append(
            [
                [(heads_own, half * half_rows)] + [(v, 0) for v in came],
                [(heads_cross, half * half_rows)] + [(v, 1) for v in cross],
            ]
        )

    acts = wholes([tie(act_near, grad_attn)] + act_far)
    down_kept, down_sent = weight_grad(x_at, acts, with_sizes(grad_near + sum(grad_far, [])), depth)
    out_kept, out_other_half = out_grad_halves(where[2:], mixed_own, tie(grad_attn, down_sent, *sum(sides, [])))
    out_parts = out_grad_parts(seq_at, out_kept, over_core(out_other_half), groups)
    out_sent = list(out_parts[1:])
    out_came = [to_seq(v, step) for v, step in zip(out_sent, steps)]

    def fed_sums(after):
        both = [(mine + over_core(tie(other, after)).astype(f32)).astype(bf16) for mine, other in fed_parts]
        sent = [jnp.concatenate([v[i * part_rows : (i + 1) * part_rows] for v in both]) for i in range(len(steps))]
        return sent, fed_own + over_core(tie(fed_other, after)).astype(f32)

    grad_qkv, x_parts = [], []
    for half in range(halves):
        if half:
            fed_sent, fed_near = fed_sums(x_parts[0][1])
            fed_far = [to_seq(v, step) for v, step in zip(fed_sent, steps)]
            up_shard = reduce_end(tie(up_z[0], x_parts[0][1]), up_z[1])
            down_z = reduce_z(tie(down_kept, x_parts[0][1]), down_sent)
            after = [x_parts[0][1], up_shard, fed_near] + down_z[1] + fed_sent
        else:
            up_z = reduce_z(tie(up_kept, down_sent), up_sent)
            after = up_z[1] + out_sent + arrived
        own = head_grads[half][0]
        own[0] = (tie(own[0][0], *after), own[0][1])
        grads = attend_back(qkv, mask, head_grads[half], logs[half], clips, half_heads, half, halves, groups)
        grads = grads.reshape(3 * cut, -1)
        grad_qkv.append(grads)
        x_parts.append(head_grad(x_at, normed1, grads, depth, () if half else [out_parts[0]] + out_came))
    if halves == 1:
        fed_sent, fed_near = fed_sums(x_parts[0][1])
        fed_far = [to_seq(v, step) for v, step in zip(fed_sent, steps)]
    fed = tie(fed_near, x_parts[-1][1])
    for v in fed_far:
        fed = fed + v.astype(f32)
    output = (after1 + (fed + lines[7:8])).astype(bf16).reshape(clip_count, local_frames, width)
    if halves == 1:
        up_shard = reduce_end(tie(up_z[0], x_parts[0][1]), up_z[1])
        down_z = reduce_z(tie(down_kept, x_parts[0][1]), down_sent)
    down_shard = reduce_end(tie(down_z[0], x_parts[-1][1]), down_z[1])
    ups = along_seq(tie(own_of_ranks(up_shard), x_parts[-1][1]))
    x_sums = [reduce_z(tie(kept, x_parts[-1][1]), sent, False) for kept, sent in x_parts[: halves - 1]]
    grad_qkv[-1] = tie(grad_qkv[-1], x_parts[-1][1], *x_sums, *fed_far)

    far_own, far_other, far_sums1, far_bias = project_back(grad_qkv, qkv_full, frames_side + frames_cross, steps, groups)
    far_cross = over_core(far_other).astype(f32)
    far1 = (far_own + far_cross).astype(bf16)
    far1 = [far1[i * tokens : (i + 1) * tokens] for i in range(len(steps))]
    kept, sent = x_parts[-1]
    x_sums.append(reduce_z(tie(kept, far_other), sent, False))
    heads_z = to_z(jnp.concatenate(x_sums, axis=2))
    near_own, near_other, near_sums1, near_bias = project_back(
        [tie(grad_qkv[0], down_shard, *far1, *heads_z[1], *ups[1:])] + grad_qkv[1:],
        qkv_full,
        [frames_own, frames_near],
        [0],
        groups,
    )
    sums1, bias_sums = far_sums1 + near_sums1, far_bias + near_bias
    near_cross = over_core(near_other)
    grad_normed1 = near_own + near_cross.astype(f32)
    far1_came = [to_seq(v, step) for v, step in zip(far1, steps)]
    downs = along_seq(tie(down_shard.reshape(piece, width), near_other, *far1_came))
    for v in far1_came:
        grad_normed1 = grad_normed1 + v.astype(f32)
    plain1, scale1 = normalized(frames_own.astype(f32))
    in_grad = (grad_after1 + norm_back(plain1, scale1, grad_normed1 * lines[0:1])).astype(bf16)

    heads_last = own_of_ranks(reduce_end(tie(heads_z[0], near_other), heads_z[1]))

    up_weight_grad, down_weight_grad = finish_feed(
        rank_at,
        ups,
        downs,
        pairs,
        groups,
    )
    bias_cols = bias_sums[0].reshape(halves, 3, cut)

    def at_rank(v):
        return lax.dynamic_update_slice_in_dim(jnp.zeros((width,), f32), v, rank * slab, 0)

    up_sums = lax.dynamic_update_index_in_dim(
        jnp.zeros((pairs, ranks, piece), f32), sums.reshape(pairs, piece), rank, 1
    ).reshape(hidden // width, width)
    tops = jnp.stack([jnp.max(v.reshape(clips, half_heads, frames), axis=(0, 2)) for v in tops])
    tops = tops.reshape(heads) / math.sqrt(HEAD_DIM)
    peak_row = lax.dynamic_update_slice_in_dim(
        jnp.full((width,), NEGATIVE, f32), tops, rank * heads, 0
    )
    added = 8 + hidden // width
    stack = jnp.concatenate(
        [
            sums1[:2],
            at_rank(bias_cols[:, 0].reshape(slab))[None],
            at_rank(bias_cols[:, 2].reshape(slab))[None],
            sums2[2:3],
            sums2[:2],
            sums2[3:4],
            up_sums,
            peak_row[None],
        ]
    )
    is_sum = (jnp.arange(added + 1) < added)[:, None]

    def combine(a, b):
        return jnp.where(is_sum, a + b, jnp.maximum(a, b))

    stack = tie(stack, near_cross)
    stack = combine(stack, over_core(stack))
    stack = combine(tie(stack, heads_last), over_x(stack))
    step = 4
    while step < shards:
        stack = combine(stack, lax.ppermute(stack, "fsdp", [(i, i ^ step) for i in range(shards)]))
        step *= 2
    stack = tie(stack, grad_normed1)
    step = 1
    while step < groups:
        stack = combine(stack, lax.ppermute(stack, "seq", [(i, i ^ step) for i in range(groups)]))
        step *= 2
    small_own = lax.dynamic_slice_in_dim(stack[:8], fsdp * own_rows, own_rows, 1)
    up_bias_grad = lax.dynamic_slice_in_dim(stack[8:added].reshape(hidden), fsdp * own_hidden, own_hidden, 0)
    logit_peak = stack[added, :head_count]

    q_weight_grad, k_weight_grad, v_weight_grad, o_weight_grad = finish_heads(
        rank_at, [tie(v, stack) if i == 0 else v for i, v in enumerate(along_seq(heads_last))], halves, groups
    )

    factor = jnp.sqrt(LOGIT_CAP / jnp.maximum(logit_peak, LOGIT_CAP))
    column_factor = jnp.repeat(factor, HEAD_DIM)
    q_weight_clipped = q_weight.astype(f32) * column_factor[None, :]
    k_weight_clipped = k_weight.astype(f32) * column_factor[None, :]
    q_bias_clipped = q_bias.astype(f32) * lax.dynamic_slice_in_dim(
        column_factor, fsdp * own_rows, own_rows, 0
    )
    return (
        output,
        in_grad.reshape(clip_count, local_frames, width),
        small_own[0],
        small_own[1],
        q_weight_grad,
        small_own[2],
        k_weight_grad,
        v_weight_grad,
        small_own[3],
        o_weight_grad,
        small_own[4],
        small_own[5],
        small_own[6],
        up_weight_grad,
        up_bias_grad,
        down_weight_grad,
        small_own[7],
        logit_peak,
        q_weight_clipped,
        q_bias_clipped,
        k_weight_clipped,
    )


def solution(mesh):
    rows, vector, clip = P("fsdp", None), P("fsdp"), P("fsdp", "seq", None)
    return jax.shard_map(
        local,
        mesh=mesh,
        in_specs=(
            clip,
            vector,
            vector,
            vector,
            rows,
            vector,
            rows,
            rows,
            vector,
            rows,
            vector,
            vector,
            vector,
            rows,
            vector,
            rows,
            vector,
            clip,
        ),
        out_specs=(
            clip,
            clip,
            vector,
            vector,
            rows,
            vector,
            rows,
            rows,
            vector,
            rows,
            vector,
            vector,
            vector,
            rows,
            vector,
            rows,
            vector,
            P(),
            rows,
            vector,
            rows,
        ),
        check_vma=False,
    )
```
